32 devices in a mesh: gx: 4 (over x, core), gy: 8 (over z, y).
Axes of the slice: x: 2, y: 2, z: 4, core: 2. Of those that a mesh axis runs over, the one named last changes fastest.
Arguments:
- features: bfloat16 [8, 16, 16, 512, 128], P('gx', 'gy'), may hold values from -6 to 6
- owner: int32 [8, 16, 16], P('gx', 'gy'), may hold values from -1 to 127, as said below
- norm_gain: float32 [8, 128], replicated, may hold values from 0.1 to 1.9
- time_shift: float32 [8, 512], replicated, may hold values from -4 to 4
- w_in: bfloat16 [8, 128, 512], replicated, may hold values from -0.5 to 0.5
- w_out: bfloat16 [8, 512, 128], replicated, may hold values from -0.25 to 0.25
- w_down: bfloat16 [2, 2, 2, 128, 128], replicated, may hold values from -0.1875 to 0.1875
- w_conv: bfloat16 [3, 3, 3, 128, 128], replicated, may hold values from -0.109375 to 0.109375
- w_up: bfloat16 [2, 2, 2, 128, 128], replicated, may hold values from -0.5 to 0.5
Outputs:
- denoised: bfloat16 [8, 16, 16, 512, 128], P('gx', 'gy')
The draws below stay inside these ranges and needn't reach their ends.
Inputs may be any that keep to these rules, and one draw needn't show every extreme that they name: Within each gx index and gy group, every owner along gy gets exactly 16 bricks, one in each compute slot; at most 4 bricks of one device go to one owner, and some device sends 4 to some owner; a device holds at most 32 occupied bricks, and some device holds exactly that many.
All inputs are finite; a program needn't handle non-finite values.
Results may differ from the reference program's by a relative error of at most 0.029.
Values may be sent and summed in bfloat16 or wider, within the bound.
No kernel may reach another device: no remote copies, remote signals or barrier semaphores. Data moves between devices by JAX's collectives and lax.ppermute only.
A program may use at most 192 MiB of HBM per device.

```python
import jax
import jax.numpy as jnp
from jax import lax

C = 128
HID = 512
LAYERS = 8
BX = 2
BY = 2
ZCAP = 16
LOAD = 16
NBX = 8
NBY = 16


def draw_owner(key, part):
    key = jax.random.fold_in(key, 7)
    groups = NBX // BX
    width = NBY // BY
    slots = BX * BY * ZCAP
    half = width // 2
    steps_i = jnp.arange(half, dtype=jnp.int32)
    delta = LOAD * steps_i // max(half - 1, 1)
    pattern = jnp.concatenate([LOAD + delta, LOAD - delta]).astype(jnp.int32)

    def one_group(group_key):
        keys = jax.random.split(group_key, width + 2)
        counts = pattern[jax.random.permutation(keys[0], width)]
        starts = jnp.cumsum(counts) - counts
        offset = jax.random.randint(keys[1], (), 0, width)
        ranks = jax.vmap(lambda k: jax.random.permutation(k, slots))(keys[2:]).astype(jnp.int32)
        placed = starts[:, None] + ranks
        codes = (placed + offset) % width * LOAD + placed // width
        codes = jnp.where(ranks < counts[:, None], codes, -1)
        return codes.reshape(width, BX, BY, ZCAP).transpose(1, 0, 2, 3).reshape(BX, NBY, ZCAP)
    group_keys = jax.random.split(key, groups)
    return jax.vmap(one_group)(group_keys).reshape(NBX, NBY, ZCAP).astype(jnp.int32)


def block_scale(key, extent, cuts, low, largest):
    gain = 1.0
    for dim, shards_of in cuts:
        heights = jax.random.uniform(jax.random.fold_in(jax.random.fold_in(key, 6), dim), (shards_of,), jnp.float32, low / len(cuts), largest / len(cuts))
        gain = gain * jnp.repeat(jnp.exp(heights), extent[dim] // shards_of).reshape((-1,) + (1,) * (len(extent) - 1 - dim))
    return gain


def normal_values(own_key, extent, spread, reach, pieces=(), kind=jnp.bfloat16):
    entries = spread * jax.random.normal(own_key, extent, jnp.float32)
    if pieces:
        entries = entries * block_scale(own_key, extent, pieces, -0.22, 0.18)
    return jnp.clip(entries, -reach, reach).astype(kind)


def setup_inputs(seed: int = 0) -> dict:
    key_of = jax.random.split(jax.random.key(seed), 10)
    features = normal_values(key_of[0], (NBX, NBY, ZCAP, 512, C), 1.0, 6.0, ((0, 4), (1, 8)))
    owner = draw_owner(jax.random.fold_in(key_of[9], 71), 0)
    norm_gain = jnp.clip(1.0 + 0.18 * jax.random.normal(key_of[2], (LAYERS, C), jnp.float32), 0.1, 1.9)
    time_shift = normal_values(key_of[3], (LAYERS, HID), 1.0, 4.0, (), jnp.float32)
    w_in = normal_values(key_of[4], (LAYERS, C, HID), C ** -0.5, 0.5)
    w_out = normal_values(key_of[5], (LAYERS, HID, C), HID ** -0.5, 0.25)
    w_down = normal_values(key_of[6], (2, 2, 2, C, C), (8 * C) ** -0.5, 0.1875)
    w_conv = normal_values(key_of[7], (3, 3, 3, C, C), (27 * C) ** -0.5, 0.109375)
    w_up = normal_values(key_of[8], (2, 2, 2, C, C), C ** -0.5, 0.5)
    return {"features": features, "owner": owner, "norm_gain": norm_gain, "time_shift": time_shift, "w_in": w_in, "w_out": w_out, "w_down": w_down, "w_conv": w_conv, "w_up": w_up}


def brick_down(bricks, live, norm_gain, time_shift, w_in, w_out, w_down):
    count, voxels, chan = bricks.shape
    stream = bricks.reshape(-1, chan)
    for layer in range(w_in.shape[0]):
        whole = stream.astype(jnp.float32)
        scale = lax.rsqrt(lax.optimization_barrier(jnp.mean(whole * whole, axis=-1, keepdims=True)) + 1e-06)
        normed = (whole * scale * norm_gain[layer]).astype(jnp.bfloat16)
        hidden = jax.nn.silu(jnp.dot(normed, w_in[layer], preferred_element_type=jnp.float32) + time_shift[layer]).astype(jnp.bfloat16)
        stream = (whole + jnp.dot(hidden, w_out[layer], preferred_element_type=jnp.float32)).astype(jnp.bfloat16)
    cells = stream.reshape(count, 4, 2, 4, 2, 4, 2, chan).astype(jnp.float32)
    down = jnp.einsum('giajbkcd,abcde->gijke', cells, w_down.astype(jnp.float32))
    return (jax.nn.silu(down).reshape(count, 64, chan) * live[:, None, None]).astype(jnp.bfloat16)

def brick_up(bricks, mixed, live, w_up):
    count, voxels, chan = bricks.shape
    coarse = mixed.reshape(count, 4, 4, 4, chan).astype(jnp.float32)
    upward = jnp.einsum('gijkd,abcde->giajbkce', coarse, w_up.astype(jnp.float32)).reshape(count, voxels, chan)
    return ((bricks.astype(jnp.float32) + upward) * live[:, None, None]).astype(jnp.bfloat16)

def reference(features, owner, norm_gain, time_shift, w_in, w_out, w_down, w_conv, w_up):
    columns = features.reshape(NBX * NBY, ZCAP, 512, C)
    live = (owner >= 0).astype(jnp.float32).reshape(NBX * NBY, ZCAP)
    coarse = lax.map(lambda pair: brick_down(pair[0], pair[1], norm_gain, time_shift, w_in, w_out, w_down), (columns, live))
    grid = coarse.reshape(NBX, NBY, ZCAP, 4, 4, 4, C).transpose(0, 3, 1, 4, 2, 5, 6).reshape(NBX * 4, NBY * 4, ZCAP * 4, C)
    padded = jnp.pad(grid, ((1, 1), (1, 1), (1, 1), (0, 0)))
    total = grid.astype(jnp.float32)
    for d in range(3):
        for e in range(3):
            for f in range(3):
                moved = padded[d:d + NBX * 4, e:e + NBY * 4, f:f + ZCAP * 4].reshape(-1, C)
                total = total + jnp.dot(moved, w_conv[d, e, f], preferred_element_type=jnp.float32).reshape(total.shape)
    live_grid = jnp.broadcast_to(live.reshape(NBX, 1, NBY, 1, ZCAP, 1, 1), (NBX, 4, NBY, 4, ZCAP, 4, 1)).reshape(NBX * 4, NBY * 4, ZCAP * 4, 1)
    mixed = (total * live_grid).astype(jnp.bfloat16)
    mixed = mixed.reshape(NBX, 4, NBY, 4, ZCAP, 4, C).transpose(0, 2, 4, 1, 3, 5, 6).reshape(NBX * NBY, ZCAP, 64, C)
    result = lax.map(lambda trio: brick_up(trio[0], trio[1], trio[2], w_up), (columns, mixed, live))
    return result.reshape(NBX, NBY, ZCAP, 512, C)
```

```python
import functools

import jax
import jax.numpy as jnp
from jax import lax
from jax.experimental import pallas as pl
from jax.experimental.pallas import tpu as pltpu
from jax.sharding import PartitionSpec as P

GROUP = 2
CHUNK = 256
VMEM_LIMIT = 56 * 1024 * 1024


def silu(value):
    half = 0.5 * value
    return half + half * jnp.tanh(half)


def down_kernel(
    owner_ref, feat_ref, gain_ref, shift_ref, w_in_ref, w_out_ref, w_down_ref, out_ref,
    held, stream, w_scaled, volume, index, sem,
):
    slots, voxels, chan = feat_ref.shape
    layers = w_in_ref.shape[0]
    cols_y, zcap = volume.shape[1] // 4, volume.shape[2] // 4

    def scan(slot, count):
        @pl.when(owner_ref[slot] >= 0)
        def _():
            index[count] = slot

        return count + (owner_ref[slot] >= 0).astype(jnp.int32)

    count = lax.fori_loop(0, slots, scan, 0)
    groups = (count + GROUP - 1) // GROUP

    def copies(group):
        side = lax.rem(group, 2)
        return [
            pltpu.make_async_copy(
                feat_ref.at[index[jnp.minimum(group * GROUP + b, count - 1)]],
                held.at[side, b],
                sem.at[side, b],
            )
            for b in range(GROUP)
        ]

    @pl.when(groups > 0)
    def _():
        for copy in copies(0):
            copy.start()

    for layer in range(layers):
        scale = 0.5 * gain_ref[:, layer : layer + 1]
        w_scaled[layer] = (w_in_ref[layer].astype(jnp.float32) * scale).astype(jnp.bfloat16)
    volume[...] = jnp.zeros_like(volume)

    pieces = GROUP * voxels // CHUNK

    def work(group, carry):
        @pl.when(group + 1 < groups)
        def _():
            for copy in copies(group + 1):
                copy.start()

        for copy in copies(group):
            copy.wait()
        side = lax.rem(group, 2)
        stream[...] = held[side].reshape(GROUP * voxels, chan).astype(jnp.float32)

        def enter(layer, piece):
            x = stream[piece * CHUNK : (piece + 1) * CHUNK]
            mean = jnp.mean(x * x, axis=-1, keepdims=True)
            normed = (x * lax.rsqrt(mean + 1e-6)).astype(jnp.bfloat16)
            return jnp.dot(normed, w_scaled[layer], preferred_element_type=jnp.float32)

        def leave(layer, piece, raw):
            half = (raw + 0.5 * shift_ref[pl.ds(layer, 1)]).astype(jnp.bfloat16)
            hidden = half + half * jnp.tanh(half)
            rows = slice(piece * CHUNK, (piece + 1) * CHUNK)
            stream[rows] = stream[rows] + jnp.dot(
                hidden, w_out_ref[layer], preferred_element_type=jnp.float32
            )

        def one_layer(layer, carry):
            raw = enter(layer, 0)
            for piece in range(pieces):
                later = enter(layer, piece + 1) if piece + 1 < pieces else None
                leave(layer, piece, raw)
                raw = later
            return carry

        lax.fori_loop(0, layers, one_layer, 0)

        weights = jnp.concatenate(
            [
                jnp.concatenate([w_down_ref[4 * a + c], w_down_ref[4 * a + 2 + c]], axis=1)
                for a in range(2)
                for c in range(2)
            ],
            axis=0,
        )
        for b in range(GROUP):
            slot = index[jnp.minimum(group * GROUP + b, count - 1)]
            taps = []
            for c in range(2):
                rows = stream[pl.ds(b * voxels + c, voxels // 2, stride=2)]
                taps.append(rows.astype(jnp.bfloat16).reshape(4, 2, 32, chan))
            cells = jnp.concatenate(
                [taps[c][:, a].reshape(128, chan) for a in range(2) for c in range(2)], axis=1
            )
            both = jnp.dot(cells, weights, preferred_element_type=jnp.float32)
            both = both.reshape(16, 8, 2 * chan)
            row = lax.broadcasted_iota(jnp.int32, (16, 8, chan), 1)
            part = jnp.where(row < 4, both[:, :, :chan], both[:, :, chan:])
            made = silu(part + pltpu.roll(part, 4, axis=1)).reshape(4, 4, 8, chan)
            z = lax.rem(slot, zcap)
            y = lax.rem(slot // zcap, cols_y)
            x = slot // (zcap * cols_y)
            where = (
                pl.ds(4 * x, 4),
                pl.ds(4 * y, 4),
                pl.ds(pl.multiple_of(8 * (z // 2), 8), 8),
            )
            row = lax.broadcasted_iota(jnp.int32, made.shape, 2)
            mine = (row // 4) == lax.rem(z, 2)
            volume[where] = jnp.where(mine, made, volume[where])
        return carry

    lax.fori_loop(0, groups, work, 0)
    out_ref[...] = volume[...].astype(jnp.bfloat16)


def up_kernel(cells_ref, feat_ref, live_ref, w_conv_ref, w_up_ref, out_ref, twice):
    chan = cells_ref.shape[-1]
    gsy, gsz = cells_ref.shape[1] - 2, cells_ref.shape[2]
    rows = gsy * gsz
    zcap = gsz // 4
    x = pl.program_id(0) * 4 + pl.program_id(1)
    planes = [cells_ref[x + d] for d in range(3)]
    near = jnp.concatenate(
        [planes[d][e : e + gsy].reshape(rows, chan) for d in range(3) for e in range(3)], axis=1
    )
    taps = jnp.concatenate(
        [
            jnp.concatenate([w_conv_ref[9 * d + 3 * e + f] for f in range(3)], axis=1)
            for d in range(3)
            for e in range(3)
        ],
        axis=0,
    )
    sums = jnp.dot(near, taps, preferred_element_type=jnp.float32).reshape(gsy, gsz, 3 * chan)
    z = lax.broadcasted_iota(jnp.int32, (gsy, gsz, chan), 1)
    below = jnp.where(z == 0, 0.0, pltpu.roll(sums[:, :, :chan], 1, axis=1))
    above = jnp.where(z == gsz - 1, 0.0, pltpu.roll(sums[:, :, 2 * chan :], gsz - 1, axis=1))
    total = planes[1][1 : 1 + gsy].astype(jnp.float32) + sums[:, :, chan : 2 * chan]
    total = (total + below + above).reshape(rows, chan)
    twice[pl.ds(0, rows, stride=2)] = total
    twice[pl.ds(1, rows, stride=2)] = total
    doubled = twice[...]
    odd = lax.rem(lax.broadcasted_iota(jnp.int32, doubled.shape, 0), 2) == 1
    split = jnp.concatenate(
        [jnp.where(odd, 0.0, doubled), jnp.where(odd, doubled, 0.0)], axis=1
    ).astype(jnp.bfloat16)
    weights = jnp.concatenate(
        [
            jnp.concatenate([w_up_ref[4 * a + 2 * b + c] for a in range(2) for b in range(2)], axis=1)
            for c in range(2)
        ],
        axis=0,
    )
    lifted = jnp.dot(split, weights, preferred_element_type=jnp.float32)
    line = 2 * gsz
    for q in range(gsy // 4):
        live = live_ref[0, q]
        live = jnp.concatenate([live, live], axis=1)
        for j in range(4):
            for a in range(2):
                top = lifted[(4 * q + j) * line : (4 * q + j + 1) * line]
                pair = [
                    top[:, (2 * a + b) * chan : (2 * a + b + 1) * chan].reshape(zcap, 8, chan)
                    for b in range(2)
                ]
                span = slice(64 * a + 16 * j, 64 * a + 16 * j + 16)
                whole = feat_ref[0, q, :, span].astype(jnp.float32) + jnp.concatenate(pair, axis=1)
                out_ref[0, q, :, span] = (whole * live).astype(jnp.bfloat16)


def extended(cells, sides, width):
    for axis, dim in sides:
        count = lax.axis_size(axis)
        ends = count - 1
        head = lax.slice_in_dim(cells, 0, width, axis=dim)
        tail = lax.slice_in_dim(cells, cells.shape[dim] - width, cells.shape[dim], axis=dim)
        cells = jnp.concatenate(
            [
                lax.ppermute(tail, axis, [(i, (i + 1) % count) for i in range(ends)]),
                cells,
                lax.ppermute(head, axis, [((i + 1) % count, i) for i in range(ends)]),
            ],
            axis=dim,
        )
    return cells


def local(features, owner, norm_gain, time_shift, w_in, w_out, w_down, w_conv, w_up):
    cols_x, cols_y, zcap, voxels, chan = features.shape
    slots = cols_x * cols_y * zcap
    gsx, gsy, gsz = cols_x * 4, cols_y * 4, zcap * 4
    layers, _, hid = w_in.shape
    vmem = pl.BlockSpec(memory_space=pltpu.VMEM)
    grid = pl.pallas_call(
        down_kernel,
        out_shape=jax.ShapeDtypeStruct((gsx, gsy, gsz, chan), jnp.bfloat16),
        in_specs=[
            pl.BlockSpec(memory_space=pltpu.SMEM),
            pl.BlockSpec(memory_space=pl.ANY),
            vmem, vmem, vmem, vmem, vmem,
        ],
        out_specs=vmem,
        scratch_shapes=[
            pltpu.VMEM((2, GROUP, voxels, chan), jnp.bfloat16),
            pltpu.VMEM((GROUP * voxels, chan), jnp.float32),
            pltpu.VMEM((layers, chan, hid), jnp.bfloat16),
            pltpu.VMEM((gsx, gsy, gsz, chan), jnp.float32),
            pltpu.SMEM((slots,), jnp.int32),
            pltpu.SemaphoreType.DMA((2, GROUP)),
        ],
        compiler_params=pltpu.CompilerParams(vmem_limit_bytes=VMEM_LIMIT),
        name="voxel_ff_down",
    )(
        owner.reshape(slots),
        features.reshape(slots, voxels, chan),
        norm_gain.T,
        time_shift,
        w_in,
        w_out,
        w_down.reshape(8, chan, chan),
    )
    rimmed = extended(grid, (("gx", 0), ("gy", 1)), 1)
    live = jnp.broadcast_to(
        (owner >= 0).astype(jnp.float32)[..., None, None], (cols_x, cols_y, zcap, 8, chan)
    )
    block = (1, cols_y, zcap, 2 * 64, chan)
    return pl.pallas_call(
        up_kernel,
        out_shape=jax.ShapeDtypeStruct(features.shape, jnp.bfloat16),
        grid=(cols_x, 4),
        in_specs=[
            vmem,
            pl.BlockSpec(block, lambda p, i: (p, 0, 0, i, 0)),
            pl.BlockSpec((1, cols_y, zcap, 8, chan), lambda p, i: (p, 0, 0, 0, 0)),
            vmem,
            vmem,
        ],
        out_specs=pl.BlockSpec(block, lambda p, i: (p, 0, 0, i, 0)),
        scratch_shapes=[pltpu.VMEM((2 * gsy * gsz, chan), jnp.float32)],
        compiler_params=pltpu.CompilerParams(vmem_limit_bytes=VMEM_LIMIT),
        name="conv_up",
    )(rimmed, features, live, w_conv.reshape(27, chan, chan), w_up.reshape(8, chan, chan))


def solution(mesh):
    in_specs = (
        P("gx", "gy", None, None, None),
        P("gx", "gy", None),
        P(),
        P(),
        P(),
        P(),
        P(),
        P(),
        P(),
    )
    out_specs = P("gx", "gy", None, None, None)
    return jax.shard_map(local, mesh=mesh, in_specs=in_specs, out_specs=out_specs, check_vma=False)
```

```python
import functools

import jax
import jax.numpy as jnp
from jax import lax
from jax.experimental import pallas as pl
from jax.experimental.pallas import tpu as pltpu
from jax.sharding import PartitionSpec as P

GROUP = 4
CHUNK = 256
UNROLL = 2
VMEM_LIMIT = 56 * 1024 * 1024


def silu(value):
    half = 0.5 * value
    return half + half * jnp.tanh(half)


def down_kernel(
    owner_ref, feat_ref, gain_ref, shift_ref, w_in_ref, w_out_ref, w_down_ref, out_ref,
    held, stream, ahead, w_scaled, volume, index, sem,
):
    cols_x, cols_y, zcap, voxels, chan = feat_ref.shape
    slots = cols_x * cols_y * zcap
    layers = w_in_ref.shape[0]

    def place(slot):
        return slot // (zcap * cols_y), lax.rem(slot // zcap, cols_y), lax.rem(slot, zcap)

    def scan(slot, count):
        alive = owner_ref[place(slot)] >= 0

        @pl.when(alive)
        def _():
            index[count] = slot

        return count + alive.astype(jnp.int32)

    count = lax.fori_loop(0, slots, scan, 0)
    groups = (count + GROUP - 1) // GROUP

    def copies(group):
        side = lax.rem(group, 2)
        return [
            pltpu.make_async_copy(
                feat_ref.at[place(index[jnp.minimum(group * GROUP + b, count - 1)])],
                held.at[side, b],
                sem.at[side, b],
            )
            for b in range(GROUP)
        ]

    @pl.when(groups > 0)
    def _():
        for copy in copies(0):
            copy.start()

    across = lax.broadcasted_iota(jnp.int32, (chan, chan), 1)
    down = lax.broadcasted_iota(jnp.int32, (chan, chan), 0)
    for layer in range(layers):
        gain = jnp.where(across == down, 0.5 * gain_ref[layer : layer + 1], 0.0)
        gain = jnp.sum(gain, axis=1, keepdims=True)
        w_scaled[layer] = (w_in_ref[layer].astype(jnp.float32) * gain).astype(jnp.bfloat16)
    volume[...] = jnp.zeros_like(volume)

    pieces = GROUP * voxels // CHUNK

    def work(group, carry):
        @pl.when(group + 1 < groups)
        def _():
            for copy in copies(group + 1):
                copy.start()

        for copy in copies(group):
            copy.wait()
        side = lax.rem(group, 2)
        stream[...] = held[side].reshape(GROUP * voxels, chan).astype(jnp.float32)

        def enter(layer, piece):
            x = stream[piece * CHUNK : (piece + 1) * CHUNK]
            mean = jnp.mean(x * x, axis=-1, keepdims=True)
            normed = (x * lax.rsqrt(mean + 1e-6)).astype(jnp.bfloat16)
            raw = jnp.dot(normed, w_scaled[layer], preferred_element_type=jnp.float32)
            shift = (0.5 * shift_ref[pl.ds(layer, 1)]).astype(jnp.bfloat16)
            return raw.astype(jnp.bfloat16) + shift

        def leave(layer, piece, half):
            hidden = half + half * jnp.tanh(half)
            rows = slice(piece * CHUNK, (piece + 1) * CHUNK)
            stream[rows] = stream[rows] + jnp.dot(
                hidden, w_out_ref[layer], preferred_element_type=jnp.float32
            )

        def some_layers(step, carry):
            half = ahead[...]
            for more in range(UNROLL):
                layer = step * UNROLL + more
                for piece in range(pieces):
                    if piece + 1 < pieces:
                        later = enter(layer, piece + 1)
                    else:
                        later = enter(jnp.minimum(layer + 1, layers - 1), 0)
                    leave(layer, piece, half)
                    half = later
            ahead[...] = half
            return carry

        ahead[...] = enter(0, 0)
        lax.fori_loop(0, layers // UNROLL, some_layers, 0)

        weights = jnp.concatenate(
            [
                jnp.concatenate([w_down_ref[4 * a + c], w_down_ref[4 * a + 2 + c]], axis=1)
                for a in range(2)
                for c in range(2)
            ],
            axis=0,
        )
        for b in range(GROUP):
            slot = index[jnp.minimum(group * GROUP + b, count - 1)]
            taps = []
            for c in range(2):
                rows = stream[pl.ds(b * voxels + c, voxels // 2, stride=2)]
                taps.append(rows.astype(jnp.bfloat16).reshape(4, 2, 32, chan))
            cells = jnp.concatenate(
                [taps[c][:, a].reshape(128, chan) for a in range(2) for c in range(2)], axis=1
            )
            both = jnp.dot(cells, weights, preferred_element_type=jnp.float32)
            both = both.reshape(16, 8, 2 * chan)
            row = lax.broadcasted_iota(jnp.int32, (16, 8, chan), 1)
            part = jnp.where(row < 4, both[:, :, :chan], both[:, :, chan:])
            made = silu(part + pltpu.roll(part, 4, axis=1)).reshape(4, 4, 8, chan)
            x, y, z = place(slot)
            where = (
                pl.ds(4 * x, 4),
                pl.ds(4 * y, 4),
                pl.ds(pl.multiple_of(8 * (z // 2), 8), 8),
            )
            row = lax.broadcasted_iota(jnp.int32, made.shape, 2)
            mine = (row // 4) == lax.rem(z, 2)
            volume[where] = jnp.where(mine, made, volume[where])
        return carry

    lax.fori_loop(0, groups, work, 0)
    out_ref[...] = volume[...].astype(jnp.bfloat16)


def up_kernel(owner_ref, cells_ref, feat_ref, w_conv_ref, w_up_ref, out_ref, twice, live):
    chan = cells_ref.shape[-1]
    gsx, gsy, gsz = cells_ref.shape[0] - 2, cells_ref.shape[1] - 2, cells_ref.shape[2]
    rows = gsy * gsz
    zcap = gsz // 4
    step = pl.program_id(0)
    column = jnp.maximum(step - 1, 0) // 4
    side = lax.rem(step, 2)

    for q in range(gsy // 4):
        for r in range(zcap):
            alive = (owner_ref[column, q, r] >= 0).astype(jnp.float32)
            live[q, r] = jnp.full((16, chan), alive, jnp.float32)

    doubled = twice[1 - side]
    odd = lax.rem(lax.broadcasted_iota(jnp.int32, doubled.shape, 0), 2) == 1
    split = jnp.concatenate(
        [jnp.where(odd, 0.0, doubled), jnp.where(odd, doubled, 0.0)], axis=1
    ).astype(jnp.bfloat16)
    weights = jnp.concatenate(
        [
            jnp.concatenate([w_up_ref[4 * a + 2 * b + c] for a in range(2) for b in range(2)], axis=1)
            for c in range(2)
        ],
        axis=0,
    )
    line = 2 * gsz
    for q in range(gsy // 4):
        for j in range(4):
            span = slice((4 * q + j) * line, (4 * q + j + 1) * line)
            top = jnp.dot(split[span], weights, preferred_element_type=jnp.float32)
            for a in range(2):
                pair = [
                    top[:, (2 * a + b) * chan : (2 * a + b + 1) * chan].reshape(zcap, 8, chan)
                    for b in range(2)
                ]
                span = slice(64 * a + 16 * j, 64 * a + 16 * j + 16)
                whole = feat_ref[0, q, :, span].astype(jnp.float32) + jnp.concatenate(pair, axis=1)
                out_ref[0, q, :, span] = (whole * live[q]).astype(jnp.bfloat16)

    x = jnp.minimum(step, gsx - 1)
    planes = [cells_ref[x + d] for d in range(3)]
    near = jnp.concatenate(
        [planes[d][e : e + gsy].reshape(rows, chan) for d in range(3) for e in range(3)], axis=1
    )
    taps = jnp.concatenate(
        [
            jnp.concatenate([w_conv_ref[9 * d + 3 * e + f] for f in range(3)], axis=1)
            for d in range(3)
            for e in range(3)
        ],
        axis=0,
    )
    sums = jnp.dot(near, taps, preferred_element_type=jnp.float32).reshape(gsy, gsz, 3 * chan)
    z = lax.broadcasted_iota(jnp.int32, (gsy, gsz, chan), 1)
    below = jnp.where(z == 0, 0.0, pltpu.roll(sums[:, :, :chan], 1, axis=1))
    above = jnp.where(z == gsz - 1, 0.0, pltpu.roll(sums[:, :, 2 * chan :], gsz - 1, axis=1))
    total = planes[1][1 : 1 + gsy].astype(jnp.float32) + sums[:, :, chan : 2 * chan]
    total = (total + below + above).reshape(rows, chan)
    twice[side, pl.ds(0, rows, stride=2)] = total
    twice[side, pl.ds(1, rows, stride=2)] = total


def extended(cells, sides, width):
    for axis, dim in sides:
        count = lax.axis_size(axis)
        ends = count - 1
        head = lax.slice_in_dim(cells, 0, width, axis=dim)
        tail = lax.slice_in_dim(cells, cells.shape[dim] - width, cells.shape[dim], axis=dim)
        cells = jnp.concatenate(
            [
                lax.ppermute(tail, axis, [(i, (i + 1) % count) for i in range(ends)]),
                cells,
                lax.ppermute(head, axis, [((i + 1) % count, i) for i in range(ends)]),
            ],
            axis=dim,
        )
    return cells


def local(features, owner, norm_gain, time_shift, w_in, w_out, w_down, w_conv, w_up):
    cols_x, cols_y, zcap, voxels, chan = features.shape
    slots = cols_x * cols_y * zcap
    gsx, gsy, gsz = cols_x * 4, cols_y * 4, zcap * 4
    layers, _, hid = w_in.shape
    vmem = pl.BlockSpec(memory_space=pltpu.VMEM)
    grid = pl.pallas_call(
        down_kernel,
        out_shape=jax.ShapeDtypeStruct((gsx, gsy, gsz, chan), jnp.bfloat16),
        in_specs=[
            pl.BlockSpec(memory_space=pltpu.SMEM),
            pl.BlockSpec(memory_space=pl.ANY),
            vmem, vmem, vmem, vmem, vmem,
        ],
        out_specs=vmem,
        scratch_shapes=[
            pltpu.VMEM((2, GROUP, voxels, chan), jnp.bfloat16),
            pltpu.VMEM((GROUP * voxels, chan), jnp.float32),
            pltpu.VMEM((CHUNK, hid), jnp.bfloat16),
            pltpu.VMEM((layers, chan, hid), jnp.bfloat16),
            pltpu.VMEM((gsx, gsy, gsz, chan), jnp.float32),
            pltpu.SMEM((slots,), jnp.int32),
            pltpu.SemaphoreType.DMA((2, GROUP)),
        ],
        compiler_params=pltpu.CompilerParams(vmem_limit_bytes=VMEM_LIMIT),
        name="voxel_ff_down",
    )(
        owner,
        features,
        norm_gain,
        time_shift,
        w_in,
        w_out,
        w_down.reshape(8, chan, chan),
    )
    rimmed = extended(grid, (("gx", 0), ("gy", 1)), 1)
    block = (1, cols_y, zcap, 2 * 64, chan)

    def spot(step):
        plane = jnp.maximum(step - 1, 0)
        return plane // 4, 0, 0, lax.rem(plane, 4), 0

    return pl.pallas_call(
        up_kernel,
        out_shape=jax.ShapeDtypeStruct(features.shape, jnp.bfloat16),
        grid=(gsx + 1,),
        in_specs=[
            pl.BlockSpec(memory_space=pltpu.SMEM),
            vmem,
            pl.BlockSpec(block, spot),
            vmem,
            vmem,
        ],
        out_specs=pl.BlockSpec(block, spot),
        scratch_shapes=[
            pltpu.VMEM((2, 2 * gsy * gsz, chan), jnp.float32),
            pltpu.VMEM((cols_y, zcap, 16, chan), jnp.float32),
        ],
        compiler_params=pltpu.CompilerParams(vmem_limit_bytes=VMEM_LIMIT),
        name="conv_up",
    )(owner, rimmed, features, w_conv.reshape(27, chan, chan), w_up.reshape(8, chan, chan))


def solution(mesh):
    in_specs = (
        P("gx", "gy", None, None, None),
        P("gx", "gy", None),
        P(),
        P(),
        P(),
        P(),
        P(),
        P(),
        P(),
    )
    out_specs = P("gx", "gy", None, None, None)
    return jax.shard_map(local, mesh=mesh, in_specs=in_specs, out_specs=out_specs, check_vma=False)
```

```python
import functools

import jax
import jax.numpy as jnp
from jax import lax
from jax.experimental import pallas as pl
from jax.experimental.pallas import tpu as pltpu
from jax.sharding import PartitionSpec as P

GROUP = 4
CHUNK = 512
UNROLL = 2
VMEM_LIMIT = 56 * 1024 * 1024


def silu(value):
    half = 0.5 * value
    return half + half * jnp.tanh(half)


def down_kernel(
    owner_ref, feat_ref, gain_ref, shift_ref, w_in_ref, w_out_ref, w_down_ref,
    out_ref, x_low_ref, x_high_ref, y_low_ref, y_high_ref,
    held, stream, ahead, w_scaled, volume, index, sem,
):
    cols_x, cols_y, zcap, voxels, chan = feat_ref.shape
    slots = cols_x * cols_y * zcap
    layers = w_in_ref.shape[0]

    def place(slot):
        return slot // (zcap * cols_y), lax.rem(slot // zcap, cols_y), lax.rem(slot, zcap)

    def scan(slot, count):
        alive = owner_ref[place(slot)] >= 0

        @pl.when(alive)
        def _():
            index[count] = slot

        return count + alive.astype(jnp.int32)

    count = lax.fori_loop(0, slots, scan, 0)
    groups = (count + GROUP - 1) // GROUP

    def copies(group):
        side = lax.rem(group, 2)
        return [
            pltpu.make_async_copy(
                feat_ref.at[place(index[jnp.minimum(group * GROUP + b, count - 1)])],
                held.at[side, b],
                sem.at[side, b],
            )
            for b in range(GROUP)
        ]

    @pl.when(groups > 0)
    def _():
        for copy in copies(0):
            copy.start()

    across = lax.broadcasted_iota(jnp.int32, (chan, chan), 1)
    down = lax.broadcasted_iota(jnp.int32, (chan, chan), 0)
    for layer in range(layers):
        gain = jnp.where(across == down, 0.5 * gain_ref[layer : layer + 1], 0.0)
        gain = jnp.sum(gain, axis=1, keepdims=True)
        w_scaled[layer] = (w_in_ref[layer].astype(jnp.float32) * gain).astype(jnp.bfloat16)
    volume[...] = jnp.zeros_like(volume)

    pieces = GROUP * voxels // CHUNK

    def work(group, carry):
        @pl.when(group + 1 < groups)
        def _():
            for copy in copies(group + 1):
                copy.start()

        for copy in copies(group):
            copy.wait()
        side = lax.rem(group, 2)
        stream[...] = held[side].reshape(GROUP * voxels, chan).astype(jnp.float32)

        def enter(layer, piece):
            x = stream[piece * CHUNK : (piece + 1) * CHUNK]
            mean = jnp.mean(x * x, axis=-1, keepdims=True)
            normed = (x * lax.rsqrt(mean + 1e-6)).astype(jnp.bfloat16)
            raw = jnp.dot(normed, w_scaled[layer], preferred_element_type=jnp.float32)
            shift = (0.5 * shift_ref[pl.ds(layer, 1)]).astype(jnp.bfloat16)
            return raw.astype(jnp.bfloat16) + shift

        def leave(layer, piece, half):
            hidden = half + half * jnp.tanh(half)
            rows = slice(piece * CHUNK, (piece + 1) * CHUNK)
            stream[rows] = stream[rows] + jnp.dot(
                hidden, w_out_ref[layer], preferred_element_type=jnp.float32
            )

        def some_layers(step, carry):
            half = ahead[...]
            for more in range(UNROLL):
                layer = step * UNROLL + more
                for piece in range(pieces):
                    if piece + 1 < pieces:
                        later = enter(layer, piece + 1)
                    else:
                        later = enter(jnp.minimum(layer + 1, layers - 1), 0)
                    leave(layer, piece, half)
                    half = later
            ahead[...] = half
            return carry

        ahead[...] = enter(0, 0)
        lax.fori_loop(0, layers // UNROLL, some_layers, 0)

        weights = jnp.concatenate(
            [
                jnp.concatenate([w_down_ref[4 * a + c], w_down_ref[4 * a + 2 + c]], axis=1)
                for a in range(2)
                for c in range(2)
            ],
            axis=0,
        )
        for b in range(GROUP):
            slot = index[jnp.minimum(group * GROUP + b, count - 1)]
            taps = []
            for c in range(2):
                rows = stream[pl.ds(b * voxels + c, voxels // 2, stride=2)]
                taps.append(rows.astype(jnp.bfloat16).reshape(4, 2, 32, chan))
            cells = jnp.concatenate(
                [taps[c][:, a].reshape(128, chan) for a in range(2) for c in range(2)], axis=1
            )
            both = jnp.dot(cells, weights, preferred_element_type=jnp.float32)
            both = both.reshape(16, 8, 2 * chan)
            row = lax.broadcasted_iota(jnp.int32, (16, 8, chan), 1)
            part = jnp.where(row < 4, both[:, :, :chan], both[:, :, chan:])
            made = silu(part + pltpu.roll(part, 4, axis=1)).reshape(4, 4, 8, chan)
            x, y, z = place(slot)
            where = (
                pl.ds(4 * x, 4),
                pl.ds(4 * y, 4),
                pl.ds(pl.multiple_of(8 * (z // 2), 8), 8),
            )
            row = lax.broadcasted_iota(jnp.int32, made.shape, 2)
            mine = (row // 4) == lax.rem(z, 2)
            volume[where] = jnp.where(mine, made, volume[where])
        return carry

    lax.fori_loop(0, groups, work, 0)
    out_ref[...] = volume[...].astype(jnp.bfloat16)
    x_low_ref[...] = out_ref[0]
    x_high_ref[...] = out_ref[out_ref.shape[0] - 1]
    y_low_ref[...] = out_ref[:, 0]
    y_high_ref[...] = out_ref[:, out_ref.shape[1] - 1]


def shifted(sums, chan):
    z = lax.broadcasted_iota(jnp.int32, sums.shape[:2] + (chan,), 1)
    length = sums.shape[1]
    below = jnp.where(z == 0, 0.0, pltpu.roll(sums[:, :, :chan], 1, axis=1))
    above = jnp.where(z == length - 1, 0.0, pltpu.roll(sums[:, :, 2 * chan :], length - 1, axis=1))
    return sums[:, :, chan : 2 * chan] + below + above


def conv_lines(pieces, w_conv_ref):
    lines, gsz, chan = pieces[0][2].shape
    near = jnp.concatenate([piece.reshape(lines * gsz, chan) for _, _, piece in pieces], axis=1)
    taps = jnp.concatenate(
        [
            jnp.concatenate([w_conv_ref[9 * d + 3 * e + f] for f in range(3)], axis=1)
            for d, e, _ in pieces
        ],
        axis=0,
    )
    sums = jnp.dot(near, taps, preferred_element_type=jnp.float32)
    return shifted(sums.reshape(lines, gsz, 3 * chan), chan)


def moved_lines(lines, e):
    blank = jnp.zeros((1,) + lines.shape[1:], lines.dtype)
    if e == 0:
        return jnp.concatenate([blank, lines[:-1]], axis=0)
    if e == 2:
        return jnp.concatenate([lines[1:], blank], axis=0)
    return lines


def own_kernel(first, cells_ref, w_conv_ref, out_ref):
    gsx = cells_ref.shape[0]
    for plane in range(out_ref.shape[0]):
        x = first + plane
        pieces = [
            (d, e, moved_lines(cells_ref[x + d - 1], e))
            for d in range(3)
            if 0 <= x + d - 1 < gsx
            for e in range(3)
        ]
        total = cells_ref[x].astype(jnp.float32) + conv_lines(pieces, w_conv_ref)
        out_ref[plane] = total.astype(jnp.bfloat16)


def up_kernel(
    owner_ref, near_ref, far_ref, x_low_ref, x_high_ref, y_low_ref, y_high_ref, feat_ref, w_conv_ref,
    w_up_ref, out_ref, total, twice, live,
):
    gsx, gsy, gsz, chan = total.shape
    rows = gsy * gsz
    zcap = gsz // 4
    step = pl.program_id(0)
    column = step // 4

    @pl.when(step == 0)
    def _():
        half = gsx // 2
        total[:half] = near_ref[...].astype(jnp.float32)
        total[half:] = far_ref[...].astype(jnp.float32)
        for line, ref, e in ((0, y_low_ref, 0), (gsy - 1, y_high_ref, 2)):
            pieces = [(d, e, ref[d : d + gsx]) for d in range(3)]
            total[:, line] = total[:, line] + conv_lines(pieces, w_conv_ref)
        for plane, ref, d in ((0, x_low_ref, 0), (gsx - 1, x_high_ref, 2)):
            pieces = [(d, e, moved_lines(ref[...], e)) for e in range(3)]
            total[plane] = total[plane] + conv_lines(pieces, w_conv_ref)

    @pl.when(lax.rem(step, 4) == 0)
    def _():
        for q in range(gsy // 4):
            for r in range(zcap):
                alive = (owner_ref[column, q, r] >= 0).astype(jnp.float32)
                live[q, r] = jnp.full((16, chan), alive, jnp.float32)

    mixed = total[step].reshape(rows, chan)
    twice[pl.ds(0, rows, stride=2)] = mixed
    twice[pl.ds(1, rows, stride=2)] = mixed
    doubled = twice[...]
    odd = lax.rem(lax.broadcasted_iota(jnp.int32, doubled.shape, 0), 2) == 1
    split = jnp.concatenate(
        [jnp.where(odd, 0.0, doubled), jnp.where(odd, doubled, 0.0)], axis=1
    ).astype(jnp.bfloat16)
    weights = jnp.concatenate(
        [
            jnp.concatenate([w_up_ref[4 * a + 2 * b + c] for a in range(2) for b in range(2)], axis=1)
            for c in range(2)
        ],
        axis=0,
    )
    line = 2 * gsz
    for q in range(gsy // 4):
        for j in range(4):
            span = slice((4 * q + j) * line, (4 * q + j + 1) * line)
            top = jnp.dot(split[span], weights, preferred_element_type=jnp.float32)
            for a in range(2):
                pair = [
                    top[:, (2 * a + b) * chan : (2 * a + b + 1) * chan].reshape(zcap, 8, chan)
                    for b in range(2)
                ]
                span = slice(64 * a + 16 * j, 64 * a + 16 * j + 16)
                whole = feat_ref[0, q, :, span].astype(jnp.float32) + jnp.concatenate(pair, axis=1)
                out_ref[0, q, :, span] = (whole * live[q]).astype(jnp.bfloat16)


def exchange(low, high, axis):
    count = lax.axis_size(axis)
    up = [(i, i + 1) for i in range(count - 1)]
    return lax.ppermute(high, axis, up), lax.ppermute(low, axis, [(j, i) for i, j in up])


def local(features, owner, norm_gain, time_shift, w_in, w_out, w_down, w_conv, w_up):
    cols_x, cols_y, zcap, voxels, chan = features.shape
    slots = cols_x * cols_y * zcap
    gsx, gsy, gsz = cols_x * 4, cols_y * 4, zcap * 4
    layers, _, hid = w_in.shape
    vmem = pl.BlockSpec(memory_space=pltpu.VMEM)
    smem = pl.BlockSpec(memory_space=pltpu.SMEM)
    params = pltpu.CompilerParams(vmem_limit_bytes=VMEM_LIMIT)

    def cells(*shape):
        return jax.ShapeDtypeStruct(shape + (gsz, chan), jnp.bfloat16)

    grid, x_low, x_high, y_low, y_high = pl.pallas_call(
        down_kernel,
        out_shape=[cells(gsx, gsy), cells(gsy), cells(gsy), cells(gsx), cells(gsx)],
        in_specs=[smem, pl.BlockSpec(memory_space=pl.ANY), vmem, vmem, vmem, vmem, vmem],
        out_specs=[vmem] * 5,
        scratch_shapes=[
            pltpu.VMEM((2, GROUP, voxels, chan), jnp.bfloat16),
            pltpu.VMEM((GROUP * voxels, chan), jnp.float32),
            pltpu.VMEM((CHUNK, hid), jnp.bfloat16),
            pltpu.VMEM((layers, chan, hid), jnp.bfloat16),
            pltpu.VMEM((gsx, gsy, gsz, chan), jnp.float32),
            pltpu.SMEM((slots,), jnp.int32),
            pltpu.SemaphoreType.DMA((2, GROUP)),
        ],
        compiler_params=params,
        name="voxel_ff_down",
    )(owner, features, norm_gain, time_shift, w_in, w_out, w_down.reshape(8, chan, chan))

    taps = w_conv.reshape(27, chan, chan)
    half = gsx // 2
    flops = 2 * 27 * half * gsy * gsz * chan * chan
    own = [
        pl.pallas_call(
            functools.partial(own_kernel, first),
            out_shape=cells(half, gsy),
            in_specs=[vmem, vmem],
            out_specs=vmem,
            compiler_params=params,
            cost_estimate=pl.CostEstimate(
                flops=4 * flops, bytes_accessed=4 * 1024 * 1024, transcendentals=0
            ),
            name="conv_own",
        )(grid, taps)
        for first in (0, half)
    ]
    x_low, x_high = exchange(x_low, x_high, "gx")
    y_low = jnp.concatenate([x_low[:1], y_low, x_high[:1]], axis=0)
    y_high = jnp.concatenate([x_low[-1:], y_high, x_high[-1:]], axis=0)
    y_low, y_high = exchange(y_low, y_high, "gy")

    block = (1, cols_y, zcap, 2 * 64, chan)

    def spot(plane):
        return plane // 4, 0, 0, lax.rem(plane, 4), 0

    return pl.pallas_call(
        up_kernel,
        out_shape=jax.ShapeDtypeStruct(features.shape, jnp.bfloat16),
        grid=(gsx,),
        in_specs=[smem] + [vmem] * 6 + [pl.BlockSpec(block, spot), vmem, vmem],
        out_specs=pl.BlockSpec(block, spot),
        scratch_shapes=[
            pltpu.VMEM((gsx, gsy, gsz, chan), jnp.float32),
            pltpu.VMEM((2 * gsy * gsz, chan), jnp.float32),
            pltpu.VMEM((cols_y, zcap, 16, chan), jnp.float32),
        ],
        compiler_params=params,
        name="rim_up",
    )(
        owner, *own, x_low, x_high, y_low, y_high, features, taps, w_up.reshape(8, chan, chan)
    )


def solution(mesh):
    in_specs = (
        P("gx", "gy", None, None, None),
        P("gx", "gy", None),
        P(),
        P(),
        P(),
        P(),
        P(),
        P(),
        P(),
    )
    out_specs = P("gx", "gy", None, None, None)
    return jax.shard_map(local, mesh=mesh, in_specs=in_specs, out_specs=out_specs, check_vma=False)
```

```python
import functools

import jax
import jax.numpy as jnp
from jax import lax
from jax.experimental import pallas as pl
from jax.experimental.pallas import tpu as pltpu
from jax.sharding import PartitionSpec as P

GROUP = 4
MOST = 32
VMEM_LIMIT = 56 * 1024 * 1024


def silu(value):
    half = 0.5 * value
    return half + half * jnp.tanh(half)


def place(slot, cols_y, zcap):
    return slot // (zcap * cols_y), lax.rem(slot // zcap, cols_y), lax.rem(slot, zcap)


def down_kernel(
    owner_ref, feat_ref, gain_ref, shift_ref, w_in_ref, w_out_ref, w_down_ref,
    out_ref, x_low_ref, x_high_ref, y_low_ref, y_high_ref, blank_ref,
    held, stream, made, w_in, w_out, volume, zeros, index, sem, w_sem, zero_sem,
):
    cols_x, cols_y, zcap, voxels, chan = feat_ref.shape
    slots = cols_x * cols_y * zcap
    layers = w_in.shape[0]
    loads = [
        pltpu.make_async_copy(w_in_ref, w_in, w_sem.at[0]),
        pltpu.make_async_copy(w_out_ref, w_out, w_sem.at[1]),
    ]
    for load in loads:
        load.start()
    zeros[...] = jnp.zeros_like(zeros)

    def at(slot):
        return place(slot, cols_y, zcap)

    def blank(slot):
        return pltpu.make_async_copy(zeros, blank_ref.at[at(slot)], zero_sem.at[slot])

    def scan(slot, count):
        alive = owner_ref[at(slot)] >= 0

        @pl.when(alive)
        def _():
            index[count] = slot

        return count + alive.astype(jnp.int32)

    count = lax.fori_loop(0, slots, scan, 0)
    groups = (count + GROUP - 1) // GROUP

    def slot_of(group, b):
        return index[jnp.minimum(group * GROUP + b, count - 1)]

    def copies(group):
        side = lax.rem(group, 2)
        return [
            pltpu.make_async_copy(
                feat_ref.at[at(slot_of(group, b))], held.at[side, b], sem.at[side, b]
            )
            for b in range(GROUP)
        ]

    @pl.when(groups > 0)
    def _():
        for copy in copies(0):
            copy.start()

    @pl.loop(0, slots)
    def _(slot):
        @pl.when(owner_ref[at(slot)] < 0)
        def _():
            blank(slot).start()

    volume[...] = jnp.zeros_like(volume)
    across = lax.broadcasted_iota(jnp.int32, (chan, chan), 1)
    below = lax.broadcasted_iota(jnp.int32, (chan, chan), 0)
    loads[0].wait()
    for layer in range(layers):
        gain = jnp.where(across == below, gain_ref[layer : layer + 1], 0.0)
        gain = jnp.sum(gain, axis=1, keepdims=True) * (0.5 * chan**0.5)
        w_in[layer] = (w_in[layer].astype(jnp.float32) * gain).astype(jnp.bfloat16)
    loads[1].wait()

    def down(group, b):
        slot = slot_of(group, b)
        weights = jnp.concatenate(
            [
                jnp.concatenate([w_down_ref[4 * a + c], w_down_ref[4 * a + 2 + c]], axis=1)
                for a in range(2)
                for c in range(2)
            ],
            axis=0,
        )
        taps = []
        for c in range(2):
            rows = made[b, pl.ds(c, voxels // 2, stride=2)]
            taps.append(rows.astype(jnp.bfloat16).reshape(4, 2, 32, chan))
        cells = jnp.concatenate(
            [taps[c][:, a].reshape(128, chan) for a in range(2) for c in range(2)], axis=1
        )
        both = jnp.dot(cells, weights, preferred_element_type=jnp.float32)
        both = both.reshape(16, 8, 2 * chan)
        row = lax.broadcasted_iota(jnp.int32, (16, 8, chan), 1)
        part = jnp.where(row < 4, both[:, :, :chan], both[:, :, chan:])
        coarse = silu(part + pltpu.roll(part, 4, axis=1)).reshape(4, 4, 8, chan)
        x, y, z = at(slot)
        where = (
            pl.ds(4 * x, 4),
            pl.ds(4 * y, 4),
            pl.ds(pl.multiple_of(8 * (z // 2), 8), 8),
        )
        row = lax.broadcasted_iota(jnp.int32, coarse.shape, 2)
        mine = (row // 4) == lax.rem(z, 2)
        volume[where] = jnp.where(mine, coarse, volume[where])

    def work(group, carry):
        @pl.when(group + 1 < groups)
        def _():
            for copy in copies(group + 1):
                copy.start()

        for copy in copies(group):
            copy.wait()
        side = lax.rem(group, 2)

        def value(layer, b):
            return held[side, b].astype(jnp.float32) if layer == 0 else stream[b]

        def enter(layer, b):
            x = value(layer, b)
            power = jnp.sum(x * x, axis=-1, keepdims=True)
            normed = (x * lax.rsqrt(power + chan * 1e-6)).astype(jnp.bfloat16)
            raw = jnp.dot(normed, w_in[layer], preferred_element_type=jnp.float32)
            shift = (0.5 * shift_ref[layer : layer + 1]).astype(jnp.bfloat16)
            return raw.astype(jnp.bfloat16) + shift

        def leave(layer, b, half):
            hidden = half + half * jnp.tanh(half)
            result = value(layer, b) + jnp.dot(
                hidden, w_out[layer], preferred_element_type=jnp.float32
            )
            if layer + 1 < layers:
                stream[b] = result
            else:
                made[b] = result

        order = [(layer, b) for layer in range(layers) for b in range(GROUP)]
        half = enter(*order[0])
        for spot, here in enumerate(order):
            later = enter(*order[spot + 1]) if spot + 1 < len(order) else None
            leave(*here, half)
            if here[0] == 1:
                down(jnp.maximum(group - 1, 0), here[1])
            half = later
        return carry

    lax.fori_loop(0, groups, work, 0)

    @pl.when(groups > 0)
    def _():
        for b in range(GROUP):
            down(groups - 1, b)

    out_ref[...] = volume[...].astype(jnp.bfloat16)
    x_low_ref[...] = out_ref[0]
    x_high_ref[...] = out_ref[out_ref.shape[0] - 1]
    y_low_ref[...] = out_ref[:, 0]
    y_high_ref[...] = out_ref[:, out_ref.shape[1] - 1]

    @pl.loop(0, slots)
    def _(slot):
        @pl.when(owner_ref[at(slot)] < 0)
        def _():
            blank(slot).wait()


def shifted(sums, chan):
    z = lax.broadcasted_iota(jnp.int32, sums.shape[:2] + (chan,), 1)
    length = sums.shape[1]
    below = jnp.where(z == 0, 0.0, pltpu.roll(sums[:, :, :chan], 1, axis=1))
    above = jnp.where(z == length - 1, 0.0, pltpu.roll(sums[:, :, 2 * chan :], length - 1, axis=1))
    return sums[:, :, chan : 2 * chan] + below + above


def conv_lines(pieces, w_conv_ref):
    lines, gsz, chan = pieces[0][2].shape
    near = jnp.concatenate([piece.reshape(lines * gsz, chan) for _, _, piece in pieces], axis=1)
    taps = jnp.concatenate(
        [
            jnp.concatenate([w_conv_ref[9 * d + 3 * e + f] for f in range(3)], axis=1)
            for d, e, _ in pieces
        ],
        axis=0,
    )
    sums = jnp.dot(near, taps, preferred_element_type=jnp.float32)
    return shifted(sums.reshape(lines, gsz, 3 * chan), chan)


def moved_lines(lines, e):
    blank = jnp.zeros((1,) + lines.shape[1:], lines.dtype)
    if e == 0:
        return jnp.concatenate([blank, lines[:-1]], axis=0)
    if e == 2:
        return jnp.concatenate([lines[1:], blank], axis=0)
    return lines


def own_kernel(first, cells_ref, w_conv_ref, out_ref):
    gsx = cells_ref.shape[0]
    for plane in range(out_ref.shape[0]):
        x = first + plane
        pieces = [
            (d, e, moved_lines(cells_ref[x + d - 1], e))
            for d in range(3)
            if 0 <= x + d - 1 < gsx
            for e in range(3)
        ]
        total = cells_ref[x].astype(jnp.float32) + conv_lines(pieces, w_conv_ref)
        out_ref[plane] = total.astype(jnp.bfloat16)


def up_kernel(
    owner_ref, near_ref, far_ref, x_low_ref, x_high_ref, y_low_ref, y_high_ref, w_conv_ref, w_up_ref,
    feat_ref, blank_ref, out_ref, held, total, twice, index, in_sem, out_sem,
):
    gsx, gsy, gsz, chan = total.shape
    cols_x, cols_y, zcap = feat_ref.shape[:3]
    slots = cols_x * cols_y * zcap

    def at(slot):
        return place(slot, cols_y, zcap)

    def load(spot):
        return pltpu.make_async_copy(feat_ref.at[at(index[spot])], held.at[spot], in_sem.at[spot])

    def store(spot):
        return pltpu.make_async_copy(held.at[spot], out_ref.at[at(index[spot])], out_sem.at[spot])

    def scan(slot, count):
        alive = owner_ref[at(slot)] >= 0

        @pl.when(alive)
        def _():
            index[count] = slot
            load(count).start()

        return count + alive.astype(jnp.int32)

    count = lax.fori_loop(0, slots, scan, 0)
    groups = (count + GROUP - 1) // GROUP

    half = gsx // 2
    total[:half] = near_ref[...].astype(jnp.float32)
    total[half:] = far_ref[...].astype(jnp.float32)
    for line, ref, e in ((0, y_low_ref, 0), (gsy - 1, y_high_ref, 2)):
        pieces = [(d, e, ref[d : d + gsx]) for d in range(3)]
        total[:, line] = total[:, line] + conv_lines(pieces, w_conv_ref)
    for plane, ref, d in ((0, x_low_ref, 0), (gsx - 1, x_high_ref, 2)):
        pieces = [(d, e, moved_lines(ref[...], e)) for e in range(3)]
        total[plane] = total[plane] + conv_lines(pieces, w_conv_ref)
    for x in range(gsx):
        for c in range(2):
            twice[x, :, pl.ds(c, gsz, stride=2)] = total[x]

    @pl.loop(0, groups)
    def _(group):
        for b in range(GROUP):
            @pl.when(group * GROUP + b < count)
            def _():
                load(group * GROUP + b).wait()

        cells = []
        for b in range(GROUP):
            x, y, z = at(index[jnp.minimum(group * GROUP + b, count - 1)])
            where = (pl.ds(4 * x, 4), pl.ds(4 * y, 4), pl.ds(pl.multiple_of(8 * z, 8), 8))
            cells.append(twice[where].reshape(128, chan))
        cells = jnp.concatenate(cells, axis=0)
        odd = lax.rem(lax.broadcasted_iota(jnp.int32, cells.shape, 0), 2) == 1
        split = jnp.concatenate(
            [jnp.where(odd, 0.0, cells), jnp.where(odd, cells, 0.0)], axis=1
        ).astype(jnp.bfloat16)
        weights = jnp.concatenate(
            [
                jnp.concatenate(
                    [w_up_ref[4 * a + 2 * b + c] for a in range(2) for b in range(2)], axis=1
                )
                for c in range(2)
            ],
            axis=0,
        )
        lifted = jnp.dot(split, weights, preferred_element_type=jnp.float32)
        for b in range(GROUP):
            top = lifted[128 * b : 128 * b + 128].reshape(16, 8, 4 * chan)
            spot = group * GROUP + b
            for a in range(2):
                pair = [top[:, :, (2 * a + e) * chan : (2 * a + e + 1) * chan] for e in range(2)]
                pair = jnp.concatenate(pair, axis=1).reshape(4, 64, chan)
                held[spot, :, a] = (held[spot, :, a].astype(jnp.float32) + pair).astype(jnp.bfloat16)
        for b in range(GROUP):
            @pl.when(group * GROUP + b < count)
            def _():
                store(group * GROUP + b).start()

    @pl.loop(0, count)
    def _(spot):
        store(spot).wait()


def exchange(low, high, axis):
    count = lax.axis_size(axis)
    up = [(i, i + 1) for i in range(count - 1)]
    return lax.ppermute(high, axis, up), lax.ppermute(low, axis, [(j, i) for i, j in up])


def local(features, owner, norm_gain, time_shift, w_in, w_out, w_down, w_conv, w_up):
    cols_x, cols_y, zcap, voxels, chan = features.shape
    slots = cols_x * cols_y * zcap
    gsx, gsy, gsz = cols_x * 4, cols_y * 4, zcap * 4
    layers, _, hid = w_in.shape
    vmem = pl.BlockSpec(memory_space=pltpu.VMEM)
    smem = pl.BlockSpec(memory_space=pltpu.SMEM)
    params = pltpu.CompilerParams(vmem_limit_bytes=VMEM_LIMIT)

    def cells(*shape):
        return jax.ShapeDtypeStruct(shape + (gsz, chan), jnp.bfloat16)

    brick = (4, 2, voxels // 8, chan)
    hbm = pl.BlockSpec(memory_space=pl.ANY)
    blank = jax.ShapeDtypeStruct((cols_x, cols_y, zcap) + brick, jnp.bfloat16)
    grid, x_low, x_high, y_low, y_high, blank = pl.pallas_call(
        down_kernel,
        out_shape=[cells(gsx, gsy), cells(gsy), cells(gsy), cells(gsx), cells(gsx), blank],
        in_specs=[smem, hbm, vmem, vmem, hbm, hbm, vmem],
        out_specs=[vmem] * 5 + [hbm],
        scratch_shapes=[
            pltpu.VMEM((2, GROUP, voxels, chan), jnp.bfloat16),
            pltpu.VMEM((GROUP, voxels, chan), jnp.float32),
            pltpu.VMEM((GROUP, voxels, chan), jnp.float32),
            pltpu.VMEM((layers, chan, hid), jnp.bfloat16),
            pltpu.VMEM((layers, hid, chan), jnp.bfloat16),
            pltpu.VMEM((gsx, gsy, gsz, chan), jnp.float32),
            pltpu.VMEM(brick, jnp.bfloat16),
            pltpu.SMEM((slots,), jnp.int32),
            pltpu.SemaphoreType.DMA((2, GROUP)),
            pltpu.SemaphoreType.DMA((2,)),
            pltpu.SemaphoreType.DMA((slots,)),
        ],
        compiler_params=params,
        name="voxel_ff_down",
    )(owner, features, norm_gain, time_shift, w_in, w_out, w_down.reshape(8, chan, chan))

    taps = w_conv.reshape(27, chan, chan)
    half = gsx // 2
    flops = 2 * 27 * half * gsy * gsz * chan * chan
    own = [
        pl.pallas_call(
            functools.partial(own_kernel, first),
            out_shape=cells(half, gsy),
            in_specs=[vmem, vmem],
            out_specs=vmem,
            compiler_params=params,
            cost_estimate=pl.CostEstimate(
                flops=4 * flops, bytes_accessed=4 * 1024 * 1024, transcendentals=0
            ),
            name="conv_own",
        )(grid, taps)
        for first in (0, half)
    ]
    x_low, x_high = exchange(x_low, x_high, "gx")
    y_low = jnp.concatenate([x_low[:1], y_low, x_high[:1]], axis=0)
    y_high = jnp.concatenate([x_low[-1:], y_high, x_high[-1:]], axis=0)
    y_low, y_high = exchange(y_low, y_high, "gy")

    result = pl.pallas_call(
        up_kernel,
        out_shape=jax.ShapeDtypeStruct(blank.shape, blank.dtype),
        in_specs=[smem] + [vmem] * 8 + [hbm, hbm],
        out_specs=hbm,
        input_output_aliases={10: 0},
        scratch_shapes=[
            pltpu.VMEM((MOST,) + brick, jnp.bfloat16),
            pltpu.VMEM((gsx, gsy, gsz, chan), jnp.float32),
            pltpu.VMEM((gsx, gsy, 2 * gsz, chan), jnp.float32),
            pltpu.SMEM((slots,), jnp.int32),
            pltpu.SemaphoreType.DMA((MOST,)),
            pltpu.SemaphoreType.DMA((MOST,)),
        ],
        compiler_params=params,
        name="rim_up",
    )(
        owner, *own, x_low, x_high, y_low, y_high, taps, w_up.reshape(8, chan, chan),
        features.reshape(blank.shape), blank,
    )
    return result.reshape(features.shape)


def solution(mesh):
    in_specs = (
        P("gx", "gy", None, None, None),
        P("gx", "gy", None),
        P(),
        P(),
        P(),
        P(),
        P(),
        P(),
        P(),
    )
    out_specs = P("gx", "gy", None, None, None)
    return jax.shard_map(local, mesh=mesh, in_specs=in_specs, out_specs=out_specs, check_vma=False)
```

```python
import functools

import jax
import jax.numpy as jnp
from jax import lax
from jax.experimental import pallas as pl
from jax.experimental.pallas import tpu as pltpu
from jax.sharding import PartitionSpec as P

GROUP = 8
LIFT = 4
MOST = 32
BLANKS = 4
MIB = 1024 * 1024


def silu(value):
    half = 0.5 * value
    return half + half * jnp.tanh(half)


def place(slot, cols_y, zcap):
    return slot // (zcap * cols_y), lax.rem(slot // zcap, cols_y), lax.rem(slot, zcap)


def down_kernel(
    owner_ref, feat_ref, gain_ref, shift_ref, w_in_ref, w_out_ref, w_down_ref,
    out_ref, x_low_ref, x_high_ref, y_low_ref, y_high_ref, index, blank_ref,
    held, stream, made, w_in, w_out, volume, zeros, sem, w_sem, zero_sem,
):
    cols_x, cols_y, zcap, voxels, chan = feat_ref.shape
    slots = cols_x * cols_y * zcap
    layers = w_in.shape[0]
    loads = [
        pltpu.make_async_copy(w_in_ref, w_in, w_sem.at[0]),
        pltpu.make_async_copy(w_out_ref, w_out, w_sem.at[1]),
    ]
    for load in loads:
        load.start()

    def at(slot):
        return place(slot, cols_y, zcap)

    def scan(slot, count):
        index[count] = slot
        return count + (owner_ref[at(slot)] >= 0).astype(jnp.int32)

    count = lax.fori_loop(0, slots, scan, 0, unroll=8)
    index[slots] = count
    groups = (count + GROUP - 1) // GROUP

    def slot_of(group, b):
        return index[jnp.minimum(group * GROUP + b, count - 1)]

    def copies(group):
        side = lax.rem(group, 2)
        return [
            pltpu.make_async_copy(
                feat_ref.at[at(slot_of(group, b))], held.at[side, b], sem.at[side, b]
            )
            for b in range(GROUP)
        ]

    @pl.when(groups > 0)
    def _():
        for copy in copies(0):
            copy.start()

    zeros[...] = jnp.zeros_like(zeros)
    parts = zcap // BLANKS
    blanks = [
        pltpu.make_async_copy(
            zeros,
            blank_ref.at[
                part // (parts * cols_y), part // parts % cols_y, pl.ds(part % parts * BLANKS, BLANKS)
            ],
            zero_sem.at[part],
        )
        for part in range(slots // BLANKS)
    ]
    for copy in blanks:
        copy.start()
    volume[...] = jnp.zeros_like(volume)
    across = lax.broadcasted_iota(jnp.int32, (chan, chan), 1)
    below = lax.broadcasted_iota(jnp.int32, (chan, chan), 0)
    loads[0].wait()
    for layer in range(layers):
        gain = jnp.where(across == below, gain_ref[layer : layer + 1], 0.0)
        gain = jnp.sum(gain, axis=1, keepdims=True) * (0.5 * chan**0.5)
        w_in[layer] = (w_in[layer].astype(jnp.float32) * gain).astype(jnp.bfloat16)
    loads[1].wait()

    def down(group, b):
        slot = slot_of(group, b)
        weights = jnp.concatenate(
            [
                jnp.concatenate([w_down_ref[4 * a + c], w_down_ref[4 * a + 2 + c]], axis=1)
                for a in range(2)
                for c in range(2)
            ],
            axis=0,
        )
        taps = []
        for c in range(2):
            rows = made[b, pl.ds(c, voxels // 2, stride=2)]
            taps.append(rows.astype(jnp.bfloat16).reshape(4, 2, 32, chan))
        cells = jnp.concatenate(
            [taps[c][:, a].reshape(128, chan) for a in range(2) for c in range(2)], axis=1
        )
        both = jnp.dot(cells, weights, preferred_element_type=jnp.float32)
        both = both.reshape(16, 8, 2 * chan)
        row = lax.broadcasted_iota(jnp.int32, (16, 8, chan), 1)
        part = jnp.where(row < 4, both[:, :, :chan], both[:, :, chan:])
        coarse = silu(part + pltpu.roll(part, 4, axis=1)).reshape(4, 4, 8, chan)
        x, y, z = at(slot)
        where = (
            pl.ds(4 * x, 4),
            pl.ds(4 * y, 4),
            pl.ds(pl.multiple_of(8 * (z // 2), 8), 8),
        )
        row = lax.broadcasted_iota(jnp.int32, coarse.shape, 2)
        mine = (row // 4) == lax.rem(z, 2)
        volume[where] = jnp.where(mine, coarse, volume[where])

    def work(group, carry):
        @pl.when(group + 1 < groups)
        def _():
            for copy in copies(group + 1):
                copy.start()

        for copy in copies(group):
            copy.wait()
        side = lax.rem(group, 2)

        def value(layer, b):
            return held[side, b].astype(jnp.float32) if layer == 0 else stream[b]

        def enter(layer, b):
            x = value(layer, b)
            power = jnp.sum(x * x, axis=-1, keepdims=True)
            normed = (x * lax.rsqrt(power + chan * 1e-6)).astype(jnp.bfloat16)
            raw = jnp.dot(normed, w_in[layer], preferred_element_type=jnp.float32)
            shift = (0.5 * shift_ref[layer : layer + 1]).astype(jnp.bfloat16)
            return raw.astype(jnp.bfloat16) + shift

        def leave(layer, b, half):
            hidden = half + half * jnp.tanh(half)
            result = value(layer, b) + jnp.dot(
                hidden, w_out[layer], preferred_element_type=jnp.float32
            )
            if layer + 1 < layers:
                stream[b] = result
            else:
                made[b] = result

        order = [(layer, b) for layer in range(layers) for b in range(GROUP)]
        half = enter(*order[0])
        for spot, here in enumerate(order):
            later = enter(*order[spot + 1]) if spot + 1 < len(order) else None
            leave(*here, half)
            if here[0] == 1:
                down(jnp.maximum(group - 1, 0), here[1])
            half = later
        return carry

    lax.fori_loop(0, groups, work, 0)

    @pl.when(groups > 0)
    def _():
        for b in range(GROUP):
            down(groups - 1, b)

    out_ref[...] = volume[...].astype(jnp.bfloat16)
    x_low_ref[...] = out_ref[0]
    x_high_ref[...] = out_ref[out_ref.shape[0] - 1]
    y_low_ref[...] = out_ref[:, 0]
    y_high_ref[...] = out_ref[:, out_ref.shape[1] - 1]

    for copy in blanks:
        copy.wait()


def shifted(sums, chan):
    z = lax.broadcasted_iota(jnp.int32, sums.shape[:2] + (chan,), 1)
    length = sums.shape[1]
    below = jnp.where(z == 0, 0.0, pltpu.roll(sums[:, :, :chan], 1, axis=1))
    above = jnp.where(z == length - 1, 0.0, pltpu.roll(sums[:, :, 2 * chan :], length - 1, axis=1))
    return sums[:, :, chan : 2 * chan] + below + above


def conv_lines(pieces, w_conv_ref):
    lines, gsz, chan = pieces[0][2].shape
    near = jnp.concatenate([piece.reshape(lines * gsz, chan) for _, _, piece in pieces], axis=1)
    taps = jnp.concatenate(
        [
            jnp.concatenate([w_conv_ref[9 * d + 3 * e + f] for f in range(3)], axis=1)
            for d, e, _ in pieces
        ],
        axis=0,
    )
    sums = jnp.dot(near, taps, preferred_element_type=jnp.float32)
    return shifted(sums.reshape(lines, gsz, 3 * chan), chan)


def moved_lines(lines, e):
    blank = jnp.zeros((1,) + lines.shape[1:], lines.dtype)
    if e == 0:
        return jnp.concatenate([blank, lines[:-1]], axis=0)
    if e == 2:
        return jnp.concatenate([lines[1:], blank], axis=0)
    return lines


def own_kernel(wanted, cells_ref, *refs):
    rims, (w_conv_ref, out_ref) = refs[:-2], refs[-2:]
    gsx = cells_ref.shape[0]
    for spot, x in enumerate(wanted):
        planes = [(d, x + d - 1, cells_ref) for d in range(3)]
        if rims:
            low_ref, high_ref = rims
            planes = [
                (d, i, low_ref if i < 0 else high_ref if i == gsx else ref) for d, i, ref in planes
            ]
        pieces = []
        for d, i, ref in planes:
            lines = ref[i] if 0 <= i < gsx else ref[...]
            pieces += [(d, e, moved_lines(lines, e)) for e in range(3)]
        total = cells_ref[x].astype(jnp.float32) + conv_lines(pieces, w_conv_ref)
        out_ref[spot] = total.astype(jnp.bfloat16)


def up_kernel(
    index, inner_ref, outer_ref, y_low_ref, y_high_ref, w_conv_ref, w_up_ref,
    feat_ref, blank_ref, out_ref, held, total, twice, in_sem, out_sem,
):
    gsx, gsy, gsz, chan = total.shape
    cols_x, cols_y, zcap = feat_ref.shape[:3]
    count = index[cols_x * cols_y * zcap]

    def at(slot):
        return place(slot, cols_y, zcap)

    def load(spot):
        return pltpu.make_async_copy(feat_ref.at[at(index[spot])], held.at[spot], in_sem.at[spot])

    def store(spot):
        return pltpu.make_async_copy(held.at[spot], out_ref.at[at(index[spot])], out_sem.at[spot])

    @pl.loop(0, count)
    def _(spot):
        load(spot).start()

    groups = (count + LIFT - 1) // LIFT

    inner, outer = split_planes(gsx)
    for wanted, ref in ((inner, inner_ref), (outer, outer_ref)):
        for spot, x in enumerate(wanted):
            total[x] = ref[spot].astype(jnp.float32)
    for line, ref, e in ((0, y_low_ref, 0), (gsy - 1, y_high_ref, 2)):
        pieces = [(d, e, ref[d : d + gsx]) for d in range(3)]
        total[:, line] = total[:, line] + conv_lines(pieces, w_conv_ref)
    for x in range(gsx):
        for c in range(2):
            twice[x, :, pl.ds(c, gsz, stride=2)] = total[x]

    @pl.loop(0, groups)
    def _(group):
        for b in range(LIFT):
            @pl.when(group * LIFT + b < count)
            def _():
                load(group * LIFT + b).wait()

        cells = []
        for b in range(LIFT):
            x, y, z = at(index[jnp.minimum(group * LIFT + b, count - 1)])
            where = (pl.ds(4 * x, 4), pl.ds(4 * y, 4), pl.ds(pl.multiple_of(8 * z, 8), 8))
            cells.append(twice[where].reshape(128, chan))
        cells = jnp.concatenate(cells, axis=0)
        odd = lax.rem(lax.broadcasted_iota(jnp.int32, cells.shape, 0), 2) == 1
        split = jnp.concatenate(
            [jnp.where(odd, 0.0, cells), jnp.where(odd, cells, 0.0)], axis=1
        ).astype(jnp.bfloat16)
        weights = jnp.concatenate(
            [
                jnp.concatenate(
                    [w_up_ref[4 * a + 2 * b + c] for a in range(2) for b in range(2)], axis=1
                )
                for c in range(2)
            ],
            axis=0,
        )
        lifted = jnp.dot(split, weights, preferred_element_type=jnp.float32)
        for b in range(LIFT):
            top = lifted[128 * b : 128 * b + 128].reshape(16, 8, 4 * chan)
            spot = group * LIFT + b
            for a in range(2):
                pair = [top[:, :, (2 * a + e) * chan : (2 * a + e + 1) * chan] for e in range(2)]
                pair = jnp.concatenate(pair, axis=1).reshape(4, 64, chan)
                held[spot, :, a] = (held[spot, :, a].astype(jnp.float32) + pair).astype(jnp.bfloat16)
        for b in range(LIFT):
            @pl.when(group * LIFT + b < count)
            def _():
                store(group * LIFT + b).start()

    @pl.loop(0, count)
    def _(spot):
        store(spot).wait()


def split_planes(gsx):
    inner = range(gsx // 4, gsx - gsx // 4)
    return inner, [x for x in range(gsx) if x not in inner]


def exchange(low, high, axis):
    count = lax.axis_size(axis)
    up = [(i, i + 1) for i in range(count - 1)]
    return lax.ppermute(high, axis, up), lax.ppermute(low, axis, [(j, i) for i, j in up])


def local(features, owner, norm_gain, time_shift, w_in, w_out, w_down, w_conv, w_up):
    cols_x, cols_y, zcap, voxels, chan = features.shape
    slots = cols_x * cols_y * zcap
    gsx, gsy, gsz = cols_x * 4, cols_y * 4, zcap * 4
    layers, _, hid = w_in.shape
    vmem = pl.BlockSpec(memory_space=pltpu.VMEM)
    smem = pl.BlockSpec(memory_space=pltpu.SMEM)
    hbm = pl.BlockSpec(memory_space=pl.ANY)

    def limit(mib):
        return pltpu.CompilerParams(vmem_limit_bytes=mib * MIB)

    def cells(*shape):
        return jax.ShapeDtypeStruct(shape + (gsz, chan), jnp.bfloat16)

    brick = (4, 2, voxels // 8, chan)
    blank = jax.ShapeDtypeStruct((cols_x, cols_y, zcap) + brick, jnp.bfloat16)
    grid, x_low, x_high, y_low, y_high, index, blank = pl.pallas_call(
        down_kernel,
        out_shape=[
            cells(gsx, gsy), cells(gsy), cells(gsy), cells(gsx), cells(gsx),
            jax.ShapeDtypeStruct((slots + 1,), jnp.int32), blank,
        ],
        in_specs=[smem, hbm, vmem, vmem, hbm, hbm, vmem],
        out_specs=[vmem] * 5 + [smem, hbm],
        scratch_shapes=[
            pltpu.VMEM((2, GROUP, voxels, chan), jnp.bfloat16),
            pltpu.VMEM((GROUP, voxels, chan), jnp.float32),
            pltpu.VMEM((GROUP, voxels, chan), jnp.float32),
            pltpu.VMEM((layers, chan, hid), jnp.bfloat16),
            pltpu.VMEM((layers, hid, chan), jnp.bfloat16),
            pltpu.VMEM((gsx, gsy, gsz, chan), jnp.float32),
            pltpu.VMEM((BLANKS,) + brick, jnp.bfloat16),
            pltpu.SemaphoreType.DMA((2, GROUP)),
            pltpu.SemaphoreType.DMA((2,)),
            pltpu.SemaphoreType.DMA((slots // BLANKS,)),
        ],
        compiler_params=limit(52),
        name="voxel_ff_down",
    )(owner, features, norm_gain, time_shift, w_in, w_out, w_down.reshape(8, chan, chan))

    taps = w_conv.reshape(27, chan, chan)
    flops = 2 * 27 * gsx // 2 * gsy * gsz * chan * chan

    def own(wanted, *operands):
        return pl.pallas_call(
            functools.partial(own_kernel, wanted),
            out_shape=cells(len(wanted), gsy),
            in_specs=[vmem] * len(operands),
            out_specs=vmem,
            compiler_params=limit(20),
            cost_estimate=pl.CostEstimate(
                flops=4 * flops, bytes_accessed=4 * MIB, transcendentals=0
            ),
            name="conv_own",
        )(*operands)

    inner, outer = split_planes(gsx)
    inner = own(inner, grid, taps)
    x_low, x_high = exchange(x_low, x_high, "gx")
    outer = own(outer, grid, x_low, x_high, taps)
    y_low = jnp.concatenate([x_low[:1], y_low, x_high[:1]], axis=0)
    y_high = jnp.concatenate([x_low[-1:], y_high, x_high[-1:]], axis=0)
    y_low, y_high = exchange(y_low, y_high, "gy")

    result = pl.pallas_call(
        up_kernel,
        out_shape=jax.ShapeDtypeStruct(blank.shape, blank.dtype),
        in_specs=[smem] + [vmem] * 6 + [hbm, hbm],
        out_specs=hbm,
        input_output_aliases={8: 0},
        scratch_shapes=[
            pltpu.VMEM((MOST,) + brick, jnp.bfloat16),
            pltpu.VMEM((gsx, gsy, gsz, chan), jnp.float32),
            pltpu.VMEM((gsx, gsy, 2 * gsz, chan), jnp.float32),
            pltpu.SemaphoreType.DMA((MOST,)),
            pltpu.SemaphoreType.DMA((MOST,)),
        ],
        compiler_params=limit(32),
        name="rim_up",
    )(
        index, inner, outer, y_low, y_high, taps, w_up.reshape(8, chan, chan),
        features.reshape(blank.shape), blank,
    )
    return result.reshape(features.shape)


def solution(mesh):
    in_specs = (
        P("gx", "gy", None, None, None),
        P("gx", "gy", None),
        P(),
        P(),
        P(),
        P(),
        P(),
        P(),
        P(),
    )
    out_specs = P("gx", "gy", None, None, None)
    return jax.shard_map(local, mesh=mesh, in_specs=in_specs, out_specs=out_specs, check_vma=False)
```

```python
import functools

import jax
import jax.numpy as jnp
from jax import lax
from jax.experimental import pallas as pl
from jax.experimental.pallas import tpu as pltpu
from jax.sharding import PartitionSpec as P

GROUP = 8
LIFT = 4
MOST = 32
BLANKS = 4
MIB = 1024 * 1024


def silu(value):
    half = 0.5 * value
    return half + half * jnp.tanh(half)


def place(slot, cols_y, zcap):
    return slot // (zcap * cols_y), lax.rem(slot // zcap, cols_y), lax.rem(slot, zcap)


def down_kernel(
    owner_hbm, feat_ref, gain_hbm, shift_hbm, w_in_hbm, w_out_hbm, w_down_hbm,
    out_ref, x_low_ref, x_high_ref, y_low_ref, y_high_ref, index, blank_ref,
    held, owner_ref, gain_ref, shift_ref, w_in, w_out, w_down_ref, stream, made, volume, zeros,
    sem, arg_sem, zero_sem,
):
    cols_x, cols_y, zcap, voxels, chan = feat_ref.shape
    slots = cols_x * cols_y * zcap
    layers = w_in.shape[0]
    pairs = (
        (owner_hbm, owner_ref),
        (gain_hbm, gain_ref),
        (shift_hbm, shift_ref),
        (w_in_hbm, w_in),
        (w_out_hbm, w_out),
        (w_down_hbm, w_down_ref),
    )
    loads = [
        pltpu.make_async_copy(source, target, arg_sem.at[i])
        for i, (source, target) in enumerate(pairs)
    ]
    for load in loads:
        load.start()
    volume[...] = jnp.zeros_like(volume)
    zeros[...] = jnp.zeros_like(zeros)
    loads[0].wait()

    def at(slot):
        return place(slot, cols_y, zcap)

    def scan(slot, count):
        index[count] = slot
        return count + (owner_ref[at(slot)] >= 0).astype(jnp.int32)

    count = lax.fori_loop(0, slots, scan, 0, unroll=8)
    index[slots] = count
    groups = (count + GROUP - 1) // GROUP

    def slot_of(group, b):
        return index[jnp.minimum(group * GROUP + b, count - 1)]

    def copies(group):
        return [
            pltpu.make_async_copy(
                feat_ref.at[at(slot_of(group, b))], held.at[group * GROUP + b], sem.at[group * GROUP + b]
            )
            for b in range(GROUP)
        ]

    @pl.when(groups > 0)
    def _():
        for copy in copies(0):
            copy.start()

    parts = zcap // BLANKS
    blanks = [
        pltpu.make_async_copy(
            zeros,
            blank_ref.at[
                part // (parts * cols_y), part // parts % cols_y, pl.ds(part % parts * BLANKS, BLANKS)
            ],
            zero_sem.at[part],
        )
        for part in range(slots // BLANKS)
    ]
    for copy in blanks:
        copy.start()
    across = lax.broadcasted_iota(jnp.int32, (chan, chan), 1)
    below = lax.broadcasted_iota(jnp.int32, (chan, chan), 0)
    for load in loads[1:]:
        load.wait()
    for layer in range(layers):
        gain = jnp.where(across == below, gain_ref[layer : layer + 1], 0.0)
        gain = jnp.sum(gain, axis=1, keepdims=True) * (0.5 * chan**0.5)
        w_in[layer] = (w_in[layer].astype(jnp.float32) * gain).astype(jnp.bfloat16)

    def down(group, b):
        slot = slot_of(group, b)
        weights = jnp.concatenate(
            [
                jnp.concatenate([w_down_ref[4 * a + c], w_down_ref[4 * a + 2 + c]], axis=1)
                for a in range(2)
                for c in range(2)
            ],
            axis=0,
        )
        taps = []
        for c in range(2):
            rows = made[b, pl.ds(c, voxels // 2, stride=2)]
            taps.append(rows.astype(jnp.bfloat16).reshape(4, 2, 32, chan))
        cells = jnp.concatenate(
            [taps[c][:, a].reshape(128, chan) for a in range(2) for c in range(2)], axis=1
        )
        both = jnp.dot(cells, weights, preferred_element_type=jnp.float32)
        both = both.reshape(16, 8, 2 * chan)
        row = lax.broadcasted_iota(jnp.int32, (16, 8, chan), 1)
        part = jnp.where(row < 4, both[:, :, :chan], both[:, :, chan:])
        coarse = silu(part + pltpu.roll(part, 4, axis=1)).reshape(4, 4, 8, chan)
        x, y, z = at(slot)
        where = (
            pl.ds(4 * x, 4),
            pl.ds(4 * y, 4),
            pl.ds(pl.multiple_of(8 * (z // 2), 8), 8),
        )
        row = lax.broadcasted_iota(jnp.int32, coarse.shape, 2)
        mine = (row // 4) == lax.rem(z, 2)
        volume[where] = jnp.where(mine, coarse, volume[where])

    def work(group, carry):
        @pl.when(group + 1 < groups)
        def _():
            for copy in copies(group + 1):
                copy.start()

        for copy in copies(group):
            copy.wait()

        def value(layer, b):
            return held[group * GROUP + b].astype(jnp.float32) if layer == 0 else stream[b]

        def enter(layer, b):
            x = value(layer, b)
            power = jnp.sum(x * x, axis=-1, keepdims=True)
            normed = (x * lax.rsqrt(power + chan * 1e-6)).astype(jnp.bfloat16)
            raw = jnp.dot(normed, w_in[layer], preferred_element_type=jnp.float32)
            shift = (0.5 * shift_ref[layer : layer + 1]).astype(jnp.bfloat16)
            return raw.astype(jnp.bfloat16) + shift

        def leave(layer, b, half):
            hidden = half + half * jnp.tanh(half)
            result = value(layer, b) + jnp.dot(
                hidden, w_out[layer], preferred_element_type=jnp.float32
            )
            if layer + 1 < layers:
                stream[b] = result
            else:
                made[b] = result

        order = [(layer, b) for layer in range(layers) for b in range(GROUP)]
        half = enter(*order[0])
        for spot, here in enumerate(order):
            later = enter(*order[spot + 1]) if spot + 1 < len(order) else None
            leave(*here, half)
            if here[0] == 1:
                down(jnp.maximum(group - 1, 0), here[1])
            half = later
        return carry

    lax.fori_loop(0, groups, work, 0)

    @pl.when(groups > 0)
    def _():
        for b in range(GROUP):
            down(groups - 1, b)

    out_ref[...] = volume[...].astype(jnp.bfloat16)
    x_low_ref[...] = out_ref[0]
    x_high_ref[...] = out_ref[out_ref.shape[0] - 1]
    y_low_ref[...] = out_ref[:, 0]
    y_high_ref[...] = out_ref[:, out_ref.shape[1] - 1]

    for copy in blanks:
        copy.wait()


def shifted(sums, chan):
    z = lax.broadcasted_iota(jnp.int32, sums.shape[:2] + (chan,), 1)
    length = sums.shape[1]
    below = jnp.where(z == 0, 0.0, pltpu.roll(sums[:, :, :chan], 1, axis=1))
    above = jnp.where(z == length - 1, 0.0, pltpu.roll(sums[:, :, 2 * chan :], length - 1, axis=1))
    return sums[:, :, chan : 2 * chan] + below + above


def conv_lines(pieces, w_conv_ref):
    lines, gsz, chan = pieces[0][2].shape
    near = jnp.concatenate([piece.reshape(lines * gsz, chan) for _, _, piece in pieces], axis=1)
    taps = jnp.concatenate(
        [
            jnp.concatenate([w_conv_ref[9 * d + 3 * e + f] for f in range(3)], axis=1)
            for d, e, _ in pieces
        ],
        axis=0,
    )
    sums = jnp.dot(near, taps, preferred_element_type=jnp.float32)
    return shifted(sums.reshape(lines, gsz, 3 * chan), chan)


def moved_lines(lines, e):
    blank = jnp.zeros((1,) + lines.shape[1:], lines.dtype)
    if e == 0:
        return jnp.concatenate([blank, lines[:-1]], axis=0)
    if e == 2:
        return jnp.concatenate([lines[1:], blank], axis=0)
    return lines


def own_kernel(wanted, cells_ref, *refs):
    rims, (w_conv_ref, out_ref) = refs[:-2], refs[-2:]
    gsx = cells_ref.shape[0]
    for spot, x in enumerate(wanted):
        planes = [(d, x + d - 1, cells_ref) for d in range(3)]
        if rims:
            low_ref, high_ref = rims
            planes = [
                (d, i, low_ref if i < 0 else high_ref if i == gsx else ref) for d, i, ref in planes
            ]
        pieces = []
        for d, i, ref in planes:
            lines = ref[i] if 0 <= i < gsx else ref[...]
            pieces += [(d, e, moved_lines(lines, e)) for e in range(3)]
        total = cells_ref[x].astype(jnp.float32) + conv_lines(pieces, w_conv_ref)
        out_ref[spot] = total.astype(jnp.bfloat16)


def up_kernel(
    index, inner_ref, outer_ref, y_low_ref, y_high_ref, w_conv_ref, w_up_ref, feat_ref, blank_ref,
    out_ref, held, total, twice, in_sem, out_sem,
):
    gsx, gsy, gsz, chan = total.shape
    cols_x, cols_y, zcap = out_ref.shape[:3]
    count = index[cols_x * cols_y * zcap]

    def at(slot):
        return place(slot, cols_y, zcap)

    def load(spot):
        return pltpu.make_async_copy(feat_ref.at[at(index[spot])], held.at[spot], in_sem.at[spot])

    def store(spot):
        return pltpu.make_async_copy(held.at[spot], out_ref.at[at(index[spot])], out_sem.at[spot])

    @pl.loop(0, count)
    def _(spot):
        load(spot).start()

    groups = (count + LIFT - 1) // LIFT

    inner, outer = split_planes(gsx)
    for wanted, ref in ((inner, inner_ref), (outer, outer_ref)):
        for spot, x in enumerate(wanted):
            total[x] = ref[spot].astype(jnp.float32)
    for line, ref, e in ((0, y_low_ref, 0), (gsy - 1, y_high_ref, 2)):
        pieces = [(d, e, ref[d : d + gsx]) for d in range(3)]
        total[:, line] = total[:, line] + conv_lines(pieces, w_conv_ref)
    for x in range(gsx):
        for c in range(2):
            twice[x, :, pl.ds(c, gsz, stride=2)] = total[x]

    @pl.loop(0, groups)
    def _(group):
        for b in range(LIFT):
            @pl.when(group * LIFT + b < count)
            def _():
                load(group * LIFT + b).wait()

        cells = []
        for b in range(LIFT):
            x, y, z = at(index[jnp.minimum(group * LIFT + b, count - 1)])
            where = (pl.ds(4 * x, 4), pl.ds(4 * y, 4), pl.ds(pl.multiple_of(8 * z, 8), 8))
            cells.append(twice[where].reshape(128, chan))
        cells = jnp.concatenate(cells, axis=0)
        odd = lax.rem(lax.broadcasted_iota(jnp.int32, cells.shape, 0), 2) == 1
        split = jnp.concatenate(
            [jnp.where(odd, 0.0, cells), jnp.where(odd, cells, 0.0)], axis=1
        ).astype(jnp.bfloat16)
        weights = jnp.concatenate(
            [
                jnp.concatenate(
                    [w_up_ref[4 * a + 2 * b + c] for a in range(2) for b in range(2)], axis=1
                )
                for c in range(2)
            ],
            axis=0,
        )
        lifted = jnp.dot(split, weights, preferred_element_type=jnp.float32)
        for b in range(LIFT):
            top = lifted[128 * b : 128 * b + 128].reshape(16, 8, 4 * chan)
            spot = group * LIFT + b
            for a in range(2):
                pair = [top[:, :, (2 * a + e) * chan : (2 * a + e + 1) * chan] for e in range(2)]
                pair = jnp.concatenate(pair, axis=1).reshape(4, 64, chan)
                held[spot, :, a] = (held[spot, :, a].astype(jnp.float32) + pair).astype(jnp.bfloat16)
        for b in range(LIFT):
            @pl.when(group * LIFT + b < count)
            def _():
                store(group * LIFT + b).start()

    @pl.loop(0, count)
    def _(spot):
        store(spot).wait()


def split_planes(gsx):
    inner = range(gsx // 4, gsx - gsx // 4)
    return inner, [x for x in range(gsx) if x not in inner]


def exchange(low, high, axis):
    count = lax.axis_size(axis)
    up = [(i, i + 1) for i in range(count - 1)]
    return lax.ppermute(high, axis, up), lax.ppermute(low, axis, [(j, i) for i, j in up])


def local(features, owner, norm_gain, time_shift, w_in, w_out, w_down, w_conv, w_up):
    cols_x, cols_y, zcap, voxels, chan = features.shape
    slots = cols_x * cols_y * zcap
    gsx, gsy, gsz = cols_x * 4, cols_y * 4, zcap * 4
    layers, _, hid = w_in.shape
    vmem = pl.BlockSpec(memory_space=pltpu.VMEM)
    smem = pl.BlockSpec(memory_space=pltpu.SMEM)
    hbm = pl.BlockSpec(memory_space=pltpu.HBM)

    def limit(mib):
        return pltpu.CompilerParams(vmem_limit_bytes=mib * MIB)

    def cells(*shape):
        return jax.ShapeDtypeStruct(shape + (gsz, chan), jnp.bfloat16)

    brick = (4, 2, voxels // 8, chan)
    blank = jax.ShapeDtypeStruct((cols_x, cols_y, zcap) + brick, jnp.bfloat16)
    grid, x_low, x_high, y_low, y_high, index, blank = pl.pallas_call(
        down_kernel,
        out_shape=[
            cells(gsx, gsy), cells(gsy), cells(gsy), cells(gsx), cells(gsx),
            jax.ShapeDtypeStruct((slots + 1,), jnp.int32),
            blank,
        ],
        in_specs=[hbm] * 7,
        out_specs=[vmem] * 5 + [smem, hbm],
        scratch_shapes=[
            pltpu.VMEM((MOST, voxels, chan), jnp.bfloat16),
            pltpu.SMEM(owner.shape, jnp.int32),
            pltpu.VMEM(norm_gain.shape, jnp.float32),
            pltpu.VMEM(time_shift.shape, jnp.float32),
            pltpu.VMEM((layers, chan, hid), jnp.bfloat16),
            pltpu.VMEM((layers, hid, chan), jnp.bfloat16),
            pltpu.VMEM((8, chan, chan), jnp.bfloat16),
            pltpu.VMEM((GROUP, voxels, chan), jnp.float32),
            pltpu.VMEM((GROUP, voxels, chan), jnp.float32),
            pltpu.VMEM((gsx, gsy, gsz, chan), jnp.float32),
            pltpu.VMEM((BLANKS,) + brick, jnp.bfloat16),
            pltpu.SemaphoreType.DMA((MOST,)),
            pltpu.SemaphoreType.DMA((7,)),
            pltpu.SemaphoreType.DMA((slots // BLANKS,)),
        ],
        compiler_params=limit(55),
        name="voxel_ff_down",
    )(owner, features, norm_gain, time_shift, w_in, w_out, w_down.reshape(8, chan, chan))

    taps = w_conv.reshape(27, chan, chan)
    flops = 2 * 27 * gsx // 2 * gsy * gsz * chan * chan

    def own(wanted, *operands):
        return pl.pallas_call(
            functools.partial(own_kernel, wanted),
            out_shape=cells(len(wanted), gsy),
            in_specs=[vmem] * len(operands),
            out_specs=vmem,
            compiler_params=limit(20),
            cost_estimate=pl.CostEstimate(
                flops=4 * flops, bytes_accessed=4 * MIB, transcendentals=0
            ),
            name="conv_own",
        )(*operands)

    inner, outer = split_planes(gsx)
    inner = own(inner, grid, taps)
    x_low, x_high = exchange(x_low, x_high, "gx")
    outer = own(outer, grid, x_low, x_high, taps)
    y_low = jnp.concatenate([x_low[:1], y_low, x_high[:1]], axis=0)
    y_high = jnp.concatenate([x_low[-1:], y_high, x_high[-1:]], axis=0)
    y_low, y_high = exchange(y_low, y_high, "gy")

    result = pl.pallas_call(
        up_kernel,
        out_shape=jax.ShapeDtypeStruct(blank.shape, blank.dtype),
        in_specs=[smem] + [vmem] * 6 + [hbm, hbm],
        out_specs=hbm,
        input_output_aliases={8: 0},
        scratch_shapes=[
            pltpu.VMEM((MOST,) + brick, jnp.bfloat16),
            pltpu.VMEM((gsx, gsy, gsz, chan), jnp.float32),
            pltpu.VMEM((gsx, gsy, 2 * gsz, chan), jnp.float32),
            pltpu.SemaphoreType.DMA((MOST,)),
            pltpu.SemaphoreType.DMA((MOST,)),
        ],
        compiler_params=limit(48),
        name="rim_up",
    )(
        index, inner, outer, y_low, y_high, taps, w_up.reshape(8, chan, chan),
        features.reshape(blank.shape), blank,
    )
    return result.reshape(features.shape)


def solution(mesh):
    in_specs = (
        P("gx", "gy", None, None, None),
        P("gx", "gy", None),
        P(),
        P(),
        P(),
        P(),
        P(),
        P(),
        P(),
    )
    out_specs = P("gx", "gy", None, None, None)
    return jax.shard_map(local, mesh=mesh, in_specs=in_specs, out_specs=out_specs, check_vma=False)
```

```python
import functools

import jax
import jax.numpy as jnp
from jax import lax
from jax.experimental import pallas as pl
from jax.experimental.pallas import tpu as pltpu
from jax.sharding import PartitionSpec as P

GROUP = 8
LIFT = 4
MOST = 32
BLANKS = 4
MIB = 1024 * 1024


def silu(value):
    half = 0.5 * value
    return half + half * jnp.tanh(half)


def place(slot, cols_y, zcap):
    return slot // (zcap * cols_y), lax.rem(slot // zcap, cols_y), lax.rem(slot, zcap)


def down_kernel(
    owner_hbm, feat_ref, gain_hbm, shift_hbm, w_in_hbm, w_out_hbm, w_down_hbm,
    out_ref, x_low_ref, x_high_ref, y_low_ref, y_high_ref, index, blank_ref,
    held, owner_ref, gain_ref, shift_ref, w_in_ref, w_out_ref, w_down_ref, w_in, w_out, shifts,
    stream, made, volume, zeros,
    sem, arg_sem, zero_sem,
):
    cols_x, cols_y, zcap, voxels, chan = feat_ref.shape
    slots = cols_x * cols_y * zcap
    layers = w_in_ref.shape[0]
    pairs = (
        (owner_hbm, owner_ref),
        (gain_hbm, gain_ref),
        (shift_hbm, shift_ref),
        (w_in_hbm, w_in_ref),
        (w_out_hbm, w_out_ref),
        (w_down_hbm, w_down_ref),
    )
    loads = [
        pltpu.make_async_copy(source, target, arg_sem.at[i])
        for i, (source, target) in enumerate(pairs)
    ]
    for load in loads:
        load.start()
    volume[...] = jnp.zeros_like(volume)
    zeros[...] = jnp.zeros_like(zeros)
    loads[0].wait()

    def at(slot):
        return place(slot, cols_y, zcap)

    def scan(slot, count):
        index[count] = slot
        return count + (owner_ref[at(slot)] >= 0).astype(jnp.int32)

    count = lax.fori_loop(0, slots, scan, 0, unroll=8)
    index[slots] = count
    groups = (count + GROUP - 1) // GROUP

    def slot_of(group, b):
        return index[jnp.minimum(group * GROUP + b, count - 1)]

    def copies(group):
        return [
            pltpu.make_async_copy(
                feat_ref.at[at(slot_of(group, b))], held.at[group * GROUP + b], sem.at[group * GROUP + b]
            )
            for b in range(GROUP)
        ]

    @pl.when(groups > 0)
    def _():
        for copy in copies(0):
            copy.start()

    parts = zcap // BLANKS
    blanks = [
        pltpu.make_async_copy(
            zeros,
            blank_ref.at[
                part // (parts * cols_y), part // parts % cols_y, pl.ds(part % parts * BLANKS, BLANKS)
            ],
            zero_sem.at[part],
        )
        for part in range(slots // BLANKS)
    ]
    for copy in blanks:
        copy.start()
    for load in loads[1:]:
        load.wait()
    for layer in range(layers):
        gain = gain_ref[layer : layer + 1] * (0.5 * chan**0.5)
        w_in[layer] = (w_in_ref[layer].astype(jnp.float32).T * gain).astype(jnp.bfloat16)
        w_out[layer] = w_out_ref[layer].astype(jnp.float32).T.astype(jnp.bfloat16)
        shift = jnp.broadcast_to(0.5 * shift_ref[layer : layer + 1], (chan, shift_ref.shape[1]))
        shifts[layer] = shift.T.astype(jnp.bfloat16)

    def down(group, b):
        slot = slot_of(group, b)
        weights = jnp.concatenate(
            [
                jnp.concatenate([w_down_ref[4 * a + c], w_down_ref[4 * a + 2 + c]], axis=1)
                for a in range(2)
                for c in range(2)
            ],
            axis=0,
        )
        taps = []
        for c in range(2):
            rows = made[b, pl.ds(c, voxels // 2, stride=2)]
            taps.append(rows.astype(jnp.bfloat16).reshape(4, 2, 32, chan))
        cells = jnp.concatenate(
            [taps[c][:, a].reshape(128, chan) for a in range(2) for c in range(2)], axis=1
        )
        both = jnp.dot(cells, weights, preferred_element_type=jnp.float32)
        both = both.reshape(16, 8, 2 * chan)
        row = lax.broadcasted_iota(jnp.int32, (16, 8, chan), 1)
        part = jnp.where(row < 4, both[:, :, :chan], both[:, :, chan:])
        coarse = silu(part + pltpu.roll(part, 4, axis=1)).reshape(4, 4, 8, chan)
        x, y, z = at(slot)
        where = (
            pl.ds(4 * x, 4),
            pl.ds(4 * y, 4),
            pl.ds(pl.multiple_of(8 * (z // 2), 8), 8),
        )
        row = lax.broadcasted_iota(jnp.int32, coarse.shape, 2)
        mine = (row // 4) == lax.rem(z, 2)
        volume[where] = jnp.where(mine, coarse, volume[where])

    def work(group, carry):
        @pl.when(group + 1 < groups)
        def _():
            for copy in copies(group + 1):
                copy.start()

        for copy in copies(group):
            copy.wait()

        def value(layer, b):
            return held[group * GROUP + b].astype(jnp.float32).T if layer == 0 else stream[b]

        def enter(layer, b):
            x = value(layer, b)
            power = jnp.sum(x * x, axis=0, keepdims=True)
            normed = (x * lax.rsqrt(power + chan * 1e-6)).astype(jnp.bfloat16)
            raw = jnp.dot(w_in[layer], normed, preferred_element_type=jnp.float32)
            shift = jnp.concatenate([shifts[layer]] * (voxels // chan), axis=1)
            return raw.astype(jnp.bfloat16) + shift

        def leave(layer, b, half):
            hidden = half + half * jnp.tanh(half)
            result = value(layer, b) + jnp.dot(
                w_out[layer], hidden, preferred_element_type=jnp.float32
            )
            if layer + 1 < layers:
                stream[b] = result
            else:
                made[b] = result.T

        order = [(layer, b) for layer in range(layers) for b in range(GROUP)]
        half = enter(*order[0])
        for spot, here in enumerate(order):
            later = enter(*order[spot + 1]) if spot + 1 < len(order) else None
            leave(*here, half)
            if here[0] == 1:
                down(jnp.maximum(group - 1, 0), here[1])
            half = later
        return carry

    lax.fori_loop(0, groups, work, 0)

    @pl.when(groups > 0)
    def _():
        for b in range(GROUP):
            down(groups - 1, b)

    out_ref[...] = volume[...].astype(jnp.bfloat16)
    x_low_ref[...] = out_ref[0]
    x_high_ref[...] = out_ref[out_ref.shape[0] - 1]
    y_low_ref[...] = out_ref[:, 0]
    y_high_ref[...] = out_ref[:, out_ref.shape[1] - 1]

    for copy in blanks:
        copy.wait()


def shifted(sums, chan):
    z = lax.broadcasted_iota(jnp.int32, sums.shape[:2] + (chan,), 1)
    length = sums.shape[1]
    below = jnp.where(z == 0, 0.0, pltpu.roll(sums[:, :, :chan], 1, axis=1))
    above = jnp.where(z == length - 1, 0.0, pltpu.roll(sums[:, :, 2 * chan :], length - 1, axis=1))
    return sums[:, :, chan : 2 * chan] + below + above


def conv_lines(pieces, w_conv_ref):
    lines, gsz, chan = pieces[0][2].shape
    near = jnp.concatenate([piece.reshape(lines * gsz, chan) for _, _, piece in pieces], axis=1)
    taps = jnp.concatenate(
        [
            jnp.concatenate([w_conv_ref[9 * d + 3 * e + f] for f in range(3)], axis=1)
            for d, e, _ in pieces
        ],
        axis=0,
    )
    sums = jnp.dot(near, taps, preferred_element_type=jnp.float32)
    return shifted(sums.reshape(lines, gsz, 3 * chan), chan)


def moved_lines(lines, e):
    blank = jnp.zeros((1,) + lines.shape[1:], lines.dtype)
    if e == 0:
        return jnp.concatenate([blank, lines[:-1]], axis=0)
    if e == 2:
        return jnp.concatenate([lines[1:], blank], axis=0)
    return lines


def own_kernel(wanted, cells_ref, *refs):
    rims, (w_conv_ref, out_ref) = refs[:-2], refs[-2:]
    gsx = cells_ref.shape[0]
    for spot, x in enumerate(wanted):
        planes = [(d, x + d - 1, cells_ref) for d in range(3)]
        if rims:
            low_ref, high_ref = rims
            planes = [
                (d, i, low_ref if i < 0 else high_ref if i == gsx else ref) for d, i, ref in planes
            ]
        pieces = []
        for d, i, ref in planes:
            lines = ref[i] if 0 <= i < gsx else ref[...]
            pieces += [(d, e, moved_lines(lines, e)) for e in range(3)]
        total = cells_ref[x].astype(jnp.float32) + conv_lines(pieces, w_conv_ref)
        out_ref[spot] = total.astype(jnp.bfloat16)


def up_kernel(
    index, inner_ref, outer_ref, y_low_ref, y_high_ref, w_conv_ref, w_up_ref, feat_ref, blank_ref,
    out_ref, held, total, twice, in_sem, out_sem,
):
    gsx, gsy, gsz, chan = total.shape
    cols_x, cols_y, zcap = out_ref.shape[:3]
    count = index[cols_x * cols_y * zcap]

    def at(slot):
        return place(slot, cols_y, zcap)

    def load(spot):
        return pltpu.make_async_copy(feat_ref.at[at(index[spot])], held.at[spot], in_sem.at[spot])

    def store(spot):
        return pltpu.make_async_copy(held.at[spot], out_ref.at[at(index[spot])], out_sem.at[spot])

    @pl.loop(0, count)
    def _(spot):
        load(spot).start()

    groups = (count + LIFT - 1) // LIFT

    inner, outer = split_planes(gsx)
    for wanted, ref in ((inner, inner_ref), (outer, outer_ref)):
        for spot, x in enumerate(wanted):
            total[x] = ref[spot].astype(jnp.float32)
    for line, ref, e in ((0, y_low_ref, 0), (gsy - 1, y_high_ref, 2)):
        pieces = [(d, e, ref[d : d + gsx]) for d in range(3)]
        total[:, line] = total[:, line] + conv_lines(pieces, w_conv_ref)
    for x in range(gsx):
        for c in range(2):
            twice[x, :, pl.ds(c, gsz, stride=2)] = total[x]

    @pl.loop(0, groups)
    def _(group):
        for b in range(LIFT):
            @pl.when(group * LIFT + b < count)
            def _():
                load(group * LIFT + b).wait()

        cells = []
        for b in range(LIFT):
            x, y, z = at(index[jnp.minimum(group * LIFT + b, count - 1)])
            where = (pl.ds(4 * x, 4), pl.ds(4 * y, 4), pl.ds(pl.multiple_of(8 * z, 8), 8))
            cells.append(twice[where].reshape(128, chan))
        cells = jnp.concatenate(cells, axis=0)
        odd = lax.rem(lax.broadcasted_iota(jnp.int32, cells.shape, 0), 2) == 1
        split = jnp.concatenate(
            [jnp.where(odd, 0.0, cells), jnp.where(odd, cells, 0.0)], axis=1
        ).astype(jnp.bfloat16)
        weights = jnp.concatenate(
            [
                jnp.concatenate(
                    [w_up_ref[4 * a + 2 * b + c] for a in range(2) for b in range(2)], axis=1
                )
                for c in range(2)
            ],
            axis=0,
        )
        lifted = jnp.dot(split, weights, preferred_element_type=jnp.float32)
        for b in range(LIFT):
            top = lifted[128 * b : 128 * b + 128].reshape(16, 8, 4 * chan)
            spot = group * LIFT + b
            for a in range(2):
                pair = [top[:, :, (2 * a + e) * chan : (2 * a + e + 1) * chan] for e in range(2)]
                pair = jnp.concatenate(pair, axis=1).reshape(4, 64, chan)
                held[spot, :, a] = (held[spot, :, a].astype(jnp.float32) + pair).astype(jnp.bfloat16)
        for b in range(LIFT):
            @pl.when(group * LIFT + b < count)
            def _():
                store(group * LIFT + b).start()

    @pl.loop(0, count)
    def _(spot):
        store(spot).wait()


def split_planes(gsx):
    inner = range(gsx // 4, gsx - gsx // 4)
    return inner, [x for x in range(gsx) if x not in inner]


def exchange(low, high, axis):
    count = lax.axis_size(axis)
    up = [(i, i + 1) for i in range(count - 1)]
    return lax.ppermute(high, axis, up), lax.ppermute(low, axis, [(j, i) for i, j in up])


def local(features, owner, norm_gain, time_shift, w_in, w_out, w_down, w_conv, w_up):
    cols_x, cols_y, zcap, voxels, chan = features.shape
    slots = cols_x * cols_y * zcap
    gsx, gsy, gsz = cols_x * 4, cols_y * 4, zcap * 4
    layers, _, hid = w_in.shape
    vmem = pl.BlockSpec(memory_space=pltpu.VMEM)
    smem = pl.BlockSpec(memory_space=pltpu.SMEM)
    hbm = pl.BlockSpec(memory_space=pltpu.HBM)

    def limit(mib):
        return pltpu.CompilerParams(vmem_limit_bytes=mib * MIB)

    def cells(*shape):
        return jax.ShapeDtypeStruct(shape + (gsz, chan), jnp.bfloat16)

    brick = (4, 2, voxels // 8, chan)
    blank = jax.ShapeDtypeStruct((cols_x, cols_y, zcap) + brick, jnp.bfloat16)
    grid, x_low, x_high, y_low, y_high, index, blank = pl.pallas_call(
        down_kernel,
        out_shape=[
            cells(gsx, gsy), cells(gsy), cells(gsy), cells(gsx), cells(gsx),
            jax.ShapeDtypeStruct((slots + 1,), jnp.int32),
            blank,
        ],
        in_specs=[hbm] * 7,
        out_specs=[vmem] * 5 + [smem, hbm],
        scratch_shapes=[
            pltpu.VMEM((MOST, voxels, chan), jnp.bfloat16),
            pltpu.SMEM(owner.shape, jnp.int32),
            pltpu.VMEM(norm_gain.shape, jnp.float32),
            pltpu.VMEM(time_shift.shape, jnp.float32),
            pltpu.VMEM((layers, chan, hid), jnp.bfloat16),
            pltpu.VMEM((layers, hid, chan), jnp.bfloat16),
            pltpu.VMEM((8, chan, chan), jnp.bfloat16),
            pltpu.VMEM((layers, hid, chan), jnp.bfloat16),
            pltpu.VMEM((layers, chan, hid), jnp.bfloat16),
            pltpu.VMEM((layers, hid, chan), jnp.bfloat16),
            pltpu.VMEM((GROUP, chan, voxels), jnp.float32),
            pltpu.VMEM((GROUP, voxels, chan), jnp.float32),
            pltpu.VMEM((gsx, gsy, gsz, chan), jnp.float32),
            pltpu.VMEM((BLANKS,) + brick, jnp.bfloat16),
            pltpu.SemaphoreType.DMA((MOST,)),
            pltpu.SemaphoreType.DMA((7,)),
            pltpu.SemaphoreType.DMA((slots // BLANKS,)),
        ],
        compiler_params=limit(55),
        name="voxel_ff_down",
    )(owner, features, norm_gain, time_shift, w_in, w_out, w_down.reshape(8, chan, chan))

    taps = w_conv.reshape(27, chan, chan)
    flops = 2 * 27 * gsx // 2 * gsy * gsz * chan * chan

    def own(wanted, *operands):
        return pl.pallas_call(
            functools.partial(own_kernel, wanted),
            out_shape=cells(len(wanted), gsy),
            in_specs=[vmem] * len(operands),
            out_specs=vmem,
            compiler_params=limit(20),
            cost_estimate=pl.CostEstimate(
                flops=4 * flops, bytes_accessed=4 * MIB, transcendentals=0
            ),
            name="conv_own",
        )(*operands)

    inner, outer = split_planes(gsx)
    inner = own(inner, grid, taps)
    x_low, x_high = exchange(x_low, x_high, "gx")
    outer = own(outer, grid, x_low, x_high, taps)
    y_low = jnp.concatenate([x_low[:1], y_low, x_high[:1]], axis=0)
    y_high = jnp.concatenate([x_low[-1:], y_high, x_high[-1:]], axis=0)
    y_low, y_high = exchange(y_low, y_high, "gy")

    result = pl.pallas_call(
        up_kernel,
        out_shape=jax.ShapeDtypeStruct(blank.shape, blank.dtype),
        in_specs=[smem] + [vmem] * 6 + [hbm, hbm],
        out_specs=hbm,
        input_output_aliases={8: 0},
        scratch_shapes=[
            pltpu.VMEM((MOST,) + brick, jnp.bfloat16),
            pltpu.VMEM((gsx, gsy, gsz, chan), jnp.float32),
            pltpu.VMEM((gsx, gsy, 2 * gsz, chan), jnp.float32),
            pltpu.SemaphoreType.DMA((MOST,)),
            pltpu.SemaphoreType.DMA((MOST,)),
        ],
        compiler_params=limit(48),
        name="rim_up",
    )(
        index, inner, outer, y_low, y_high, taps, w_up.reshape(8, chan, chan),
        features.reshape(blank.shape), blank,
    )
    return result.reshape(features.shape)


def solution(mesh):
    in_specs = (
        P("gx", "gy", None, None, None),
        P("gx", "gy", None),
        P(),
        P(),
        P(),
        P(),
        P(),
        P(),
        P(),
    )
    out_specs = P("gx", "gy", None, None, None)
    return jax.shard_map(local, mesh=mesh, in_specs=in_specs, out_specs=out_specs, check_vma=False)
```

```python
import functools

import jax
import jax.numpy as jnp
from jax import lax
from jax.experimental import pallas as pl
from jax.experimental.pallas import tpu as pltpu
from jax.sharding import PartitionSpec as P

GROUP = 8
WAIT = 2
CHUNK = 256
LIFT = 4
MOST = 32
BLANKS = 4
MIB = 1024 * 1024


def silu(value):
    half = 0.5 * value
    return half + half * jnp.tanh(half)


def place(slot, cols_y, zcap):
    return slot // (zcap * cols_y), lax.rem(slot // zcap, cols_y), lax.rem(slot, zcap)


def down_kernel(
    owner_hbm, feat_ref, gain_hbm, shift_hbm, w_in_hbm, w_out_hbm, w_down_hbm,
    out_ref, x_low_ref, x_high_ref, y_low_ref, y_high_ref, index, blank_ref,
    held, owner_ref, gain_ref, shift_ref, w_in_ref, w_out_ref, w_down_ref, w_in, w_out, shifts,
    stream, made, volume, zeros,
    sem, arg_sem, zero_sem,
):
    cols_x, cols_y, zcap, voxels, chan = feat_ref.shape
    slots = cols_x * cols_y * zcap
    layers = w_in_ref.shape[0]
    pairs = (
        (owner_hbm, owner_ref),
        (gain_hbm, gain_ref),
        (shift_hbm, shift_ref),
        (w_in_hbm, w_in_ref),
        (w_out_hbm, w_out_ref),
        (w_down_hbm, w_down_ref),
    )
    loads = [
        pltpu.make_async_copy(source, target, arg_sem.at[i])
        for i, (source, target) in enumerate(pairs)
    ]
    for load in loads:
        load.start()
    volume[...] = jnp.zeros_like(volume)
    zeros[...] = jnp.zeros_like(zeros)
    loads[0].wait()

    def at(slot):
        return place(slot, cols_y, zcap)

    def scan(slot, count):
        index[count] = slot
        return count + (owner_ref[at(slot)] >= 0).astype(jnp.int32)

    count = lax.fori_loop(0, slots, scan, 0, unroll=8)
    index[slots] = count
    groups = (count + GROUP - 1) // GROUP

    def slot_of(group, b):
        return index[jnp.minimum(group * GROUP + b, count - 1)]

    def copies(group):
        return [
            pltpu.make_async_copy(
                feat_ref.at[at(slot_of(group, b))], held.at[group * GROUP + b], sem.at[group * GROUP + b]
            )
            for b in range(GROUP)
        ]

    @pl.when(groups > 0)
    def _():
        for copy in copies(0):
            copy.start()

    parts = zcap // BLANKS
    blanks = [
        pltpu.make_async_copy(
            zeros,
            blank_ref.at[
                part // (parts * cols_y), part // parts % cols_y, pl.ds(part % parts * BLANKS, BLANKS)
            ],
            zero_sem.at[part],
        )
        for part in range(slots // BLANKS)
    ]
    for copy in blanks:
        copy.start()
    for load in loads[1:]:
        load.wait()
    for layer in range(layers):
        gain = gain_ref[layer : layer + 1] * (0.5 * chan**0.5)
        w_in[layer] = (w_in_ref[layer].T.astype(jnp.float32) * gain).astype(jnp.bfloat16)
        w_out[layer] = w_out_ref[layer].T
        shift = jnp.broadcast_to(0.5 * shift_ref[layer : layer + 1], (chan, shift_ref.shape[1]))
        shifts[layer] = shift.astype(jnp.bfloat16).T

    def down(group, b):
        slot = slot_of(group, b)
        weights = jnp.concatenate(
            [
                jnp.concatenate([w_down_ref[4 * a + c], w_down_ref[4 * a + 2 + c]], axis=1)
                for a in range(2)
                for c in range(2)
            ],
            axis=0,
        )
        taps = []
        for c in range(2):
            rows = made[b, pl.ds(c, voxels // 2, stride=2)]
            taps.append(rows.astype(jnp.bfloat16).reshape(4, 2, 32, chan))
        cells = jnp.concatenate(
            [taps[c][:, a].reshape(128, chan) for a in range(2) for c in range(2)], axis=1
        )
        both = jnp.dot(cells, weights, preferred_element_type=jnp.float32)
        both = both.reshape(16, 8, 2 * chan)
        row = lax.broadcasted_iota(jnp.int32, (16, 8, chan), 1)
        part = jnp.where(row < 4, both[:, :, :chan], both[:, :, chan:])
        coarse = silu(part + pltpu.roll(part, 4, axis=1)).reshape(4, 4, 8, chan)
        x, y, z = at(slot)
        where = (
            pl.ds(4 * x, 4),
            pl.ds(4 * y, 4),
            pl.ds(pl.multiple_of(8 * (z // 2), 8), 8),
        )
        row = lax.broadcasted_iota(jnp.int32, coarse.shape, 2)
        mine = (row // 4) == lax.rem(z, 2)
        volume[where] = jnp.where(mine, coarse, volume[where])

    def work(group, carry):
        @pl.when(group + 1 < groups)
        def _():
            for copy in copies(group + 1):
                copy.start()

        for copy in copies(group):
            copy.wait()

        def value(layer, b, span):
            if layer == 0:
                return held[group * GROUP + b, span].astype(jnp.float32).T
            return stream[b, :, span]

        def enter(layer, b, span):
            x = value(layer, b, span)
            power = jnp.sum(x * x, axis=0, keepdims=True)
            normed = (x * lax.rsqrt(power + chan * 1e-6)).astype(jnp.bfloat16)
            raw = jnp.dot(w_in[layer], normed, preferred_element_type=jnp.float32)
            shift = jnp.concatenate([shifts[layer]] * (CHUNK // chan), axis=1)
            return raw.astype(jnp.bfloat16) + shift

        def leave(layer, b, span, half):
            hidden = half + half * jnp.tanh(half)
            result = value(layer, b, span) + jnp.dot(
                w_out[layer], hidden, preferred_element_type=jnp.float32
            )
            if layer + 1 < layers:
                stream[b, :, span] = result
            else:
                made[b, span] = result.T

        order = [
            (layer, b, slice(v, v + CHUNK))
            for layer in range(layers)
            for b in range(GROUP)
            for v in range(0, voxels, CHUNK)
        ]
        half = enter(*order[0])
        for spot, (layer, b, span) in enumerate(order):
            later = enter(*order[spot + 1]) if spot + 1 < len(order) else None
            leave(layer, b, span, half)
            half = later
            if span.stop == voxels:
                if layer == 1 and b >= GROUP - WAIT:
                    down(jnp.maximum(group - 1, 0), b)
                if layer + 1 == layers and b < GROUP - WAIT:
                    down(group, b)
        return carry

    lax.fori_loop(0, groups, work, 0)

    @pl.when(groups > 0)
    def _():
        for b in range(GROUP - WAIT, GROUP):
            down(groups - 1, b)

    out_ref[...] = volume[...].astype(jnp.bfloat16)
    x_low_ref[...] = out_ref[0]
    x_high_ref[...] = out_ref[out_ref.shape[0] - 1]
    y_low_ref[...] = out_ref[:, 0]
    y_high_ref[...] = out_ref[:, out_ref.shape[1] - 1]

    for copy in blanks:
        copy.wait()


def shifted(sums, chan):
    z = lax.broadcasted_iota(jnp.int32, sums.shape[:2] + (chan,), 1)
    length = sums.shape[1]
    below = jnp.where(z == 0, 0.0, pltpu.roll(sums[:, :, :chan], 1, axis=1))
    above = jnp.where(z == length - 1, 0.0, pltpu.roll(sums[:, :, 2 * chan :], length - 1, axis=1))
    return sums[:, :, chan : 2 * chan] + below + above


def conv_lines(pieces, w_conv_ref):
    lines, gsz, chan = pieces[0][2].shape
    near = jnp.concatenate([piece.reshape(lines * gsz, chan) for _, _, piece in pieces], axis=1)
    taps = jnp.concatenate(
        [
            jnp.concatenate([w_conv_ref[9 * d + 3 * e + f] for f in range(3)], axis=1)
            for d, e, _ in pieces
        ],
        axis=0,
    )
    sums = jnp.dot(near, taps, preferred_element_type=jnp.float32)
    return shifted(sums.reshape(lines, gsz, 3 * chan), chan)


def moved_lines(lines, e):
    blank = jnp.zeros((1,) + lines.shape[1:], lines.dtype)
    if e == 0:
        return jnp.concatenate([blank, lines[:-1]], axis=0)
    if e == 2:
        return jnp.concatenate([lines[1:], blank], axis=0)
    return lines


def own_kernel(wanted, cells_ref, *refs):
    rims, (w_conv_ref, out_ref) = refs[:-2], refs[-2:]
    gsx = cells_ref.shape[0]
    for spot, x in enumerate(wanted):
        planes = [(d, x + d - 1, cells_ref) for d in range(3)]
        if rims:
            low_ref, high_ref = rims
            planes = [
                (d, i, low_ref if i < 0 else high_ref if i == gsx else ref) for d, i, ref in planes
            ]
        pieces = []
        for d, i, ref in planes:
            lines = ref[i] if 0 <= i < gsx else ref[...]
            pieces += [(d, e, moved_lines(lines, e)) for e in range(3)]
        total = cells_ref[x].astype(jnp.float32) + conv_lines(pieces, w_conv_ref)
        out_ref[spot] = total.astype(jnp.bfloat16)


def up_kernel(
    index, inner_ref, outer_ref, y_low_ref, y_high_ref, w_conv_ref, w_up_ref, feat_ref, blank_ref,
    out_ref, held, total, twice, in_sem, out_sem,
):
    gsx, gsy, gsz, chan = total.shape
    cols_x, cols_y, zcap = out_ref.shape[:3]
    count = index[cols_x * cols_y * zcap]

    def at(slot):
        return place(slot, cols_y, zcap)

    def load(spot):
        return pltpu.make_async_copy(feat_ref.at[at(index[spot])], held.at[spot], in_sem.at[spot])

    def store(spot):
        return pltpu.make_async_copy(held.at[spot], out_ref.at[at(index[spot])], out_sem.at[spot])

    @pl.loop(0, count)
    def _(spot):
        load(spot).start()

    groups = (count + LIFT - 1) // LIFT

    inner, outer = split_planes(gsx)
    for wanted, ref in ((inner, inner_ref), (outer, outer_ref)):
        for spot, x in enumerate(wanted):
            total[x] = ref[spot].astype(jnp.float32)
    for line, ref, e in ((0, y_low_ref, 0), (gsy - 1, y_high_ref, 2)):
        pieces = [(d, e, ref[d : d + gsx]) for d in range(3)]
        total[:, line] = total[:, line] + conv_lines(pieces, w_conv_ref)
    for x in range(gsx):
        for c in range(2):
            twice[x, :, pl.ds(c, gsz, stride=2)] = total[x]

    @pl.loop(0, groups)
    def _(group):
        for b in range(LIFT):
            @pl.when(group * LIFT + b < count)
            def _():
                load(group * LIFT + b).wait()

        cells = []
        for b in range(LIFT):
            x, y, z = at(index[jnp.minimum(group * LIFT + b, count - 1)])
            where = (pl.ds(4 * x, 4), pl.ds(4 * y, 4), pl.ds(pl.multiple_of(8 * z, 8), 8))
            cells.append(twice[where].reshape(128, chan))
        cells = jnp.concatenate(cells, axis=0)
        odd = lax.rem(lax.broadcasted_iota(jnp.int32, cells.shape, 0), 2) == 1
        split = jnp.concatenate(
            [jnp.where(odd, 0.0, cells), jnp.where(odd, cells, 0.0)], axis=1
        ).astype(jnp.bfloat16)
        weights = jnp.concatenate(
            [
                jnp.concatenate(
                    [w_up_ref[4 * a + 2 * b + c] for a in range(2) for b in range(2)], axis=1
                )
                for c in range(2)
            ],
            axis=0,
        )
        lifted = jnp.dot(split, weights, preferred_element_type=jnp.float32)
        for b in range(LIFT):
            top = lifted[128 * b : 128 * b + 128].reshape(16, 8, 4 * chan)
            spot = group * LIFT + b
            for a in range(2):
                pair = [top[:, :, (2 * a + e) * chan : (2 * a + e + 1) * chan] for e in range(2)]
                pair = jnp.concatenate(pair, axis=1).reshape(4, 64, chan)
                held[spot, :, a] = (held[spot, :, a].astype(jnp.float32) + pair).astype(jnp.bfloat16)
        for b in range(LIFT):
            @pl.when(group * LIFT + b < count)
            def _():
                store(group * LIFT + b).start()

    @pl.loop(0, count)
    def _(spot):
        store(spot).wait()


def split_planes(gsx):
    inner = range(gsx // 4, gsx - gsx // 4)
    return inner, [x for x in range(gsx) if x not in inner]


def exchange(low, high, axis):
    count = lax.axis_size(axis)
    up = [(i, i + 1) for i in range(count - 1)]
    return lax.ppermute(high, axis, up), lax.ppermute(low, axis, [(j, i) for i, j in up])


def local(features, owner, norm_gain, time_shift, w_in, w_out, w_down, w_conv, w_up):
    cols_x, cols_y, zcap, voxels, chan = features.shape
    slots = cols_x * cols_y * zcap
    gsx, gsy, gsz = cols_x * 4, cols_y * 4, zcap * 4
    layers, _, hid = w_in.shape
    vmem = pl.BlockSpec(memory_space=pltpu.VMEM)
    smem = pl.BlockSpec(memory_space=pltpu.SMEM)
    hbm = pl.BlockSpec(memory_space=pltpu.HBM)

    def limit(mib):
        return pltpu.CompilerParams(vmem_limit_bytes=mib * MIB)

    def cells(*shape):
        return jax.ShapeDtypeStruct(shape + (gsz, chan), jnp.bfloat16)

    brick = (4, 2, voxels // 8, chan)
    blank = jax.ShapeDtypeStruct((cols_x, cols_y, zcap) + brick, jnp.bfloat16)
    grid, x_low, x_high, y_low, y_high, index, blank = pl.pallas_call(
        down_kernel,
        out_shape=[
            cells(gsx, gsy), cells(gsy), cells(gsy), cells(gsx), cells(gsx),
            jax.ShapeDtypeStruct((slots + 1,), jnp.int32),
            blank,
        ],
        in_specs=[hbm] * 7,
        out_specs=[vmem] * 5 + [smem, hbm],
        scratch_shapes=[
            pltpu.VMEM((MOST, voxels, chan), jnp.bfloat16),
            pltpu.SMEM(owner.shape, jnp.int32),
            pltpu.VMEM(norm_gain.shape, jnp.float32),
            pltpu.VMEM(time_shift.shape, jnp.float32),
            pltpu.VMEM((layers, chan, hid), jnp.bfloat16),
            pltpu.VMEM((layers, hid, chan), jnp.bfloat16),
            pltpu.VMEM((8, chan, chan), jnp.bfloat16),
            pltpu.VMEM((layers, hid, chan), jnp.bfloat16),
            pltpu.VMEM((layers, chan, hid), jnp.bfloat16),
            pltpu.VMEM((layers, hid, chan), jnp.bfloat16),
            pltpu.VMEM((GROUP, chan, voxels), jnp.float32),
            pltpu.VMEM((GROUP, voxels, chan), jnp.float32),
            pltpu.VMEM((gsx, gsy, gsz, chan), jnp.float32),
            pltpu.VMEM((BLANKS,) + brick, jnp.bfloat16),
            pltpu.SemaphoreType.DMA((MOST,)),
            pltpu.SemaphoreType.DMA((7,)),
            pltpu.SemaphoreType.DMA((slots // BLANKS,)),
        ],
        compiler_params=limit(55),
        name="voxel_ff_down",
    )(owner, features, norm_gain, time_shift, w_in, w_out, w_down.reshape(8, chan, chan))

    taps = w_conv.reshape(27, chan, chan)
    flops = 2 * 27 * gsx // 2 * gsy * gsz * chan * chan

    def own(wanted, *operands):
        return pl.pallas_call(
            functools.partial(own_kernel, wanted),
            out_shape=cells(len(wanted), gsy),
            in_specs=[vmem] * len(operands),
            out_specs=vmem,
            compiler_params=limit(20),
            cost_estimate=pl.CostEstimate(
                flops=4 * flops, bytes_accessed=4 * MIB, transcendentals=0
            ),
            name="conv_own",
        )(*operands)

    inner, outer = split_planes(gsx)
    inner = own(inner, grid, taps)
    x_low, x_high = exchange(x_low, x_high, "gx")
    outer = own(outer, grid, x_low, x_high, taps)
    y_low = jnp.concatenate([x_low[:1], y_low, x_high[:1]], axis=0)
    y_high = jnp.concatenate([x_low[-1:], y_high, x_high[-1:]], axis=0)
    y_low, y_high = exchange(y_low, y_high, "gy")

    result = pl.pallas_call(
        up_kernel,
        out_shape=jax.ShapeDtypeStruct(blank.shape, blank.dtype),
        in_specs=[smem] + [vmem] * 6 + [hbm, hbm],
        out_specs=hbm,
        input_output_aliases={8: 0},
        scratch_shapes=[
            pltpu.VMEM((MOST,) + brick, jnp.bfloat16),
            pltpu.VMEM((gsx, gsy, gsz, chan), jnp.float32),
            pltpu.VMEM((gsx, gsy, 2 * gsz, chan), jnp.float32),
            pltpu.SemaphoreType.DMA((MOST,)),
            pltpu.SemaphoreType.DMA((MOST,)),
        ],
        compiler_params=limit(48),
        name="rim_up",
    )(
        index, inner, outer, y_low, y_high, taps, w_up.reshape(8, chan, chan),
        features.reshape(blank.shape), blank,
    )
    return result.reshape(features.shape)


def solution(mesh):
    in_specs = (
        P("gx", "gy", None, None, None),
        P("gx", "gy", None),
        P(),
        P(),
        P(),
        P(),
        P(),
        P(),
        P(),
    )
    out_specs = P("gx", "gy", None, None, None)
    return jax.shard_map(local, mesh=mesh, in_specs=in_specs, out_specs=out_specs, check_vma=False)
```

```python
import functools

import jax
import jax.numpy as jnp
from jax import lax
from jax.experimental import pallas as pl
from jax.experimental.pallas import tpu as pltpu
from jax.sharding import PartitionSpec as P

GROUP = 8
PIECE = 2
LIFT = 4
MOST = 32
BLANKS = 4
MIB = 1024 * 1024


def silu(value):
    half = 0.5 * value
    return half + half * jnp.tanh(half)


def place(slot, cols_y, zcap):
    return slot // (zcap * cols_y), lax.rem(slot // zcap, cols_y), lax.rem(slot, zcap)


def down_kernel(
    owner_hbm, feat_ref, gain_hbm, shift_hbm, w_in_hbm, w_out_hbm, w_down_hbm,
    out_ref, x_low_ref, x_high_ref, y_low_ref, y_high_ref, index, blank_ref,
    held, owner_ref, gain_ref, shift_ref, w_in_ref, w_out_ref, w_down_ref, w_in, w_out, shifts,
    stream, made, volume, zeros,
    sem, arg_sem, zero_sem,
):
    cols_x, cols_y, zcap, voxels, chan = feat_ref.shape
    slots = cols_x * cols_y * zcap
    layers = w_in_ref.shape[0]
    pairs = (
        (owner_hbm, owner_ref),
        (gain_hbm, gain_ref),
        (shift_hbm, shift_ref),
        (w_in_hbm, w_in_ref),
        (w_out_hbm, w_out_ref),
        (w_down_hbm, w_down_ref),
    )
    loads = [
        pltpu.make_async_copy(source, target, arg_sem.at[i])
        for i, (source, target) in enumerate(pairs)
    ]
    for load in loads:
        load.start()
    volume[...] = jnp.zeros_like(volume)
    zeros[...] = jnp.zeros_like(zeros)
    loads[0].wait()

    def at(slot):
        return place(slot, cols_y, zcap)

    def scan(slot, count):
        index[count] = slot
        return count + (owner_ref[at(slot)] >= 0).astype(jnp.int32)

    count = lax.fori_loop(0, slots, scan, 0, unroll=8)
    index[slots] = count
    groups = (count + GROUP - 1) // GROUP

    def slot_of(group, b):
        return index[jnp.minimum(group * GROUP + b, count - 1)]

    def copies(group):
        return [
            pltpu.make_async_copy(
                feat_ref.at[at(slot_of(group, b))], held.at[group * GROUP + b], sem.at[group * GROUP + b]
            )
            for b in range(GROUP)
        ]

    @pl.when(groups > 0)
    def _():
        for copy in copies(0):
            copy.start()

    parts = zcap // BLANKS
    blanks = [
        pltpu.make_async_copy(
            zeros,
            blank_ref.at[
                part // (parts * cols_y), part // parts % cols_y, pl.ds(part % parts * BLANKS, BLANKS)
            ],
            zero_sem.at[part],
        )
        for part in range(slots // BLANKS)
    ]
    for copy in blanks:
        copy.start()
    for load in loads[1:]:
        load.wait()
    for layer in range(layers):
        gain = gain_ref[layer : layer + 1] * (0.5 * chan**0.5)
        w_in[layer] = (w_in_ref[layer].T.astype(jnp.float32) * gain).astype(jnp.bfloat16)
        w_out[layer] = w_out_ref[layer].T
        shift = jnp.broadcast_to(0.5 * shift_ref[layer : layer + 1], (chan, shift_ref.shape[1]))
        shifts[layer] = shift.astype(jnp.bfloat16).T

    def down(group, b):
        slot = slot_of(group, b)
        weights = jnp.concatenate(
            [
                jnp.concatenate([w_down_ref[4 * a + c], w_down_ref[4 * a + 2 + c]], axis=1)
                for a in range(2)
                for c in range(2)
            ],
            axis=0,
        )
        taps = []
        for c in range(2):
            rows = made[b, pl.ds(c, voxels // 2, stride=2)]
            taps.append(rows.astype(jnp.bfloat16).reshape(4, 2, 32, chan))
        cells = jnp.concatenate(
            [taps[c][:, a].reshape(128, chan) for a in range(2) for c in range(2)], axis=1
        )
        both = jnp.dot(cells, weights, preferred_element_type=jnp.float32)
        both = both.reshape(16, 8, 2 * chan)
        row = lax.broadcasted_iota(jnp.int32, (16, 8, chan), 1)
        part = jnp.where(row < 4, both[:, :, :chan], both[:, :, chan:])
        coarse = silu(part + pltpu.roll(part, 4, axis=1)).reshape(4, 4, 8, chan)
        x, y, z = at(slot)
        where = (
            pl.ds(4 * x, 4),
            pl.ds(4 * y, 4),
            pl.ds(pl.multiple_of(8 * (z // 2), 8), 8),
        )
        row = lax.broadcasted_iota(jnp.int32, coarse.shape, 2)
        mine = (row // 4) == lax.rem(z, 2)
        volume[where] = jnp.where(mine, coarse, volume[where])

    def work(group, carry):
        @pl.when(group + 1 < groups)
        def _():
            for copy in copies(group + 1):
                copy.start()

        for copy in copies(group):
            copy.wait()

        def value(layer, piece):
            if layer > 0:
                return stream[piece]
            bricks = [group * GROUP + piece * PIECE + b for b in range(PIECE)]
            return jnp.concatenate([held[b].astype(jnp.float32).T for b in bricks], axis=1)

        def enter(layer, piece):
            x = value(layer, piece)
            power = jnp.sum(x * x, axis=0, keepdims=True)
            normed = (x * lax.rsqrt(power + chan * 1e-6)).astype(jnp.bfloat16)
            raw = jnp.dot(w_in[layer], normed, preferred_element_type=jnp.float32)
            shift = jnp.concatenate([shifts[layer]] * (PIECE * voxels // chan), axis=1)
            return raw.astype(jnp.bfloat16) + shift

        def leave(layer, piece, half):
            hidden = half + half * jnp.tanh(half)
            result = value(layer, piece) + jnp.dot(
                w_out[layer], hidden, preferred_element_type=jnp.float32
            )
            if layer + 1 < layers:
                stream[piece] = result
            else:
                for b in range(PIECE):
                    made[piece * PIECE + b] = result[:, b * voxels : (b + 1) * voxels].T

        order = [(layer, piece) for layer in range(layers) for piece in range(GROUP // PIECE)]
        half = enter(*order[0])
        for spot, here in enumerate(order):
            later = enter(*order[spot + 1]) if spot + 1 < len(order) else None
            leave(*here, half)
            half = later
            if here[0] == 1:
                for b in range(PIECE):
                    down(jnp.maximum(group - 1, 0), here[1] * PIECE + b)
        return carry

    lax.fori_loop(0, groups, work, 0)

    @pl.when(groups > 0)
    def _():
        for b in range(GROUP):
            down(groups - 1, b)

    out_ref[...] = volume[...].astype(jnp.bfloat16)
    x_low_ref[...] = out_ref[0]
    x_high_ref[...] = out_ref[out_ref.shape[0] - 1]
    y_low_ref[...] = out_ref[:, 0]
    y_high_ref[...] = out_ref[:, out_ref.shape[1] - 1]

    for copy in blanks:
        copy.wait()


def shifted(sums, chan):
    z = lax.broadcasted_iota(jnp.int32, sums.shape[:2] + (chan,), 1)
    length = sums.shape[1]
    below = jnp.where(z == 0, 0.0, pltpu.roll(sums[:, :, :chan], 1, axis=1))
    above = jnp.where(z == length - 1, 0.0, pltpu.roll(sums[:, :, 2 * chan :], length - 1, axis=1))
    return sums[:, :, chan : 2 * chan] + below + above


def conv_lines(pieces, w_conv_ref):
    lines, gsz, chan = pieces[0][2].shape
    near = jnp.concatenate([piece.reshape(lines * gsz, chan) for _, _, piece in pieces], axis=1)
    taps = jnp.concatenate(
        [
            jnp.concatenate([w_conv_ref[9 * d + 3 * e + f] for f in range(3)], axis=1)
            for d, e, _ in pieces
        ],
        axis=0,
    )
    sums = jnp.dot(near, taps, preferred_element_type=jnp.float32)
    return shifted(sums.reshape(lines, gsz, 3 * chan), chan)


def moved_lines(lines, e):
    blank = jnp.zeros((1,) + lines.shape[1:], lines.dtype)
    if e == 0:
        return jnp.concatenate([blank, lines[:-1]], axis=0)
    if e == 2:
        return jnp.concatenate([lines[1:], blank], axis=0)
    return lines


def own_kernel(wanted, cells_ref, *refs):
    rims, (w_conv_ref, out_ref) = refs[:-2], refs[-2:]
    gsx = cells_ref.shape[0]
    for spot, x in enumerate(wanted):
        planes = [(d, x + d - 1, cells_ref) for d in range(3)]
        if rims:
            low_ref, high_ref = rims
            planes = [
                (d, i, low_ref if i < 0 else high_ref if i == gsx else ref) for d, i, ref in planes
            ]
        pieces = []
        for d, i, ref in planes:
            lines = ref[i] if 0 <= i < gsx else ref[...]
            pieces += [(d, e, moved_lines(lines, e)) for e in range(3)]
        total = cells_ref[x].astype(jnp.float32) + conv_lines(pieces, w_conv_ref)
        out_ref[spot] = total.astype(jnp.bfloat16)


def up_kernel(
    index, inner_ref, outer_ref, y_low_ref, y_high_ref, w_conv_ref, w_up_ref, feat_ref, blank_ref,
    out_ref, held, total, twice, in_sem, out_sem,
):
    gsx, gsy, gsz, chan = total.shape
    cols_x, cols_y, zcap = out_ref.shape[:3]
    count = index[cols_x * cols_y * zcap]

    def at(slot):
        return place(slot, cols_y, zcap)

    def load(spot):
        return pltpu.make_async_copy(feat_ref.at[at(index[spot])], held.at[spot], in_sem.at[spot])

    def store(spot):
        return pltpu.make_async_copy(held.at[spot], out_ref.at[at(index[spot])], out_sem.at[spot])

    @pl.loop(0, count)
    def _(spot):
        load(spot).start()

    groups = (count + LIFT - 1) // LIFT

    inner, outer = split_planes(gsx)
    for wanted, ref in ((inner, inner_ref), (outer, outer_ref)):
        for spot, x in enumerate(wanted):
            total[x] = ref[spot].astype(jnp.float32)
    for line, ref, e in ((0, y_low_ref, 0), (gsy - 1, y_high_ref, 2)):
        pieces = [(d, e, ref[d : d + gsx]) for d in range(3)]
        total[:, line] = total[:, line] + conv_lines(pieces, w_conv_ref)
    for x in range(gsx):
        for c in range(2):
            twice[x, :, pl.ds(c, gsz, stride=2)] = total[x]

    @pl.loop(0, groups)
    def _(group):
        for b in range(LIFT):
            @pl.when(group * LIFT + b < count)
            def _():
                load(group * LIFT + b).wait()

        cells = []
        for b in range(LIFT):
            x, y, z = at(index[jnp.minimum(group * LIFT + b, count - 1)])
            where = (pl.ds(4 * x, 4), pl.ds(4 * y, 4), pl.ds(pl.multiple_of(8 * z, 8), 8))
            cells.append(twice[where].reshape(128, chan))
        cells = jnp.concatenate(cells, axis=0)
        odd = lax.rem(lax.broadcasted_iota(jnp.int32, cells.shape, 0), 2) == 1
        split = jnp.concatenate(
            [jnp.where(odd, 0.0, cells), jnp.where(odd, cells, 0.0)], axis=1
        ).astype(jnp.bfloat16)
        weights = jnp.concatenate(
            [
                jnp.concatenate(
                    [w_up_ref[4 * a + 2 * b + c] for a in range(2) for b in range(2)], axis=1
                )
                for c in range(2)
            ],
            axis=0,
        )
        lifted = jnp.dot(split, weights, preferred_element_type=jnp.float32)
        for b in range(LIFT):
            top = lifted[128 * b : 128 * b + 128].reshape(16, 8, 4 * chan)
            spot = group * LIFT + b
            for a in range(2):
                pair = [top[:, :, (2 * a + e) * chan : (2 * a + e + 1) * chan] for e in range(2)]
                pair = jnp.concatenate(pair, axis=1).reshape(4, 64, chan)
                held[spot, :, a] = (held[spot, :, a].astype(jnp.float32) + pair).astype(jnp.bfloat16)
        for b in range(LIFT):
            @pl.when(group * LIFT + b < count)
            def _():
                store(group * LIFT + b).start()

    @pl.loop(0, count)
    def _(spot):
        store(spot).wait()


def split_planes(gsx):
    inner = range(gsx // 4, gsx - gsx // 4)
    return inner, [x for x in range(gsx) if x not in inner]


def exchange(low, high, axis):
    count = lax.axis_size(axis)
    up = [(i, i + 1) for i in range(count - 1)]
    return lax.ppermute(high, axis, up), lax.ppermute(low, axis, [(j, i) for i, j in up])


def local(features, owner, norm_gain, time_shift, w_in, w_out, w_down, w_conv, w_up):
    cols_x, cols_y, zcap, voxels, chan = features.shape
    slots = cols_x * cols_y * zcap
    gsx, gsy, gsz = cols_x * 4, cols_y * 4, zcap * 4
    layers, _, hid = w_in.shape
    vmem = pl.BlockSpec(memory_space=pltpu.VMEM)
    smem = pl.BlockSpec(memory_space=pltpu.SMEM)
    hbm = pl.BlockSpec(memory_space=pltpu.HBM)

    def limit(mib):
        return pltpu.CompilerParams(vmem_limit_bytes=mib * MIB)

    def cells(*shape):
        return jax.ShapeDtypeStruct(shape + (gsz, chan), jnp.bfloat16)

    brick = (4, 2, voxels // 8, chan)
    blank = jax.ShapeDtypeStruct((cols_x, cols_y, zcap) + brick, jnp.bfloat16)
    grid, x_low, x_high, y_low, y_high, index, blank = pl.pallas_call(
        down_kernel,
        out_shape=[
            cells(gsx, gsy), cells(gsy), cells(gsy), cells(gsx), cells(gsx),
            jax.ShapeDtypeStruct((slots + 1,), jnp.int32),
            blank,
        ],
        in_specs=[hbm] * 7,
        out_specs=[vmem] * 5 + [smem, hbm],
        scratch_shapes=[
            pltpu.VMEM((MOST, voxels, chan), jnp.bfloat16),
            pltpu.SMEM(owner.shape, jnp.int32),
            pltpu.VMEM(norm_gain.shape, jnp.float32),
            pltpu.VMEM(time_shift.shape, jnp.float32),
            pltpu.VMEM((layers, chan, hid), jnp.bfloat16),
            pltpu.VMEM((layers, hid, chan), jnp.bfloat16),
            pltpu.VMEM((8, chan, chan), jnp.bfloat16),
            pltpu.VMEM((layers, hid, chan), jnp.bfloat16),
            pltpu.VMEM((layers, chan, hid), jnp.bfloat16),
            pltpu.VMEM((layers, hid, chan), jnp.bfloat16),
            pltpu.VMEM((GROUP // PIECE, chan, PIECE * voxels), jnp.float32),
            pltpu.VMEM((GROUP, voxels, chan), jnp.float32),
            pltpu.VMEM((gsx, gsy, gsz, chan), jnp.float32),
            pltpu.VMEM((BLANKS,) + brick, jnp.bfloat16),
            pltpu.SemaphoreType.DMA((MOST,)),
            pltpu.SemaphoreType.DMA((7,)),
            pltpu.SemaphoreType.DMA((slots // BLANKS,)),
        ],
        compiler_params=limit(55),
        name="voxel_ff_down",
    )(owner, features, norm_gain, time_shift, w_in, w_out, w_down.reshape(8, chan, chan))

    taps = w_conv.reshape(27, chan, chan)
    flops = 2 * 27 * gsx // 2 * gsy * gsz * chan * chan

    def own(wanted, *operands):
        return pl.pallas_call(
            functools.partial(own_kernel, wanted),
            out_shape=cells(len(wanted), gsy),
            in_specs=[vmem] * len(operands),
            out_specs=vmem,
            compiler_params=limit(20),
            cost_estimate=pl.CostEstimate(
                flops=4 * flops, bytes_accessed=4 * MIB, transcendentals=0
            ),
            name="conv_own",
        )(*operands)

    inner, outer = split_planes(gsx)
    inner = own(inner, grid, taps)
    x_low, x_high = exchange(x_low, x_high, "gx")
    outer = own(outer, grid, x_low, x_high, taps)
    y_low = jnp.concatenate([x_low[:1], y_low, x_high[:1]], axis=0)
    y_high = jnp.concatenate([x_low[-1:], y_high, x_high[-1:]], axis=0)
    y_low, y_high = exchange(y_low, y_high, "gy")

    result = pl.pallas_call(
        up_kernel,
        out_shape=jax.ShapeDtypeStruct(blank.shape, blank.dtype),
        in_specs=[smem] + [vmem] * 6 + [hbm, hbm],
        out_specs=hbm,
        input_output_aliases={8: 0},
        scratch_shapes=[
            pltpu.VMEM((MOST,) + brick, jnp.bfloat16),
            pltpu.VMEM((gsx, gsy, gsz, chan), jnp.float32),
            pltpu.VMEM((gsx, gsy, 2 * gsz, chan), jnp.float32),
            pltpu.SemaphoreType.DMA((MOST,)),
            pltpu.SemaphoreType.DMA((MOST,)),
        ],
        compiler_params=limit(48),
        name="rim_up",
    )(
        index, inner, outer, y_low, y_high, taps, w_up.reshape(8, chan, chan),
        features.reshape(blank.shape), blank,
    )
    return result.reshape(features.shape)


def solution(mesh):
    in_specs = (
        P("gx", "gy", None, None, None),
        P("gx", "gy", None),
        P(),
        P(),
        P(),
        P(),
        P(),
        P(),
        P(),
    )
    out_specs = P("gx", "gy", None, None, None)
    return jax.shard_map(local, mesh=mesh, in_specs=in_specs, out_specs=out_specs, check_vma=False)
```

```python
import functools

import jax
import jax.numpy as jnp
from jax import lax
from jax.experimental import pallas as pl
from jax.experimental.pallas import tpu as pltpu
from jax.sharding import PartitionSpec as P

GROUP = 8
LIFT = 4
MOST = 32
BLANKS = 4
MIB = 1024 * 1024


def silu(value):
    half = 0.5 * value
    return half + half * jnp.tanh(half)


def place(slot, cols_y, zcap):
    return slot // (zcap * cols_y), lax.rem(slot // zcap, cols_y), lax.rem(slot, zcap)


def down_kernel(
    owner_hbm, feat_ref, gain_hbm, shift_hbm, w_in_hbm, w_out_hbm, w_down_hbm,
    out_ref, x_low_ref, x_high_ref, y_low_ref, y_high_ref, index, blank_ref,
    held, owner_ref, gain_ref, shift_ref, w_in_ref, w_out_ref, w_down_ref, w_in, w_out, shifts,
    stream, made, volume, zeros,
    sem, arg_sem, zero_sem,
):
    cols_x, cols_y, zcap, voxels, chan = feat_ref.shape
    slots = cols_x * cols_y * zcap
    layers = w_in_ref.shape[0]
    pairs = (
        (owner_hbm, owner_ref),
        (gain_hbm, gain_ref),
        (shift_hbm, shift_ref),
        (w_in_hbm, w_in_ref),
        (w_out_hbm, w_out_ref),
        (w_down_hbm, w_down_ref),
    )
    loads = [
        pltpu.make_async_copy(source, target, arg_sem.at[i])
        for i, (source, target) in enumerate(pairs)
    ]
    for load in loads:
        load.start()
    volume[...] = jnp.zeros_like(volume)
    zeros[...] = jnp.zeros_like(zeros)
    loads[0].wait()

    def at(slot):
        return place(slot, cols_y, zcap)

    def scan(slot, count):
        index[count] = slot
        return count + (owner_ref[at(slot)] >= 0).astype(jnp.int32)

    count = lax.fori_loop(0, slots, scan, 0, unroll=8)
    index[slots] = count
    groups = (count + GROUP - 1) // GROUP

    def slot_of(group, b):
        return index[jnp.minimum(group * GROUP + b, count - 1)]

    def copies(group):
        return [
            pltpu.make_async_copy(
                feat_ref.at[at(slot_of(group, b))], held.at[group * GROUP + b], sem.at[group * GROUP + b]
            )
            for b in range(GROUP)
        ]

    @pl.when(groups > 0)
    def _():
        for copy in copies(0):
            copy.start()

    parts = zcap // BLANKS
    blanks = [
        pltpu.make_async_copy(
            zeros,
            blank_ref.at[
                part // (parts * cols_y), part // parts % cols_y, pl.ds(part % parts * BLANKS, BLANKS)
            ],
            zero_sem.at[part],
        )
        for part in range(slots // BLANKS)
    ]
    for copy in blanks:
        copy.start()
    for load in loads[1:]:
        load.wait()
    for layer in range(layers):
        gain = gain_ref[layer : layer + 1] * (0.5 * chan**0.5)
        w_in[layer] = (w_in_ref[layer].astype(jnp.float32).T * gain).astype(jnp.bfloat16)
        w_out[layer] = w_out_ref[layer].astype(jnp.float32).T.astype(jnp.bfloat16)
        shift = jnp.broadcast_to(0.5 * shift_ref[layer : layer + 1], (chan, shift_ref.shape[1]))
        shifts[layer] = shift.T.astype(jnp.bfloat16)

    def down(group, b):
        slot = slot_of(group, b)
        weights = jnp.concatenate(
            [
                jnp.concatenate([w_down_ref[4 * a + c], w_down_ref[4 * a + 2 + c]], axis=1)
                for a in range(2)
                for c in range(2)
            ],
            axis=0,
        )
        taps = []
        for c in range(2):
            rows = made[b, pl.ds(c, voxels // 2, stride=2)]
            taps.append(rows.astype(jnp.bfloat16).reshape(4, 2, 32, chan))
        cells = jnp.concatenate(
            [taps[c][:, a].reshape(128, chan) for a in range(2) for c in range(2)], axis=1
        )
        both = jnp.dot(cells, weights, preferred_element_type=jnp.float32)
        both = both.reshape(16, 8, 2 * chan)
        row = lax.broadcasted_iota(jnp.int32, (16, 8, chan), 1)
        part = jnp.where(row < 4, both[:, :, :chan], both[:, :, chan:])
        coarse = silu(part + pltpu.roll(part, 4, axis=1)).reshape(4, 4, 8, chan)
        x, y, z = at(slot)
        where = (
            pl.ds(4 * x, 4),
            pl.ds(4 * y, 4),
            pl.ds(pl.multiple_of(8 * (z // 2), 8), 8),
        )
        row = lax.broadcasted_iota(jnp.int32, coarse.shape, 2)
        mine = (row // 4) == lax.rem(z, 2)
        volume[where] = jnp.where(mine, coarse, volume[where])

    def work(group, carry):
        @pl.when(group + 1 < groups)
        def _():
            for copy in copies(group + 1):
                copy.start()

        for copy in copies(group):
            copy.wait()

        def value(layer, b):
            return held[group * GROUP + b].astype(jnp.float32).T if layer == 0 else stream[b]

        def enter(layer, b):
            x = value(layer, b)
            power = jnp.sum(x * x, axis=0, keepdims=True)
            normed = (x * lax.rsqrt(power + chan * 1e-6)).astype(jnp.bfloat16)
            raw = jnp.dot(w_in[layer], normed, preferred_element_type=jnp.float32)
            shift = jnp.concatenate([shifts[layer]] * (voxels // chan), axis=1)
            return raw.astype(jnp.bfloat16) + shift

        def leave(layer, b, half):
            hidden = half + half * jnp.tanh(half)
            result = value(layer, b) + jnp.dot(
                w_out[layer], hidden, preferred_element_type=jnp.float32
            )
            if layer + 1 < layers:
                stream[b] = result
            else:
                made[b] = result.T

        order = [(layer, b) for layer in range(layers) for b in range(GROUP)]
        half = enter(*order[0])
        for spot, here in enumerate(order):
            later = enter(*order[spot + 1]) if spot + 1 < len(order) else None
            leave(*here, half)
            if here[0] == 1:
                down(jnp.maximum(group - 1, 0), here[1])
            half = later
        return carry

    lax.fori_loop(0, groups, work, 0)

    @pl.when(groups > 0)
    def _():
        for b in range(GROUP):
            down(groups - 1, b)

    out_ref[...] = volume[...].astype(jnp.bfloat16)
    x_low_ref[...] = out_ref[0]
    x_high_ref[...] = out_ref[out_ref.shape[0] - 1]
    y_low_ref[...] = out_ref[:, 0]
    y_high_ref[...] = out_ref[:, out_ref.shape[1] - 1]

    for copy in blanks:
        copy.wait()


def shifted(sums, chan):
    z = lax.broadcasted_iota(jnp.int32, sums.shape[:2] + (chan,), 1)
    length = sums.shape[1]
    below = jnp.where(z == 0, 0.0, pltpu.roll(sums[:, :, :chan], 1, axis=1))
    above = jnp.where(z == length - 1, 0.0, pltpu.roll(sums[:, :, 2 * chan :], length - 1, axis=1))
    return sums[:, :, chan : 2 * chan] + below + above


def conv_lines(pieces, w_conv_ref):
    lines, gsz, chan = pieces[0][2].shape
    near = jnp.concatenate([piece.reshape(lines * gsz, chan) for _, _, piece in pieces], axis=1)
    taps = jnp.concatenate(
        [
            jnp.concatenate([w_conv_ref[9 * d + 3 * e + f] for f in range(3)], axis=1)
            for d, e, _ in pieces
        ],
        axis=0,
    )
    sums = jnp.dot(near, taps, preferred_element_type=jnp.float32)
    return shifted(sums.reshape(lines, gsz, 3 * chan), chan)


def moved_lines(lines, e):
    blank = jnp.zeros((1,) + lines.shape[1:], lines.dtype)
    if e == 0:
        return jnp.concatenate([blank, lines[:-1]], axis=0)
    if e == 2:
        return jnp.concatenate([lines[1:], blank], axis=0)
    return lines


def own_kernel(wanted, cells_ref, *refs):
    rims, (w_conv_ref, out_ref) = refs[:-2], refs[-2:]
    gsy = cells_ref.shape[1]
    for spot, y in enumerate(wanted):
        pieces = []
        for e in range(3):
            i = y + e - 1
            if 0 <= i < gsy:
                lines = cells_ref[:, i]
            elif rims:
                lines = rims[0 if i < 0 else 1][...]
            else:
                continue
            pieces += [(d, e, moved_lines(lines, d)) for d in range(3)]
        total = cells_ref[:, y].astype(jnp.float32) + conv_lines(pieces, w_conv_ref)
        out_ref[spot] = total.astype(jnp.bfloat16)


def up_kernel(
    index, inner_ref, outer_ref, x_low_ref, x_high_ref, w_conv_ref, w_up_ref, feat_ref, blank_ref,
    out_ref, held, total, twice, in_sem, out_sem,
):
    gsx, gsy, gsz, chan = total.shape
    cols_x, cols_y, zcap = out_ref.shape[:3]
    count = index[cols_x * cols_y * zcap]

    def at(slot):
        return place(slot, cols_y, zcap)

    def load(spot):
        return pltpu.make_async_copy(feat_ref.at[at(index[spot])], held.at[spot], in_sem.at[spot])

    def store(spot):
        return pltpu.make_async_copy(held.at[spot], out_ref.at[at(index[spot])], out_sem.at[spot])

    @pl.loop(0, count)
    def _(spot):
        load(spot).start()

    groups = (count + LIFT - 1) // LIFT

    inner, outer = split_planes(gsy)
    for wanted, ref in ((inner, inner_ref), (outer, outer_ref)):
        for spot, y in enumerate(wanted):
            total[:, y] = ref[spot].astype(jnp.float32)
    for plane, ref, d in ((0, x_low_ref, 0), (gsx - 1, x_high_ref, 2)):
        pieces = [(d, e, ref[e : e + gsy]) for e in range(3)]
        total[plane] = total[plane] + conv_lines(pieces, w_conv_ref)
    for x in range(gsx):
        for c in range(2):
            twice[x, :, pl.ds(c, gsz, stride=2)] = total[x]

    @pl.loop(0, groups)
    def _(group):
        for b in range(LIFT):
            @pl.when(group * LIFT + b < count)
            def _():
                load(group * LIFT + b).wait()

        cells = []
        for b in range(LIFT):
            x, y, z = at(index[jnp.minimum(group * LIFT + b, count - 1)])
            where = (pl.ds(4 * x, 4), pl.ds(4 * y, 4), pl.ds(pl.multiple_of(8 * z, 8), 8))
            cells.append(twice[where].reshape(128, chan))
        cells = jnp.concatenate(cells, axis=0)
        odd = lax.rem(lax.broadcasted_iota(jnp.int32, cells.shape, 0), 2) == 1
        split = jnp.concatenate(
            [jnp.where(odd, 0.0, cells), jnp.where(odd, cells, 0.0)], axis=1
        ).astype(jnp.bfloat16)
        weights = jnp.concatenate(
            [
                jnp.concatenate(
                    [w_up_ref[4 * a + 2 * b + c] for a in range(2) for b in range(2)], axis=1
                )
                for c in range(2)
            ],
            axis=0,
        )
        lifted = jnp.dot(split, weights, preferred_element_type=jnp.float32)
        for b in range(LIFT):
            top = lifted[128 * b : 128 * b + 128].reshape(16, 8, 4 * chan)
            spot = group * LIFT + b
            for a in range(2):
                pair = [top[:, :, (2 * a + e) * chan : (2 * a + e + 1) * chan] for e in range(2)]
                pair = jnp.concatenate(pair, axis=1).reshape(4, 64, chan)
                held[spot, :, a] = (held[spot, :, a].astype(jnp.float32) + pair).astype(jnp.bfloat16)
        for b in range(LIFT):
            @pl.when(group * LIFT + b < count)
            def _():
                store(group * LIFT + b).start()

    @pl.loop(0, count)
    def _(spot):
        store(spot).wait()


def split_planes(gsy):
    return range(1, gsy - 1), (0, gsy - 1)


def exchange(low, high, axis):
    count = lax.axis_size(axis)
    up = [(i, i + 1) for i in range(count - 1)]
    return lax.ppermute(high, axis, up), lax.ppermute(low, axis, [(j, i) for i, j in up])


def local(features, owner, norm_gain, time_shift, w_in, w_out, w_down, w_conv, w_up):
    cols_x, cols_y, zcap, voxels, chan = features.shape
    slots = cols_x * cols_y * zcap
    gsx, gsy, gsz = cols_x * 4, cols_y * 4, zcap * 4
    layers, _, hid = w_in.shape
    vmem = pl.BlockSpec(memory_space=pltpu.VMEM)
    smem = pl.BlockSpec(memory_space=pltpu.SMEM)
    hbm = pl.BlockSpec(memory_space=pltpu.HBM)

    def limit(mib):
        return pltpu.CompilerParams(vmem_limit_bytes=mib * MIB)

    def cells(*shape):
        return jax.ShapeDtypeStruct(shape + (gsz, chan), jnp.bfloat16)

    brick = (4, 2, voxels // 8, chan)
    blank = jax.ShapeDtypeStruct((cols_x, cols_y, zcap) + brick, jnp.bfloat16)
    grid, x_low, x_high, y_low, y_high, index, blank = pl.pallas_call(
        down_kernel,
        out_shape=[
            cells(gsx, gsy), cells(gsy), cells(gsy), cells(gsx), cells(gsx),
            jax.ShapeDtypeStruct((slots + 1,), jnp.int32),
            blank,
        ],
        in_specs=[hbm] * 7,
        out_specs=[vmem] * 5 + [smem, hbm],
        scratch_shapes=[
            pltpu.VMEM((MOST, voxels, chan), jnp.bfloat16),
            pltpu.SMEM(owner.shape, jnp.int32),
            pltpu.VMEM(norm_gain.shape, jnp.float32),
            pltpu.VMEM(time_shift.shape, jnp.float32),
            pltpu.VMEM((layers, chan, hid), jnp.bfloat16),
            pltpu.VMEM((layers, hid, chan), jnp.bfloat16),
            pltpu.VMEM((8, chan, chan), jnp.bfloat16),
            pltpu.VMEM((layers, hid, chan), jnp.bfloat16),
            pltpu.VMEM((layers, chan, hid), jnp.bfloat16),
            pltpu.VMEM((layers, hid, chan), jnp.bfloat16),
            pltpu.VMEM((GROUP, chan, voxels), jnp.float32),
            pltpu.VMEM((GROUP, voxels, chan), jnp.float32),
            pltpu.VMEM((gsx, gsy, gsz, chan), jnp.float32),
            pltpu.VMEM((BLANKS,) + brick, jnp.bfloat16),
            pltpu.SemaphoreType.DMA((MOST,)),
            pltpu.SemaphoreType.DMA((7,)),
            pltpu.SemaphoreType.DMA((slots // BLANKS,)),
        ],
        compiler_params=limit(55),
        name="voxel_ff_down",
    )(owner, features, norm_gain, time_shift, w_in, w_out, w_down.reshape(8, chan, chan))

    taps = w_conv.reshape(27, chan, chan)
    def own(wanted, *operands):
        return pl.pallas_call(
            functools.partial(own_kernel, wanted),
            out_shape=cells(len(wanted), gsx),
            in_specs=[vmem] * len(operands),
            out_specs=vmem,
            compiler_params=limit(20),
            cost_estimate=pl.CostEstimate(
                flops=200 * len(wanted) * gsx * gsz * chan * chan,
                bytes_accessed=4 * MIB,
                transcendentals=0,
            ),
            name="conv_own",
        )(*operands)

    inner, outer = split_planes(gsy)
    y_low, y_high = exchange(y_low, y_high, "gy")
    inner = own(inner, grid, taps)
    outer = own(outer, grid, y_low, y_high, taps)
    x_low = jnp.concatenate([y_low[:1], x_low, y_high[:1]], axis=0)
    x_high = jnp.concatenate([y_low[-1:], x_high, y_high[-1:]], axis=0)
    x_low, x_high = exchange(x_low, x_high, "gx")

    result = pl.pallas_call(
        up_kernel,
        out_shape=jax.ShapeDtypeStruct(blank.shape, blank.dtype),
        in_specs=[smem] + [vmem] * 6 + [hbm, hbm],
        out_specs=hbm,
        input_output_aliases={8: 0},
        scratch_shapes=[
            pltpu.VMEM((MOST,) + brick, jnp.bfloat16),
            pltpu.VMEM((gsx, gsy, gsz, chan), jnp.float32),
            pltpu.VMEM((gsx, gsy, 2 * gsz, chan), jnp.float32),
            pltpu.SemaphoreType.DMA((MOST,)),
            pltpu.SemaphoreType.DMA((MOST,)),
        ],
        compiler_params=limit(48),
        name="rim_up",
    )(
        index, inner, outer, x_low, x_high, taps, w_up.reshape(8, chan, chan),
        features.reshape(blank.shape), blank,
    )
    return result.reshape(features.shape)


def solution(mesh):
    in_specs = (
        P("gx", "gy", None, None, None),
        P("gx", "gy", None),
        P(),
        P(),
        P(),
        P(),
        P(),
        P(),
        P(),
    )
    out_specs = P("gx", "gy", None, None, None)
    return jax.shard_map(local, mesh=mesh, in_specs=in_specs, out_specs=out_specs, check_vma=False)
```

```python
import functools

import jax
import jax.numpy as jnp
from jax import lax
from jax.experimental import pallas as pl
from jax.experimental.pallas import tpu as pltpu
from jax.sharding import PartitionSpec as P

GROUP = 8
LIFT = 4
MOST = 32
BLANKS = 4
MIB = 1024 * 1024


def silu(value):
    half = 0.5 * value
    return half + half * jnp.tanh(half)


def place(slot, cols_y, zcap):
    return slot // (zcap * cols_y), lax.rem(slot // zcap, cols_y), lax.rem(slot, zcap)


def down_kernel(
    owner_hbm, feat_ref, gain_hbm, shift_hbm, w_in_hbm, w_out_hbm, w_down_hbm,
    out_ref, x_low_ref, x_high_ref, y_first_ref, y_second_ref, index, blank_ref,
    held, owner_ref, gain_ref, shift_ref, w_in_ref, w_out_ref, w_down_ref, w_in, w_out, shifts,
    stream, made, volume, zeros,
    sem, arg_sem, zero_sem,
):
    cols_x, cols_y, zcap, voxels, chan = feat_ref.shape
    slots = cols_x * cols_y * zcap
    layers = w_in_ref.shape[0]
    pairs = (
        (owner_hbm, owner_ref),
        (gain_hbm, gain_ref),
        (shift_hbm, shift_ref),
        (w_in_hbm, w_in_ref),
        (w_out_hbm, w_out_ref),
        (w_down_hbm, w_down_ref),
    )
    loads = [
        pltpu.make_async_copy(source, target, arg_sem.at[i])
        for i, (source, target) in enumerate(pairs)
    ]
    for load in loads:
        load.start()
    volume[...] = jnp.zeros_like(volume)
    zeros[...] = jnp.zeros_like(zeros)
    loads[0].wait()

    def at(slot):
        return place(slot, cols_y, zcap)

    def scan(slot, count):
        index[count] = slot
        return count + (owner_ref[at(slot)] >= 0).astype(jnp.int32)

    count = lax.fori_loop(0, slots, scan, 0, unroll=8)
    index[slots] = count
    groups = (count + GROUP - 1) // GROUP

    def slot_of(group, b):
        return index[jnp.minimum(group * GROUP + b, count - 1)]

    def copies(group):
        return [
            pltpu.make_async_copy(
                feat_ref.at[at(slot_of(group, b))], held.at[group * GROUP + b], sem.at[group * GROUP + b]
            )
            for b in range(GROUP)
        ]

    @pl.when(groups > 0)
    def _():
        for copy in copies(0):
            copy.start()

    parts = zcap // BLANKS
    blanks = [
        pltpu.make_async_copy(
            zeros,
            blank_ref.at[
                part // (parts * cols_y), part // parts % cols_y, pl.ds(part % parts * BLANKS, BLANKS)
            ],
            zero_sem.at[part],
        )
        for part in range(slots // BLANKS)
    ]
    for copy in blanks:
        copy.start()
    for load in loads[1:]:
        load.wait()
    for layer in range(layers):
        gain = gain_ref[layer : layer + 1] * (0.5 * chan**0.5)
        w_in[layer] = (w_in_ref[layer].astype(jnp.float32).T * gain).astype(jnp.bfloat16)
        w_out[layer] = w_out_ref[layer].astype(jnp.float32).T.astype(jnp.bfloat16)
        shift = jnp.broadcast_to(0.5 * shift_ref[layer : layer + 1], (chan, shift_ref.shape[1]))
        shifts[layer] = shift.T.astype(jnp.bfloat16)

    def down(group, b):
        slot = slot_of(group, b)
        weights = jnp.concatenate(
            [
                jnp.concatenate([w_down_ref[4 * a + c], w_down_ref[4 * a + 2 + c]], axis=1)
                for a in range(2)
                for c in range(2)
            ],
            axis=0,
        )
        taps = []
        for c in range(2):
            rows = made[b, pl.ds(c, voxels // 2, stride=2)]
            taps.append(rows.astype(jnp.bfloat16).reshape(4, 2, 32, chan))
        cells = jnp.concatenate(
            [taps[c][:, a].reshape(128, chan) for a in range(2) for c in range(2)], axis=1
        )
        both = jnp.dot(cells, weights, preferred_element_type=jnp.float32)
        both = both.reshape(16, 8, 2 * chan)
        row = lax.broadcasted_iota(jnp.int32, (16, 8, chan), 1)
        part = jnp.where(row < 4, both[:, :, :chan], both[:, :, chan:])
        coarse = silu(part + pltpu.roll(part, 4, axis=1)).reshape(4, 4, 8, chan)
        x, y, z = at(slot)
        where = (
            pl.ds(4 * x, 4),
            pl.ds(4 * y, 4),
            pl.ds(pl.multiple_of(8 * (z // 2), 8), 8),
        )
        row = lax.broadcasted_iota(jnp.int32, coarse.shape, 2)
        mine = (row // 4) == lax.rem(z, 2)
        volume[where] = jnp.where(mine, coarse, volume[where])

    def work(group, carry):
        @pl.when(group + 1 < groups)
        def _():
            for copy in copies(group + 1):
                copy.start()

        for copy in copies(group):
            copy.wait()

        def value(layer, b):
            return held[group * GROUP + b].astype(jnp.float32).T if layer == 0 else stream[b]

        def enter(layer, b):
            x = value(layer, b)
            power = jnp.sum(x * x, axis=0, keepdims=True)
            normed = (x * lax.rsqrt(power + chan * 1e-6)).astype(jnp.bfloat16)
            raw = jnp.dot(w_in[layer], normed, preferred_element_type=jnp.float32)
            shift = jnp.concatenate([shifts[layer]] * (voxels // chan), axis=1)
            return raw.astype(jnp.bfloat16) + shift

        def leave(layer, b, half):
            hidden = half + half * jnp.tanh(half)
            result = value(layer, b) + jnp.dot(
                w_out[layer], hidden, preferred_element_type=jnp.float32
            )
            if layer + 1 < layers:
                stream[b] = result
            else:
                made[b] = result.T

        order = [(layer, b) for layer in range(layers) for b in range(GROUP)]
        half = enter(*order[0])
        for spot, here in enumerate(order):
            later = enter(*order[spot + 1]) if spot + 1 < len(order) else None
            leave(*here, half)
            if here[0] == 1:
                down(jnp.maximum(group - 1, 0), here[1])
            half = later
        return carry

    lax.fori_loop(0, groups, work, 0)

    @pl.when(groups > 0)
    def _():
        for b in range(GROUP):
            down(groups - 1, b)

    out_ref[...] = volume[...].astype(jnp.bfloat16)
    x_low_ref[...] = out_ref[0]
    x_high_ref[...] = out_ref[out_ref.shape[0] - 1]
    last = out_ref.shape[1] - 1
    odd = lax.rem(lax.axis_index("gy"), 2)
    y_first_ref[...] = out_ref[:, (1 - odd) * last]
    y_second_ref[...] = out_ref[:, odd * last]

    for copy in blanks:
        copy.wait()


def shifted(sums, chan):
    z = lax.broadcasted_iota(jnp.int32, sums.shape[:2] + (chan,), 1)
    length = sums.shape[1]
    below = jnp.where(z == 0, 0.0, pltpu.roll(sums[:, :, :chan], 1, axis=1))
    above = jnp.where(z == length - 1, 0.0, pltpu.roll(sums[:, :, 2 * chan :], length - 1, axis=1))
    return sums[:, :, chan : 2 * chan] + below + above


def conv_lines(pieces, w_conv_ref):
    lines, gsz, chan = pieces[0][2].shape
    near = jnp.concatenate([piece.reshape(lines * gsz, chan) for _, _, piece in pieces], axis=1)
    taps = jnp.concatenate(
        [
            jnp.concatenate([w_conv_ref[9 * d + 3 * e + f] for f in range(3)], axis=1)
            for d, e, _ in pieces
        ],
        axis=0,
    )
    sums = jnp.dot(near, taps, preferred_element_type=jnp.float32)
    return shifted(sums.reshape(lines, gsz, 3 * chan), chan)


def moved_lines(lines, e):
    blank = jnp.zeros((1,) + lines.shape[1:], lines.dtype)
    if e == 0:
        return jnp.concatenate([blank, lines[:-1]], axis=0)
    if e == 2:
        return jnp.concatenate([lines[1:], blank], axis=0)
    return lines


def own_kernel(wanted, cells_ref, *refs):
    rims, (w_conv_ref, out_ref) = refs[:-2], refs[-2:]
    gsy = cells_ref.shape[1]
    for spot, y in enumerate(wanted):
        pieces = []
        for e in range(3):
            i = y + e - 1
            if 0 <= i < gsy:
                lines = cells_ref[:, i]
            elif rims:
                lines = rims[0 if i < 0 else 1][...]
            else:
                continue
            pieces += [(d, e, moved_lines(lines, d)) for d in range(3)]
        total = cells_ref[:, y].astype(jnp.float32) + conv_lines(pieces, w_conv_ref)
        out_ref[spot] = total.astype(jnp.bfloat16)


def up_kernel(
    index, inner_ref, outer_ref, x_low_ref, x_high_ref, w_conv_ref, w_up_ref, feat_ref, blank_ref,
    out_ref, held, total, twice, in_sem, out_sem,
):
    gsx, gsy, gsz, chan = total.shape
    cols_x, cols_y, zcap = out_ref.shape[:3]
    count = index[cols_x * cols_y * zcap]

    def at(slot):
        return place(slot, cols_y, zcap)

    def load(spot):
        return pltpu.make_async_copy(feat_ref.at[at(index[spot])], held.at[spot], in_sem.at[spot])

    def store(spot):
        return pltpu.make_async_copy(held.at[spot], out_ref.at[at(index[spot])], out_sem.at[spot])

    @pl.loop(0, count)
    def _(spot):
        load(spot).start()

    groups = (count + LIFT - 1) // LIFT

    inner, outer = split_planes(gsy)
    for wanted, ref in ((inner, inner_ref), (outer, outer_ref)):
        for spot, y in enumerate(wanted):
            total[:, y] = ref[spot].astype(jnp.float32)
    for plane, ref, d in ((0, x_low_ref, 0), (gsx - 1, x_high_ref, 2)):
        pieces = [(d, e, ref[e : e + gsy]) for e in range(3)]
        total[plane] = total[plane] + conv_lines(pieces, w_conv_ref)
    for x in range(gsx):
        for c in range(2):
            twice[x, :, pl.ds(c, gsz, stride=2)] = total[x]

    @pl.loop(0, groups)
    def _(group):
        for b in range(LIFT):
            @pl.when(group * LIFT + b < count)
            def _():
                load(group * LIFT + b).wait()

        cells = []
        for b in range(LIFT):
            x, y, z = at(index[jnp.minimum(group * LIFT + b, count - 1)])
            where = (pl.ds(4 * x, 4), pl.ds(4 * y, 4), pl.ds(pl.multiple_of(8 * z, 8), 8))
            cells.append(twice[where].reshape(128, chan))
        cells = jnp.concatenate(cells, axis=0)
        odd = lax.rem(lax.broadcasted_iota(jnp.int32, cells.shape, 0), 2) == 1
        split = jnp.concatenate(
            [jnp.where(odd, 0.0, cells), jnp.where(odd, cells, 0.0)], axis=1
        ).astype(jnp.bfloat16)
        weights = jnp.concatenate(
            [
                jnp.concatenate(
                    [w_up_ref[4 * a + 2 * b + c] for a in range(2) for b in range(2)], axis=1
                )
                for c in range(2)
            ],
            axis=0,
        )
        lifted = jnp.dot(split, weights, preferred_element_type=jnp.float32)
        for b in range(LIFT):
            top = lifted[128 * b : 128 * b + 128].reshape(16, 8, 4 * chan)
            spot = group * LIFT + b
            for a in range(2):
                pair = [top[:, :, (2 * a + e) * chan : (2 * a + e + 1) * chan] for e in range(2)]
                pair = jnp.concatenate(pair, axis=1).reshape(4, 64, chan)
                held[spot, :, a] = (held[spot, :, a].astype(jnp.float32) + pair).astype(jnp.bfloat16)
        for b in range(LIFT):
            @pl.when(group * LIFT + b < count)
            def _():
                store(group * LIFT + b).start()

    @pl.loop(0, count)
    def _(spot):
        store(spot).wait()


def split_planes(gsy):
    return range(1, gsy - 1), (0, gsy - 1)


def swap(first, second, axis):
    count = lax.axis_size(axis)
    pairs = [[(i, i + 1) for i in range(start, count - 1, 2)] for start in range(2)]
    both = [
        lax.ppermute(face, axis, ahead + [(j, i) for i, j in ahead])
        for face, ahead in zip((first, second), pairs)
    ]
    return choose(axis, *both)


def choose(axis, first, second):
    odd = lax.axis_index(axis) % 2 == 1
    return jnp.where(odd, first, second), jnp.where(odd, second, first)


def local(features, owner, norm_gain, time_shift, w_in, w_out, w_down, w_conv, w_up):
    cols_x, cols_y, zcap, voxels, chan = features.shape
    slots = cols_x * cols_y * zcap
    gsx, gsy, gsz = cols_x * 4, cols_y * 4, zcap * 4
    layers, _, hid = w_in.shape
    vmem = pl.BlockSpec(memory_space=pltpu.VMEM)
    smem = pl.BlockSpec(memory_space=pltpu.SMEM)
    hbm = pl.BlockSpec(memory_space=pltpu.HBM)

    def limit(mib):
        return pltpu.CompilerParams(vmem_limit_bytes=mib * MIB)

    def cells(*shape):
        return jax.ShapeDtypeStruct(shape + (gsz, chan), jnp.bfloat16)

    brick = (4, 2, voxels // 8, chan)
    blank = jax.ShapeDtypeStruct((cols_x, cols_y, zcap) + brick, jnp.bfloat16)
    grid, x_low, x_high, y_first, y_second, index, blank = pl.pallas_call(
        down_kernel,
        out_shape=[
            cells(gsx, gsy), cells(gsy), cells(gsy), cells(gsx), cells(gsx),
            jax.ShapeDtypeStruct((slots + 1,), jnp.int32),
            blank,
        ],
        in_specs=[hbm] * 7,
        out_specs=[vmem] * 5 + [smem, hbm],
        scratch_shapes=[
            pltpu.VMEM((MOST, voxels, chan), jnp.bfloat16),
            pltpu.SMEM(owner.shape, jnp.int32),
            pltpu.VMEM(norm_gain.shape, jnp.float32),
            pltpu.VMEM(time_shift.shape, jnp.float32),
            pltpu.VMEM((layers, chan, hid), jnp.bfloat16),
            pltpu.VMEM((layers, hid, chan), jnp.bfloat16),
            pltpu.VMEM((8, chan, chan), jnp.bfloat16),
            pltpu.VMEM((layers, hid, chan), jnp.bfloat16),
            pltpu.VMEM((layers, chan, hid), jnp.bfloat16),
            pltpu.VMEM((layers, hid, chan), jnp.bfloat16),
            pltpu.VMEM((GROUP, chan, voxels), jnp.float32),
            pltpu.VMEM((GROUP, voxels, chan), jnp.float32),
            pltpu.VMEM((gsx, gsy, gsz, chan), jnp.float32),
            pltpu.VMEM((BLANKS,) + brick, jnp.bfloat16),
            pltpu.SemaphoreType.DMA((MOST,)),
            pltpu.SemaphoreType.DMA((7,)),
            pltpu.SemaphoreType.DMA((slots // BLANKS,)),
        ],
        compiler_params=limit(55),
        name="voxel_ff_down",
    )(owner, features, norm_gain, time_shift, w_in, w_out, w_down.reshape(8, chan, chan))

    taps = w_conv.reshape(27, chan, chan)
    def own(wanted, *operands):
        return pl.pallas_call(
            functools.partial(own_kernel, wanted),
            out_shape=cells(len(wanted), gsx),
            in_specs=[vmem] * len(operands),
            out_specs=vmem,
            compiler_params=limit(20),
            cost_estimate=pl.CostEstimate(
                flops=200 * len(wanted) * gsx * gsz * chan * chan,
                bytes_accessed=4 * MIB,
                transcendentals=0,
            ),
            name="conv_own",
        )(*operands)

    inner, outer = split_planes(gsy)
    y_low, y_high = swap(y_first, y_second, "gy")
    inner = own(inner, grid, taps)
    outer = own(outer, grid, y_low, y_high, taps)
    x_low = jnp.concatenate([y_low[:1], x_low, y_high[:1]], axis=0)
    x_high = jnp.concatenate([y_low[-1:], x_high, y_high[-1:]], axis=0)
    x_low, x_high = swap(*choose("gx", x_low, x_high), "gx")

    result = pl.pallas_call(
        up_kernel,
        out_shape=jax.ShapeDtypeStruct(blank.shape, blank.dtype),
        in_specs=[smem] + [vmem] * 6 + [hbm, hbm],
        out_specs=hbm,
        input_output_aliases={8: 0},
        scratch_shapes=[
            pltpu.VMEM((MOST,) + brick, jnp.bfloat16),
            pltpu.VMEM((gsx, gsy, gsz, chan), jnp.float32),
            pltpu.VMEM((gsx, gsy, 2 * gsz, chan), jnp.float32),
            pltpu.SemaphoreType.DMA((MOST,)),
            pltpu.SemaphoreType.DMA((MOST,)),
        ],
        compiler_params=limit(48),
        name="rim_up",
    )(
        index, inner, outer, x_low, x_high, taps, w_up.reshape(8, chan, chan),
        features.reshape(blank.shape), blank,
    )
    return result.reshape(features.shape)


def solution(mesh):
    in_specs = (
        P("gx", "gy", None, None, None),
        P("gx", "gy", None),
        P(),
        P(),
        P(),
        P(),
        P(),
        P(),
        P(),
    )
    out_specs = P("gx", "gy", None, None, None)
    return jax.shard_map(local, mesh=mesh, in_specs=in_specs, out_specs=out_specs, check_vma=False)
```

```python
import functools

import jax
import jax.numpy as jnp
from jax import lax
from jax.experimental import pallas as pl
from jax.experimental.pallas import tpu as pltpu
from jax.sharding import PartitionSpec as P

GROUP = 8
PARTS = 2
LIFT = 4
MOST = 32
BLANKS = 4
MIB = 1024 * 1024


def silu(value):
    half = 0.5 * value
    return half + half * jnp.tanh(half)


def place(slot, cols_y, zcap):
    return slot // (zcap * cols_y), lax.rem(slot // zcap, cols_y), lax.rem(slot, zcap)


def down_kernel(
    owner_hbm, feat_ref, gain_hbm, shift_hbm, w_in_hbm, w_out_hbm, w_down_hbm,
    out_ref, x_low_ref, x_high_ref, y_first_ref, y_second_ref, index, blank_ref,
    held, owner_ref, gain_ref, shift_ref, w_in_ref, w_out_ref, w_down_ref, w_in, w_out, shifts,
    stream, made, volume, zeros,
    sem, arg_sem, zero_sem,
):
    cols_x, cols_y, zcap, voxels, chan = feat_ref.shape
    slots = cols_x * cols_y * zcap
    layers = w_in_ref.shape[0]
    pairs = (
        (owner_hbm, owner_ref),
        (gain_hbm, gain_ref),
        (shift_hbm, shift_ref),
        (w_in_hbm, w_in_ref),
        (w_out_hbm, w_out_ref),
        (w_down_hbm, w_down_ref),
    )
    loads = [
        pltpu.make_async_copy(source, target, arg_sem.at[i])
        for i, (source, target) in enumerate(pairs)
    ]
    for load in loads:
        load.start()
    volume[...] = jnp.zeros_like(volume)
    zeros[...] = jnp.zeros_like(zeros)
    loads[0].wait()

    def at(slot):
        return place(slot, cols_y, zcap)

    def scan(slot, count):
        index[count] = slot
        return count + (owner_ref[at(slot)] >= 0).astype(jnp.int32)

    count = lax.fori_loop(0, slots, scan, 0, unroll=8)
    index[slots] = count
    groups = (count + GROUP - 1) // GROUP

    def slot_of(group, b):
        return index[jnp.minimum(group * GROUP + b, count - 1)]

    def copies(group):
        return [
            pltpu.make_async_copy(
                feat_ref.at[at(slot_of(group, b))], held.at[group * GROUP + b], sem.at[group * GROUP + b]
            )
            for b in range(GROUP)
        ]

    @pl.when(groups > 0)
    def _():
        for copy in copies(0):
            copy.start()

    parts = zcap // BLANKS
    blanks = [
        pltpu.make_async_copy(
            zeros,
            blank_ref.at[
                part // (parts * cols_y), part // parts % cols_y, pl.ds(part % parts * BLANKS, BLANKS)
            ],
            zero_sem.at[part],
        )
        for part in range(slots // BLANKS)
    ]
    for copy in blanks:
        copy.start()
    for load in loads[1:]:
        load.wait()
    for layer in range(layers):
        gain = gain_ref[layer : layer + 1] * (0.5 * chan**0.5)
        w_in[layer] = (w_in_ref[layer].astype(jnp.float32).T * gain).astype(jnp.bfloat16)
        w_out[layer] = w_out_ref[layer].astype(jnp.float32).T.astype(jnp.bfloat16)
        shift = jnp.broadcast_to(0.5 * shift_ref[layer : layer + 1], (chan, shift_ref.shape[1]))
        shifts[layer] = shift.T.astype(jnp.bfloat16)

    def down(group, b):
        slot = slot_of(group, b)
        weights = jnp.concatenate(
            [
                jnp.concatenate([w_down_ref[4 * a + c], w_down_ref[4 * a + 2 + c]], axis=1)
                for a in range(2)
                for c in range(2)
            ],
            axis=0,
        )
        taps = []
        for c in range(2):
            rows = made[b, pl.ds(c, voxels // 2, stride=2)]
            taps.append(rows.astype(jnp.bfloat16).reshape(4, 2, 32, chan))
        cells = jnp.concatenate(
            [taps[c][:, a].reshape(128, chan) for a in range(2) for c in range(2)], axis=1
        )
        both = jnp.dot(cells, weights, preferred_element_type=jnp.float32)
        both = both.reshape(16, 8, 2 * chan)
        row = lax.broadcasted_iota(jnp.int32, (16, 8, chan), 1)
        part = jnp.where(row < 4, both[:, :, :chan], both[:, :, chan:])
        coarse = silu(part + pltpu.roll(part, 4, axis=1)).reshape(4, 4, 8, chan)
        x, y, z = at(slot)
        where = (
            pl.ds(4 * x, 4),
            pl.ds(4 * y, 4),
            pl.ds(pl.multiple_of(8 * (z // 2), 8), 8),
        )
        row = lax.broadcasted_iota(jnp.int32, coarse.shape, 2)
        mine = (row // 4) == lax.rem(z, 2)
        volume[where] = jnp.where(mine, coarse, volume[where])

    def work(group, carry):
        @pl.when(group + 1 < groups)
        def _():
            for copy in copies(group + 1):
                copy.start()

        for copy in copies(group):
            copy.wait()

        def value(layer, b):
            return held[group * GROUP + b].astype(jnp.float32).T if layer == 0 else stream[b]

        def norm(layer, b):
            x = value(layer, b)
            power = jnp.sum(x * x, axis=0, keepdims=True)
            return (x * lax.rsqrt(power + chan * 1e-6)).astype(jnp.bfloat16)

        def enter(layer, normed, part):
            units = w_in.shape[1] // PARTS
            span = slice(part * units, (part + 1) * units)
            raw = jnp.dot(w_in[layer, span], normed, preferred_element_type=jnp.float32)
            shift = jnp.concatenate([shifts[layer, span]] * (voxels // chan), axis=1)
            return raw.astype(jnp.bfloat16) + shift

        def leave(layer, b, hidden):
            result = value(layer, b) + jnp.dot(
                w_out[layer], hidden, preferred_element_type=jnp.float32
            )
            if layer + 1 < layers:
                stream[b] = result
            else:
                made[b] = result.T

        order = [(layer, b) for layer in range(layers) for b in range(GROUP)]
        normed = norm(*order[0])
        halves = [enter(0, normed, part) for part in range(PARTS)]
        for spot, here in enumerate(order):
            ahead = order[spot + 1] if spot + 1 < len(order) else None
            normed = norm(*ahead) if ahead else None
            later, hidden = [], []
            for part in range(PARTS):
                if ahead:
                    later.append(enter(ahead[0], normed, part))
                hidden.append(halves[part] + halves[part] * jnp.tanh(halves[part]))
            leave(*here, jnp.concatenate(hidden, axis=0))
            if here[0] == 1:
                down(jnp.maximum(group - 1, 0), here[1])
            halves = later
        return carry

    lax.fori_loop(0, groups, work, 0)

    @pl.when(groups > 0)
    def _():
        for b in range(GROUP):
            down(groups - 1, b)

    out_ref[...] = volume[...].astype(jnp.bfloat16)
    x_low_ref[...] = out_ref[0]
    x_high_ref[...] = out_ref[out_ref.shape[0] - 1]
    last = out_ref.shape[1] - 1
    odd = lax.rem(lax.axis_index("gy"), 2)
    y_first_ref[...] = out_ref[:, (1 - odd) * last]
    y_second_ref[...] = out_ref[:, odd * last]

    for copy in blanks:
        copy.wait()


def shifted(sums, chan):
    z = lax.broadcasted_iota(jnp.int32, sums.shape[:2] + (chan,), 1)
    length = sums.shape[1]
    below = jnp.where(z == 0, 0.0, pltpu.roll(sums[:, :, :chan], 1, axis=1))
    above = jnp.where(z == length - 1, 0.0, pltpu.roll(sums[:, :, 2 * chan :], length - 1, axis=1))
    return sums[:, :, chan : 2 * chan] + below + above


def conv_lines(pieces, w_conv_ref):
    lines, gsz, chan = pieces[0][2].shape
    near = jnp.concatenate([piece.reshape(lines * gsz, chan) for _, _, piece in pieces], axis=1)
    taps = jnp.concatenate(
        [
            jnp.concatenate([w_conv_ref[9 * d + 3 * e + f] for f in range(3)], axis=1)
            for d, e, _ in pieces
        ],
        axis=0,
    )
    sums = jnp.dot(near, taps, preferred_element_type=jnp.float32)
    return shifted(sums.reshape(lines, gsz, 3 * chan), chan)


def moved_lines(lines, e):
    blank = jnp.zeros((1,) + lines.shape[1:], lines.dtype)
    if e == 0:
        return jnp.concatenate([blank, lines[:-1]], axis=0)
    if e == 2:
        return jnp.concatenate([lines[1:], blank], axis=0)
    return lines


def own_kernel(wanted, cells_ref, *refs):
    rims, (w_conv_ref, out_ref) = refs[:-2], refs[-2:]
    gsy = cells_ref.shape[1]
    for spot, y in enumerate(wanted):
        pieces = []
        for e in range(3):
            i = y + e - 1
            if 0 <= i < gsy:
                lines = cells_ref[:, i]
            elif rims:
                lines = rims[0 if i < 0 else 1][...]
            else:
                continue
            pieces += [(d, e, moved_lines(lines, d)) for d in range(3)]
        total = cells_ref[:, y].astype(jnp.float32) + conv_lines(pieces, w_conv_ref)
        out_ref[spot] = total.astype(jnp.bfloat16)


def up_kernel(
    index, inner_ref, outer_ref, x_low_ref, x_high_ref, w_conv_ref, w_up_ref, feat_ref, blank_ref,
    out_ref, held, total, twice, in_sem, out_sem,
):
    gsx, gsy, gsz, chan = total.shape
    cols_x, cols_y, zcap = out_ref.shape[:3]
    count = index[cols_x * cols_y * zcap]

    def at(slot):
        return place(slot, cols_y, zcap)

    def load(spot):
        return pltpu.make_async_copy(feat_ref.at[at(index[spot])], held.at[spot], in_sem.at[spot])

    def store(spot):
        return pltpu.make_async_copy(held.at[spot], out_ref.at[at(index[spot])], out_sem.at[spot])

    @pl.loop(0, count)
    def _(spot):
        load(spot).start()

    groups = (count + LIFT - 1) // LIFT

    inner, outer = split_planes(gsy)
    for wanted, ref in ((inner, inner_ref), (outer, outer_ref)):
        for spot, y in enumerate(wanted):
            total[:, y] = ref[spot].astype(jnp.float32)
    for plane, ref, d in ((0, x_low_ref, 0), (gsx - 1, x_high_ref, 2)):
        pieces = [(d, e, ref[e : e + gsy]) for e in range(3)]
        total[plane] = total[plane] + conv_lines(pieces, w_conv_ref)
    for x in range(gsx):
        for c in range(2):
            twice[x, :, pl.ds(c, gsz, stride=2)] = total[x]

    @pl.loop(0, groups)
    def _(group):
        for b in range(LIFT):
            @pl.when(group * LIFT + b < count)
            def _():
                load(group * LIFT + b).wait()

        cells = []
        for b in range(LIFT):
            x, y, z = at(index[jnp.minimum(group * LIFT + b, count - 1)])
            where = (pl.ds(4 * x, 4), pl.ds(4 * y, 4), pl.ds(pl.multiple_of(8 * z, 8), 8))
            cells.append(twice[where].reshape(128, chan))
        cells = jnp.concatenate(cells, axis=0)
        odd = lax.rem(lax.broadcasted_iota(jnp.int32, cells.shape, 0), 2) == 1
        split = jnp.concatenate(
            [jnp.where(odd, 0.0, cells), jnp.where(odd, cells, 0.0)], axis=1
        ).astype(jnp.bfloat16)
        weights = jnp.concatenate(
            [
                jnp.concatenate(
                    [w_up_ref[4 * a + 2 * b + c] for a in range(2) for b in range(2)], axis=1
                )
                for c in range(2)
            ],
            axis=0,
        )
        lifted = jnp.dot(split, weights, preferred_element_type=jnp.float32)
        for b in range(LIFT):
            top = lifted[128 * b : 128 * b + 128].reshape(16, 8, 4 * chan)
            spot = group * LIFT + b
            for a in range(2):
                pair = [top[:, :, (2 * a + e) * chan : (2 * a + e + 1) * chan] for e in range(2)]
                pair = jnp.concatenate(pair, axis=1).reshape(4, 64, chan)
                held[spot, :, a] = (held[spot, :, a].astype(jnp.float32) + pair).astype(jnp.bfloat16)
        for b in range(LIFT):
            @pl.when(group * LIFT + b < count)
            def _():
                store(group * LIFT + b).start()

    @pl.loop(0, count)
    def _(spot):
        store(spot).wait()


def split_planes(gsy):
    return range(1, gsy - 1), (0, gsy - 1)


def swap(first, second, axis):
    count = lax.axis_size(axis)
    pairs = [[(i, i + 1) for i in range(start, count - 1, 2)] for start in range(2)]
    both = [
        lax.ppermute(face, axis, ahead + [(j, i) for i, j in ahead])
        for face, ahead in zip((first, second), pairs)
    ]
    return choose(axis, *both)


def choose(axis, first, second):
    odd = lax.axis_index(axis) % 2 == 1
    return jnp.where(odd, first, second), jnp.where(odd, second, first)


def local(features, owner, norm_gain, time_shift, w_in, w_out, w_down, w_conv, w_up):
    cols_x, cols_y, zcap, voxels, chan = features.shape
    slots = cols_x * cols_y * zcap
    gsx, gsy, gsz = cols_x * 4, cols_y * 4, zcap * 4
    layers, _, hid = w_in.shape
    vmem = pl.BlockSpec(memory_space=pltpu.VMEM)
    smem = pl.BlockSpec(memory_space=pltpu.SMEM)
    hbm = pl.BlockSpec(memory_space=pltpu.HBM)

    def limit(mib):
        return pltpu.CompilerParams(vmem_limit_bytes=mib * MIB)

    def cells(*shape):
        return jax.ShapeDtypeStruct(shape + (gsz, chan), jnp.bfloat16)

    brick = (4, 2, voxels // 8, chan)
    blank = jax.ShapeDtypeStruct((cols_x, cols_y, zcap) + brick, jnp.bfloat16)
    grid, x_low, x_high, y_first, y_second, index, blank = pl.pallas_call(
        down_kernel,
        out_shape=[
            cells(gsx, gsy), cells(gsy), cells(gsy), cells(gsx), cells(gsx),
            jax.ShapeDtypeStruct((slots + 1,), jnp.int32),
            blank,
        ],
        in_specs=[hbm] * 7,
        out_specs=[vmem] * 5 + [smem, hbm],
        scratch_shapes=[
            pltpu.VMEM((MOST, voxels, chan), jnp.bfloat16),
            pltpu.SMEM(owner.shape, jnp.int32),
            pltpu.VMEM(norm_gain.shape, jnp.float32),
            pltpu.VMEM(time_shift.shape, jnp.float32),
            pltpu.VMEM((layers, chan, hid), jnp.bfloat16),
            pltpu.VMEM((layers, hid, chan), jnp.bfloat16),
            pltpu.VMEM((8, chan, chan), jnp.bfloat16),
            pltpu.VMEM((layers, hid, chan), jnp.bfloat16),
            pltpu.VMEM((layers, chan, hid), jnp.bfloat16),
            pltpu.VMEM((layers, hid, chan), jnp.bfloat16),
            pltpu.VMEM((GROUP, chan, voxels), jnp.float32),
            pltpu.VMEM((GROUP, voxels, chan), jnp.float32),
            pltpu.VMEM((gsx, gsy, gsz, chan), jnp.float32),
            pltpu.VMEM((BLANKS,) + brick, jnp.bfloat16),
            pltpu.SemaphoreType.DMA((MOST,)),
            pltpu.SemaphoreType.DMA((7,)),
            pltpu.SemaphoreType.DMA((slots // BLANKS,)),
        ],
        compiler_params=limit(55),
        name="voxel_ff_down",
    )(owner, features, norm_gain, time_shift, w_in, w_out, w_down.reshape(8, chan, chan))

    taps = w_conv.reshape(27, chan, chan)
    def own(wanted, *operands):
        return pl.pallas_call(
            functools.partial(own_kernel, wanted),
            out_shape=cells(len(wanted), gsx),
            in_specs=[vmem] * len(operands),
            out_specs=vmem,
            compiler_params=limit(20),
            cost_estimate=pl.CostEstimate(
                flops=200 * len(wanted) * gsx * gsz * chan * chan,
                bytes_accessed=4 * MIB,
                transcendentals=0,
            ),
            name="conv_own",
        )(*operands)

    inner, outer = split_planes(gsy)
    y_low, y_high = swap(y_first, y_second, "gy")
    inner = own(inner, grid, taps)
    outer = own(outer, grid, y_low, y_high, taps)
    x_low = jnp.concatenate([y_low[:1], x_low, y_high[:1]], axis=0)
    x_high = jnp.concatenate([y_low[-1:], x_high, y_high[-1:]], axis=0)
    x_low, x_high = swap(*choose("gx", x_low, x_high), "gx")

    result = pl.pallas_call(
        up_kernel,
        out_shape=jax.ShapeDtypeStruct(blank.shape, blank.dtype),
        in_specs=[smem] + [vmem] * 6 + [hbm, hbm],
        out_specs=hbm,
        input_output_aliases={8: 0},
        scratch_shapes=[
            pltpu.VMEM((MOST,) + brick, jnp.bfloat16),
            pltpu.VMEM((gsx, gsy, gsz, chan), jnp.float32),
            pltpu.VMEM((gsx, gsy, 2 * gsz, chan), jnp.float32),
            pltpu.SemaphoreType.DMA((MOST,)),
            pltpu.SemaphoreType.DMA((MOST,)),
        ],
        compiler_params=limit(48),
        name="rim_up",
    )(
        index, inner, outer, x_low, x_high, taps, w_up.reshape(8, chan, chan),
        features.reshape(blank.shape), blank,
    )
    return result.reshape(features.shape)


def solution(mesh):
    in_specs = (
        P("gx", "gy", None, None, None),
        P("gx", "gy", None),
        P(),
        P(),
        P(),
        P(),
        P(),
        P(),
        P(),
    )
    out_specs = P("gx", "gy", None, None, None)
    return jax.shard_map(local, mesh=mesh, in_specs=in_specs, out_specs=out_specs, check_vma=False)
```
